256 devices in a mesh: zone: 16 (over y_hi, x, core), sector: 16 (over z, y_lo).
Axes of the slice: x: 4, y: 4 (y_hi: 2, y_lo: 2; y = y_hi * 2 + y_lo), z: 8, core: 2. Of those that a mesh axis runs over, the one named last changes fastest.
Arguments:
- kernel: bfloat16 [32, 1024, 6144], P(None, 'zone', 'sector'), may hold values from -16 to 16
- lon_halo: int32 [1024], replicated, may hold values from 12 to 48, as said below
- lat_reach: int32 [1024], P('zone'), may hold values from 8 to 32, as said below
- polar_rows: int32 [96], replicated, may hold values from 0 to 1023, as said below
- polar_shift: int32 [96], replicated, may hold values from 0 to 6143
- blend: bfloat16 [32, 32], replicated, may hold values from -1 to 1
Outputs:
- smoothed: bfloat16 [32, 1024, 6144], P(None, 'zone', 'sector')
The draws below stay inside these ranges and needn't reach their ends.
Inputs may be any that keep to these rules, and one draw needn't show every extreme that they name: `lon_halo`: some row has the half-width 48. `lat_reach`: some row has the half-width 32. `polar_rows`: the first 48 entries are distinct rows among the first 64 rows, ascending, starting with row 0; the last 48 are distinct rows among the last 64 rows, ascending, ending with row 1023.
All inputs are finite; a program needn't handle non-finite values.
Results may differ from the reference program's by a relative error of at most 0.0071.
Values may be sent and summed in bfloat16 or wider, within the bound.
No kernel may reach another device: no remote copies, remote signals or barrier semaphores. Data moves between devices by JAX's collectives and lax.ppermute only.
A program may use at most 256 MiB of HBM per device.

```python
import jax
import jax.numpy as jnp
from jax import lax

SHELLS = 32
LAT_DEV = 64
LON_DEV = 384
HMAX = 48
LMAX = 32
POLAR = 48
NLAT = 1024
NLON = 6144
N_ZONE = 16
N_SECTOR = 16


def draw_kernel(key, part):
    first = jax.random.fold_in(jax.random.fold_in(key, 5), 0)
    rough = 8.0 * jax.random.normal(first, (SHELLS, NLAT, NLON), jnp.float32)
    return jnp.clip(rough, -16.0, 16.0).astype(jnp.bfloat16)


def draw_lon_halo(key, part):
    first, second = jax.random.split(jax.random.fold_in(key, 11))
    widths = jax.random.randint(first, (NLAT,), HMAX // 4, HMAX + 1)
    place = jax.random.randint(second, (), 0, NLAT)
    return jnp.where(jnp.arange(NLAT) == place, HMAX, widths).astype(jnp.int32)


def draw_lat_reach(key, part):
    first, second = jax.random.split(jax.random.fold_in(key, 23))
    widths = jax.random.randint(first, (NLAT,), LMAX // 4, LMAX + 1)
    place = jax.random.randint(second, (), 0, NLAT)
    return jnp.where(jnp.arange(NLAT) == place, LMAX, widths).astype(jnp.int32)


def draw_polar_rows(key, part):
    first, second = jax.random.split(jax.random.fold_in(key, 37))
    upper = jax.random.permutation(first, LAT_DEV - 1)[:POLAR - 1].astype(jnp.int32) + 1
    upper = jnp.sort(jnp.concatenate([jnp.zeros((1,), jnp.int32), upper]))
    lower = jax.random.permutation(second, LAT_DEV - 1)[:POLAR - 1].astype(jnp.int32) + (NLAT - LAT_DEV)
    lower = jnp.sort(jnp.concatenate([lower, jnp.full((1,), NLAT - 1, jnp.int32)]))
    return jnp.concatenate([upper, lower]).astype(jnp.int32)


def draw_polar_shift(key, part):
    first, second = jax.random.split(jax.random.fold_in(key, 41))
    offsets = jax.random.randint(first, (2 * POLAR,), 0, NLON)
    place = jax.random.randint(second, (), 0, 2 * POLAR)
    position = jnp.arange(2 * POLAR)
    offsets = jnp.where(position == place, NLON - 1, offsets)
    offsets = jnp.where(position == (place + 1) % (2 * POLAR), 0, offsets)
    return offsets.astype(jnp.int32)


def noise(key, dims, spread, bound, held_as=jnp.bfloat16):
    return jnp.clip(spread * jax.random.normal(key, dims, jnp.float32), -bound, bound).astype(held_as)


def setup_inputs(seed: int = 0) -> dict:
    key_list = jax.random.split(jax.random.key(seed), 7)
    kernel = draw_kernel(jax.random.fold_in(key_list[6], 71), 0)
    lon_halo = draw_lon_halo(jax.random.fold_in(key_list[6], 71), 0)
    lat_reach = draw_lat_reach(jax.random.fold_in(key_list[6], 71), 0)
    polar_rows = draw_polar_rows(jax.random.fold_in(key_list[6], 71), 0)
    polar_shift = draw_polar_shift(jax.random.fold_in(key_list[6], 71), 0)
    blend = noise(key_list[5], (SHELLS, SHELLS), SHELLS ** -0.5, 1.0)
    return {"kernel": kernel, "lon_halo": lon_halo, "lat_reach": lat_reach, "polar_rows": polar_rows, "polar_shift": polar_shift, "blend": blend}


def band_matrix(half, window, width):
    half_f = half.astype(jnp.float32)
    rate = 4.5 / (half_f * half_f)
    taps = jnp.arange(-HMAX, HMAX + 1, dtype=jnp.int32).astype(jnp.float32)
    kept = jnp.abs(taps)[None, :] <= half_f[:, None]
    total = jnp.sum(jnp.where(kept, jnp.exp(-rate[:, None] * (taps * taps)[None, :]), jnp.float32(0.0)), axis=1)
    offset = (jnp.arange(window, dtype=jnp.int32)[:, None] - HMAX - jnp.arange(width, dtype=jnp.int32)[None, :]).astype(jnp.float32)
    inside = jnp.abs(offset)[None, :, :] <= half_f[:, None, None]
    weights = jnp.where(inside, jnp.exp(-rate[:, None, None] * (offset * offset)[None, :, :]), jnp.float32(0.0))
    return (weights / total[:, None, None]).astype(jnp.bfloat16)


def lat_matrix(reach, first_row, row_total, margin):
    count = reach.shape[0]
    reach_f = reach.astype(jnp.float32)
    rate = 4.5 / (reach_f * reach_f)
    column = jnp.arange(count + 2 * margin, dtype=jnp.int32)
    line = jnp.arange(count, dtype=jnp.int32)
    offset = column[None, :] - margin - line[:, None]
    source = first_row - margin + column
    valid = (jnp.abs(offset) <= reach[:, None]) & (source >= 0)[None, :] & (source < row_total)[None, :]
    offset_f = offset.astype(jnp.float32)
    weights = jnp.where(valid, jnp.exp(-rate[:, None] * (offset_f * offset_f)), jnp.float32(0.0))
    total = jnp.sum(weights, axis=1)
    return (weights / total[:, None]).astype(jnp.bfloat16)


def reference(kernel, lon_halo, lat_reach, polar_rows, polar_shift, blend):
    turned = jnp.transpose(kernel, (1, 0, 2))
    window = LON_DEV + 2 * HMAX
    tile_index = jnp.arange(N_SECTOR, dtype=jnp.int32)[:, None] * LON_DEV + jnp.arange(window, dtype=jnp.int32)[None, :]
    shift = jnp.zeros((NLAT,), jnp.int32).at[polar_rows].set(polar_shift.astype(jnp.int32))

    def lon_row(packed):
        values, half, offset = packed
        tripled = jnp.concatenate([values, values, values], axis=1)
        start = ((NLON - HMAX - offset) % NLON).astype(jnp.int32)
        extended = lax.dynamic_slice_in_dim(tripled, start, NLON + 2 * HMAX, 1)
        tiles = extended[:, tile_index].astype(jnp.float32)
        matrix = band_matrix(half[None], window, LON_DEV)[0].astype(jnp.float32)
        result = jnp.einsum('stk,kj->stj', tiles, matrix, precision=lax.Precision.HIGHEST)
        return result.reshape(SHELLS, NLON).astype(jnp.bfloat16)

    lon_smooth = lax.map(lon_row, (turned, lon_halo, shift))
    framed = jnp.pad(lon_smooth, ((LMAX, LMAX), (0, 0), (0, 0)))
    blend_f = blend.astype(jnp.float32)

    def lat_zone(zone_id):
        start = (zone_id * LAT_DEV).astype(jnp.int32)
        slab = lax.dynamic_slice_in_dim(framed, start, LAT_DEV + 2 * LMAX, 0)
        reach = lax.dynamic_slice_in_dim(lat_reach, start, LAT_DEV, 0)
        matrix = lat_matrix(reach, start, NLAT, LMAX).astype(jnp.float32)
        flat = slab.reshape(LAT_DEV + 2 * LMAX, SHELLS * NLON).astype(jnp.float32)
        lat = jnp.dot(matrix, flat, precision=lax.Precision.HIGHEST).reshape(LAT_DEV, SHELLS, NLON)
        lat_b = lax.optimization_barrier(lat.astype(jnp.bfloat16))
        mixed = jnp.einsum('st,itj->isj', blend_f, lat_b.astype(jnp.float32), precision=lax.Precision.HIGHEST)
        return mixed.astype(jnp.bfloat16)

    blocks = lax.map(lat_zone, jnp.arange(N_ZONE, dtype=jnp.int32))
    return jnp.transpose(blocks.reshape(NLAT, SHELLS, NLON), (1, 0, 2))
```

```python
import functools

import jax
import jax.numpy as jnp
from jax import lax
from jax.experimental import pallas as pl
from jax.experimental.pallas import tpu as pltpu
from jax.sharding import PartitionSpec as P

HMAX = 48
LMAX = 32
LANES = 128
F32 = jnp.float32
BF16 = jnp.bfloat16
VMEM_LIMIT = 40 * 1024 * 1024


def pack_kernel(zone_ref, rows_ref, x_ref, send_ref, low_ref, high_ref, wide_ref):
    shells, row_count, col_count = x_ref.shape
    total = shells * row_count
    half = total // 2
    zone = zone_ref[0]
    tiles = col_count // LANES
    for t in range(tiles):
        wide_ref[t] = x_ref[:, :, t * LANES : (t + 1) * LANES].reshape(total, LANES).astype(F32)
    holders, held = send_ref.shape[1], send_ref.shape[2]
    cap = jnp.where(zone < 8, 0, holders * held)

    def one_holder(k, carry):
        for r in range(held):
            row = jnp.clip(rows_ref[cap + k * held + r] - zone * row_count, 0, row_count - 1)
            for t in range(tiles):
                values = wide_ref[t, pl.ds(row, shells, stride=row_count), :].astype(BF16)
                for part in range(2):
                    send_ref[part, k, r, t * 16 : (t + 1) * 16, :] = values[part * 16 : (part + 1) * 16]
        return carry

    lax.fori_loop(0, holders, one_holder, 0)
    gap = jnp.zeros((half, LANES - 2 * HMAX), F32)
    for out_ref, t, first in ((low_ref, 0, 0), (high_ref, tiles - 1, LANES - HMAX)):
        edge = wide_ref[t, :, first : first + HMAX]
        out_ref[...] = jnp.concatenate([edge[:half], edge[half:], gap], axis=1).astype(BF16)


def band_rate(half_width):
    half_f = jnp.full((1, LANES), half_width, jnp.int32).astype(F32)
    rate = 4.5 / (half_f * half_f)
    tap = (lax.broadcasted_iota(jnp.int32, (1, LANES), 1) - HMAX).astype(F32)
    terms = jnp.where(jnp.abs(tap) <= half_f, jnp.exp(-rate * (tap * tap)), 0.0)
    total = jnp.sum(terms, axis=1, keepdims=True)
    return half_f, rate, total


def lon_kernel(zone_ref, halo_ref, x_ref, before_ref, after_ref, reach_ref, blend_ref,
               out_ref, weight_ref, mix_ref, wide_ref, done_ref):
    shells, row_count, col_count = x_ref.shape
    total = shells * row_count
    half = total // 2
    zone = zone_ref[0]

    def edge(ref):
        packed = ref[...].astype(F32)
        return jnp.concatenate([packed[:, :HMAX], packed[:, HMAX : 2 * HMAX]], axis=0)

    tiles = col_count // LANES
    wide = jnp.concatenate(
        [
            edge(before_ref),
            x_ref[...].reshape(total, col_count).astype(F32),
            edge(after_ref),
            jnp.zeros((total, LANES - 2 * HMAX), F32),
        ],
        axis=1,
    )
    for t in range(tiles + 1):
        wide_ref[t] = wide[:, t * LANES : (t + 1) * LANES]
    depth = 2 * LANES
    offset = (
        lax.broadcasted_iota(jnp.int32, (depth, LANES), 1)
        - lax.broadcasted_iota(jnp.int32, (depth, LANES), 0)
        + HMAX
    ).astype(F32)
    square = offset * offset
    distance = jnp.abs(offset)

    def one_row(i, carry):
        half_f, rate, terms = band_rate(halo_ref[zone * row_count + i])
        band = jnp.where(distance <= half_f, jnp.exp(-rate * square), 0.0) / terms
        values = [wide_ref[t, pl.ds(i, shells, stride=row_count), :].astype(BF16) for t in range(tiles + 1)]
        stacked = jnp.concatenate(
            [jnp.concatenate(values[:tiles], axis=0), jnp.concatenate(values[1:], axis=0)], axis=1
        )
        result = jnp.dot(stacked, band.astype(BF16), preferred_element_type=F32)
        for t in range(tiles):
            done_ref[t, pl.ds(i, shells, stride=row_count), :] = result[t * shells : (t + 1) * shells]
        return carry

    lax.fori_loop(0, row_count, one_row, 0)
    for t in range(tiles):
        out_ref[:, :, t * LANES : (t + 1) * LANES] = done_ref[t].astype(BF16).reshape(shells, row_count, LANES)
    frame_rows = weight_ref.shape[1]
    reach = reach_ref[...]
    column = lax.broadcasted_iota(jnp.int32, (row_count, frame_rows), 1)
    line = lax.broadcasted_iota(jnp.int32, (row_count, frame_rows), 0)
    away = column - LMAX - line
    source = zone * row_count - LMAX + column
    valid = (jnp.abs(away) <= reach) & (source >= 0) & (source < halo_ref.shape[0])
    reach_f = reach.astype(F32)
    away_f = away.astype(F32)
    weights = jnp.where(valid, jnp.exp(-(4.5 / (reach_f * reach_f)) * (away_f * away_f)), 0.0)
    weight_ref[...] = (weights / jnp.sum(weights, axis=1, keepdims=True)).astype(BF16)
    size = mix_ref.shape[0]
    group = size // shells
    spread = (
        lax.broadcasted_iota(jnp.int32, (size, shells), 0) // group
        == lax.broadcasted_iota(jnp.int32, (size, shells), 1)
    ).astype(F32).astype(BF16)
    tall = jnp.dot(spread, blend_ref[...], preferred_element_type=F32).astype(BF16)
    full = lax.dot_general(tall, spread, (((1,), (1,)), ((), ())), preferred_element_type=F32)
    same = (
        lax.broadcasted_iota(jnp.int32, (size, size), 0) % group
        == lax.broadcasted_iota(jnp.int32, (size, size), 1) % group
    )
    mix_ref[...] = jnp.where(same, full, 0.0).astype(BF16)


def hold_kernel(place_ref, rows_ref, shift_ref, halo_ref, x_ref, out_ref, circle_ref):
    sectors, held, block, _ = x_ref.shape
    zone, sector = place_ref[0], place_ref[1]
    cap = jnp.where(zone < 8, 0, sectors * held)
    part = 16
    length = sectors * block
    full_lon = length // part * LANES
    for r in range(held):
        for copy in range(2):
            circle_ref[r, copy * length : (copy + 1) * length, :] = x_ref[:, r].reshape(length, LANES)
        circle_ref[r, 2 * length : 2 * length + 2 * part, :] = circle_ref[r, 0 : 2 * part, :]
    for r in range(held):
        entry = cap + sector * held + r
        half_f, rate, terms = band_rate(halo_ref[rows_ref[entry]])
        start = lax.rem(2 * full_lon - shift_ref[entry] - HMAX, full_lon)
        first = start // LANES
        rest = start - first * LANES
        depth = 3 * LANES
        offset = (
            lax.broadcasted_iota(jnp.int32, (depth, LANES), 1)
            - lax.broadcasted_iota(jnp.int32, (depth, LANES), 0)
            + (rest + HMAX)
        ).astype(F32)
        band = jnp.where(jnp.abs(offset) <= half_f, jnp.exp(-rate * (offset * offset)), 0.0) / terms
        values = jnp.concatenate(
            [circle_ref[r, pl.ds(pl.multiple_of((first + u) * part, part), length), :] for u in range(3)], axis=1
        )
        result = jnp.dot(values, band.astype(BF16), preferred_element_type=F32)
        out_ref[:, r] = result.astype(BF16).reshape(sectors, block, LANES)


def lat_kernel(zone_ref, rows_ref, above_ref, own_ref, below_ref, mine_ref, other_ref, weight_ref, mix_ref,
               out_ref, frame_ref, lat_ref):
    shells, row_count, col_count = own_ref.shape
    frame_rows = row_count + 2 * LMAX
    zone = zone_ref[0]
    zones = 16
    tiles = col_count // LANES

    def one_frame(s, carry):
        base = pl.multiple_of(s * frame_rows, frame_rows)
        for t in range(tiles):
            columns = slice(t * LANES, (t + 1) * LANES)
            frame_ref[t, pl.ds(base, LMAX), :] = above_ref[s, :, columns].astype(F32)
            frame_ref[t, pl.ds(base + LMAX, row_count), :] = own_ref[s, :, columns].astype(F32)
            frame_ref[t, pl.ds(base + LMAX + row_count, LMAX), :] = below_ref[s, :, columns].astype(F32)
        return carry

    lax.fori_loop(0, shells, one_frame, 0)

    @pl.when((zone <= 1) | (zone >= zones - 2))
    def _():
        holders, held, block, _ = mine_ref.shape
        cap = jnp.where(zone < 8, 0, holders * held)
        outer = (zone == 0) | (zone == zones - 1)
        mine_part = jnp.where(outer, 0, 1)

        def one_holder(k, carry):
            for r in range(held):
                place = rows_ref[cap + k * held + r] - zone * row_count + LMAX

                @pl.when((place >= 0) & (place < frame_rows))
                def _():
                    for ref, part in ((mine_ref, mine_part), (other_ref, 1 - mine_part)):
                        for t in range(tiles):
                            frame_ref[
                                t, pl.ds(part * (16 * frame_rows) + place, 16, stride=frame_rows), :
                            ] = ref[k, r, t * 16 : (t + 1) * 16, :].astype(F32)

            return carry

        lax.fori_loop(0, holders, one_holder, 0)

    weight = weight_ref[...]

    def one_shell(s, carry):
        base = pl.multiple_of(s * frame_rows, frame_rows)
        values = jnp.concatenate(
            [frame_ref[t, pl.ds(base, frame_rows), :].astype(BF16) for t in range(tiles)], axis=1
        )
        lat_ref[s] = jnp.dot(weight, values, preferred_element_type=F32).astype(BF16)
        return carry

    lax.fori_loop(0, shells, one_shell, 0)
    group = mix_ref.shape[0] // shells
    for g in range(row_count // group):
        values = lat_ref[:, g * group : (g + 1) * group, :].reshape(shells * group, col_count)
        mixed = jnp.dot(mix_ref[...], values, preferred_element_type=F32)
        out_ref[:, g * group : (g + 1) * group, :] = mixed.astype(BF16).reshape(shells, group, col_count)


def call(kernel, name, out_shape, scalars, arrays, scratch, flops=0, moved=0):
    smem = pl.BlockSpec(memory_space=pltpu.SMEM)
    vmem = pl.BlockSpec(memory_space=pltpu.VMEM)
    many = isinstance(out_shape, tuple)
    return pl.pallas_call(
        kernel,
        out_shape=out_shape,
        in_specs=[smem] * len(scalars) + [vmem] * len(arrays),
        out_specs=(vmem,) * len(out_shape) if many else vmem,
        scratch_shapes=scratch,
        compiler_params=pltpu.CompilerParams(vmem_limit_bytes=VMEM_LIMIT),
        cost_estimate=pl.CostEstimate(flops=flops, bytes_accessed=moved, transcendentals=0),
        name=name,
    )(*scalars, *arrays)


def per_device(kernel, lon_halo, lat_reach, polar_rows, polar_shift, blend):
    shells, row_count, col_count = kernel.shape
    sectors = lax.axis_size("sector")
    zones = lax.axis_size("zone")
    zone_id = lax.axis_index("zone").astype(jnp.int32)
    sector_id = lax.axis_index("sector").astype(jnp.int32)
    place = jnp.stack([zone_id, sector_id])
    held = polar_rows.shape[0] // 2 // sectors
    tiles = col_count // LANES
    block = tiles * 16
    half = shells * row_count // 2
    struct = jax.ShapeDtypeStruct

    send, low, high = call(
        pack_kernel,
        "pack_polar_rows_and_edges",
        (
            struct((2, sectors, held, block, LANES), BF16),
            struct((half, LANES), BF16),
            struct((half, LANES), BF16),
        ),
        [place, polar_rows],
        [kernel],
        [pltpu.VMEM((tiles, shells * row_count, LANES), F32)],
        moved=4 << 20,
    )
    last = zones - 1
    given = lax.ppermute(send[1], "zone", [(0, 1), (last, last - 1)])
    up = [(i, (i + 1) % sectors) for i in range(sectors)]
    down = [(j, i) for i, j in up]
    before = lax.ppermute(high, "sector", up)
    after = lax.ppermute(low, "sector", down)
    inner = (zone_id == 1) | (zone_id == last - 1)
    parts = jnp.where(inner, given, send[0])
    circles = lax.all_to_all(parts, "sector", 0, 0, tiled=True)
    lon_smooth, lat_weight, mix = call(
        lon_kernel,
        "smooth_along_longitude",
        (
            struct((shells, row_count, col_count), BF16),
            struct((row_count, row_count + 2 * LMAX), BF16),
            struct((shells * 16, shells * 16), BF16),
        ),
        [place, lon_halo],
        [kernel, before, after, lat_reach[:, None], blend],
        [
            pltpu.VMEM((tiles + 1, shells * row_count, LANES), F32),
            pltpu.VMEM((tiles, shells * row_count, LANES), F32),
        ],
        flops=1 << 32,
        moved=16 << 20,
    )
    north = [(i, i + 1) for i in range(zones - 1)]
    south = [(j, i) for i, j in north]
    above = lax.ppermute(lon_smooth[:, row_count - LMAX :], "zone", north)
    below = lax.ppermute(lon_smooth[:, :LMAX], "zone", south)
    turned = call(
        hold_kernel,
        "smooth_and_turn_polar_circles",
        struct((sectors, held, block, LANES), BF16),
        [place, polar_rows, polar_shift, lon_halo],
        [circles],
        [pltpu.VMEM((held, 2 * sectors * block + 32, LANES), BF16)],
        flops=1 << 30,
        moved=4 << 20,
    )
    mine = lax.all_to_all(turned, "sector", 0, 0, tiled=True)
    other = lax.ppermute(mine, "zone", [(0, 1), (1, 0), (last, last - 1), (last - 1, last)])
    return call(
        lat_kernel,
        "smooth_along_latitude_and_blend",
        struct((shells, row_count, col_count), BF16),
        [place, polar_rows],
        [above, lon_smooth, below, mine, other, lat_weight, mix],
        [
            pltpu.VMEM((tiles, shells * (row_count + 2 * LMAX), LANES), F32),
            pltpu.VMEM((shells, row_count, col_count), BF16),
        ],
        flops=1 << 31,
        moved=8 << 20,
    )


def solution(mesh):
    in_specs = (P(None, "zone", "sector"), P(), P("zone"), P(), P(), P())
    out_specs = P(None, "zone", "sector")
    return jax.shard_map(
        per_device, mesh=mesh, in_specs=in_specs, out_specs=out_specs, check_vma=False
    )
```

```python
import jax
import jax.numpy as jnp
from jax import lax
from jax.experimental import pallas as pl
from jax.experimental.pallas import tpu as pltpu
from jax.sharding import PartitionSpec as P

HMAX = 48
LMAX = 32
LANES = 128
PART = 16
UNROLL = 8
F32 = jnp.float32
BF16 = jnp.bfloat16
VMEM_LIMIT = 32 * 1024 * 1024


def lanes_of(rows):
    return lax.broadcasted_iota(jnp.int32, (rows, LANES), 1)


def write_edges(x_ref, low_ref, high_ref):
    shells, row_count, col_count = x_ref.shape
    half = shells // 2
    size = half * row_count
    lane = lanes_of(size)

    def part(first, column):
        return x_ref[first : first + half, :, column : column + LANES].reshape(size, LANES).astype(F32)

    last = col_count - LANES
    low_ref[...] = jnp.where(lane < HMAX, part(0, 0), pltpu.roll(part(half, 0), HMAX, 1)).astype(BF16)
    high_ref[...] = jnp.where(
        lane < HMAX, pltpu.roll(part(0, last), HMAX, 1), pltpu.roll(part(half, last), 2 * HMAX, 1)
    ).astype(BF16)


def write_polar(half, place_ref, rows_ref, x_ref, send_ref, wide_ref):
    _, row_count, col_count = x_ref.shape
    tiles = col_count // LANES
    zone = place_ref[0]
    for t in range(tiles):
        wide_ref[t] = (
            x_ref[half * PART : (half + 1) * PART, :, t * LANES : (t + 1) * LANES]
            .reshape(PART * row_count, LANES)
            .astype(F32)
        )
    holders, held = send_ref.shape[0], send_ref.shape[1]
    cap = jnp.where(zone < 8, 0, holders * held)
    for k in range(holders):
        for r in range(held):
            row = jnp.clip(rows_ref[cap + k * held + r] - zone * row_count, 0, row_count - 1)
            for t in range(tiles):
                values = wide_ref[t, pl.ds(row, PART, stride=row_count), :]
                send_ref[k, r, t * PART : (t + 1) * PART, :] = values.astype(BF16)


def first_kernel(place_ref, rows_ref, x_ref, send_ref, low_ref, high_ref, wide_ref):
    write_polar(1, place_ref, rows_ref, x_ref, send_ref, wide_ref)
    write_edges(x_ref, low_ref, high_ref)


def second_kernel(place_ref, rows_ref, x_ref, low_ref, send_ref, wide_ref):
    write_polar(0, place_ref, rows_ref, x_ref, send_ref, wide_ref)


def band_terms(half_f):
    rate = 4.5 / (half_f * half_f)
    tap = (lanes_of(half_f.shape[0]) - HMAX).astype(F32)
    terms = jnp.where(jnp.abs(tap) <= half_f, jnp.exp(-rate * (tap * tap)), 0.0)
    return rate, jnp.broadcast_to(1.0 / jnp.sum(terms, axis=1, keepdims=True), half_f.shape)


def lon_kernel(place_ref, halo_ref, x_ref, before_ref, after_ref, reach_ref, blend_ref,
               out_ref, weight_ref, mix_ref, wide_ref, done_ref, half_ref, rate_ref, scale_ref):
    shells, row_count, col_count = x_ref.shape
    total = shells * row_count
    size = total // 2
    tiles = col_count // LANES
    zone = place_ref[0]
    for i in range(row_count):
        half_ref[i : i + 1, :] = jnp.full((1, LANES), halo_ref[zone * row_count + i], jnp.int32).astype(F32)
    rate_ref[...], scale_ref[...] = band_terms(half_ref[...])
    lane = lanes_of(size)
    for part in range(2):
        rows = pl.ds(part * size, size)
        shell = slice(part * (shells // 2), (part + 1) * (shells // 2))
        edge = before_ref[...].astype(F32)
        previous = edge if part == 0 else pltpu.roll(edge, LANES - HMAX, 1)
        for t in range(tiles):
            turned = pltpu.roll(
                x_ref[shell, :, t * LANES : (t + 1) * LANES].reshape(size, LANES).astype(F32), HMAX, 1
            )
            wide_ref[t, rows, :] = jnp.where(lane < HMAX, previous, turned)
            previous = turned
        edge = after_ref[...].astype(F32)
        edge = pltpu.roll(edge, HMAX, 1) if part == 0 else edge
        wide_ref[tiles, rows, :] = jnp.where(lane < HMAX, previous, jnp.where(lane < 2 * HMAX, edge, 0.0))
    depth = 2 * LANES
    offset = (lanes_of(depth) - lax.broadcasted_iota(jnp.int32, (depth, LANES), 0) + HMAX).astype(F32)
    square = offset * offset
    distance = jnp.abs(offset)

    def some_rows(block, carry):
        for u in range(UNROLL):
            i = block * UNROLL + u
            line = pl.ds(i, 1)
            band = jnp.where(distance <= half_ref[line, :], jnp.exp(-rate_ref[line, :] * square), 0.0)
            band = (band * scale_ref[line, :]).astype(BF16)
            values = [wide_ref[t, pl.ds(i, shells, stride=row_count), :].astype(BF16) for t in range(tiles + 1)]
            stacked = jnp.concatenate(
                [jnp.concatenate(values[:tiles], axis=0), jnp.concatenate(values[1:], axis=0)], axis=1
            )
            result = jnp.dot(stacked, band, preferred_element_type=F32)
            for t in range(tiles):
                done_ref[t, pl.ds(i, shells, stride=row_count), :] = result[t * shells : (t + 1) * shells]
        return carry

    lax.fori_loop(0, row_count // UNROLL, some_rows, 0)
    for t in range(tiles):
        out_ref[:, :, t * LANES : (t + 1) * LANES] = done_ref[t].astype(BF16).reshape(shells, row_count, LANES)
    frame_rows = weight_ref.shape[1]
    reach = reach_ref[...]
    column = lax.broadcasted_iota(jnp.int32, (row_count, frame_rows), 1)
    away = column - LMAX - lax.broadcasted_iota(jnp.int32, (row_count, frame_rows), 0)
    source = zone * row_count - LMAX + column
    valid = (jnp.abs(away) <= reach) & (source >= 0) & (source < halo_ref.shape[0])
    reach_f = reach.astype(F32)
    away_f = away.astype(F32)
    weights = jnp.where(valid, jnp.exp(-(4.5 / (reach_f * reach_f)) * (away_f * away_f)), 0.0)
    weight_ref[...] = (weights / jnp.sum(weights, axis=1, keepdims=True)).astype(BF16)
    length = mix_ref.shape[0]
    group = length // shells
    spread = (
        lax.broadcasted_iota(jnp.int32, (length, shells), 0) // group
        == lax.broadcasted_iota(jnp.int32, (length, shells), 1)
    ).astype(F32).astype(BF16)
    tall = jnp.dot(spread, blend_ref[...], preferred_element_type=F32).astype(BF16)
    full = lax.dot_general(tall, spread, (((1,), (1,)), ((), ())), preferred_element_type=F32)
    same = (
        lax.broadcasted_iota(jnp.int32, (length, length), 0) % group
        == lax.broadcasted_iota(jnp.int32, (length, length), 1) % group
    )
    mix_ref[...] = jnp.where(same, full, 0.0).astype(BF16)


def hold_kernel(place_ref, rows_ref, shift_ref, halo_ref, x_ref, after_ref, out_ref, circle_ref):
    sectors, held, block, _ = x_ref.shape
    zone, sector = place_ref[0], place_ref[1]
    cap = jnp.where(zone < 8, 0, sectors * held)
    length = sectors * block
    full_lon = length // PART * LANES
    depth = 3 * LANES
    for r in range(held):
        for copy in range(2):
            circle_ref[r, copy * length : (copy + 1) * length, :] = x_ref[:, r].reshape(length, LANES)
        circle_ref[r, 2 * length : 2 * length + 2 * PART, :] = circle_ref[r, 0 : 2 * PART, :]
    for r in range(held):
        entry = cap + sector * held + r
        half_f = jnp.full((1, LANES), halo_ref[rows_ref[entry]], jnp.int32).astype(F32)
        rate, scale = band_terms(half_f)
        start = lax.rem(2 * full_lon - shift_ref[entry] - HMAX, full_lon)
        first = start // LANES
        rest = start - first * LANES
        offset = (
            lanes_of(depth) - lax.broadcasted_iota(jnp.int32, (depth, LANES), 0) + (rest + HMAX)
        ).astype(F32)
        band = jnp.where(jnp.abs(offset) <= half_f, jnp.exp(-rate * (offset * offset)), 0.0) * scale
        values = jnp.concatenate(
            [circle_ref[r, pl.ds(pl.multiple_of((first + u) * PART, PART), length), :] for u in range(3)], axis=1
        )
        result = jnp.dot(values, band.astype(BF16), preferred_element_type=F32)
        out_ref[:, r] = result.astype(BF16).reshape(sectors, block, LANES)


def lat_kernel(place_ref, rows_ref, above_ref, own_ref, below_ref, weight_ref,
               out_ref, polar_weight_ref, pick_ref):
    shells, row_count, col_count = own_ref.shape
    frame_rows = weight_ref.shape[1]
    polar = pick_ref.shape[0]
    zone = place_ref[0]
    cap = jnp.where(zone < 8, 0, polar)
    lane = lanes_of(1)
    for p in range(polar):
        pick_ref[p : p + 1, :] = (lane == rows_ref[cap + p] - zone * row_count + LMAX).astype(F32)
    pick = pick_ref[...]
    weight = weight_ref[...]
    polar_weight_ref[...] = lax.dot_general(
        weight, pick.astype(BF16), (((1,), (1,)), ((), ())), preferred_element_type=F32
    ).astype(BF16)
    rest = (weight.astype(F32) * (1.0 - jnp.sum(pick, axis=0, keepdims=True))).astype(BF16)

    def some_shells(block, carry):
        for u in range(4):
            s = block * 4 + u
            values = jnp.concatenate([above_ref[s], own_ref[s], below_ref[s]], axis=0)
            out_ref[s] = jnp.dot(rest, values, preferred_element_type=F32)
        return carry

    lax.fori_loop(0, shells // 4, some_shells, 0)


def final_kernel(place_ref, lat_ref, mine_ref, other_ref, polar_weight_ref, mix_ref, out_ref, polar_ref, sum_ref):
    shells, row_count, col_count = lat_ref.shape
    holders, held, block, _ = mine_ref.shape
    tiles = col_count // LANES
    polar = holders * held
    zone = place_ref[0]
    outer = (zone == 0) | (zone == 15)
    mine_first = jnp.where(outer, 0, PART * polar)
    for ref, first in ((mine_ref, mine_first), (other_ref, PART * polar - mine_first)):
        for k in range(holders):
            for r in range(held):
                for t in range(tiles):
                    polar_ref[t, pl.ds(first + k * held + r, PART, stride=polar), :] = ref[
                        k, r, t * PART : (t + 1) * PART, :
                    ].astype(F32)
    weight = polar_weight_ref[...]

    def some_shells(index, carry):
        for u in range(4):
            s = index * 4 + u
            base = pl.multiple_of(s * polar, PART)
            values = jnp.concatenate(
                [polar_ref[t, pl.ds(base, polar), :].astype(BF16) for t in range(tiles)], axis=1
            )
            sum_ref[s] = lat_ref[s] + jnp.dot(weight, values, preferred_element_type=F32)
        return carry

    lax.fori_loop(0, shells // 4, some_shells, 0)
    group = mix_ref.shape[0] // shells
    mix = mix_ref[...]
    for g in range(row_count // (2 * group)):
        mixed = []
        for e in range(2):
            first = (2 * g + e) * group
            values = sum_ref[:, first : first + group, :].reshape(shells * group, col_count).astype(BF16)
            mixed.append(jnp.dot(mix, values, preferred_element_type=F32).reshape(shells, group, col_count))
        out_ref[:, 2 * g * group : 2 * (g + 1) * group, :] = jnp.concatenate(mixed, axis=1).astype(BF16)


def call(kernel, name, out_shape, scalars, arrays, scratch, flops=0, moved=0, unread=()):
    smem = pl.BlockSpec(memory_space=pltpu.SMEM)
    vmem = pl.BlockSpec(memory_space=pltpu.VMEM)
    anywhere = pl.BlockSpec(memory_space=pl.ANY)
    many = isinstance(out_shape, tuple)
    return pl.pallas_call(
        kernel,
        out_shape=out_shape,
        in_specs=[smem] * len(scalars) + [vmem] * len(arrays) + [anywhere] * len(unread),
        out_specs=(vmem,) * len(out_shape) if many else vmem,
        scratch_shapes=scratch,
        compiler_params=pltpu.CompilerParams(vmem_limit_bytes=VMEM_LIMIT),
        cost_estimate=pl.CostEstimate(flops=flops, bytes_accessed=moved, transcendentals=0),
        name=name,
    )(*scalars, *arrays, *unread)


struct = jax.ShapeDtypeStruct


def pack(place, polar_rows, kernel, sectors):
    shells, row_count, col_count = kernel.shape
    tiles = col_count // LANES
    held = polar_rows.shape[0] // 2 // sectors
    send = struct((sectors, held, tiles * PART, LANES), BF16)
    edge = struct((shells * row_count // 2, LANES), BF16)
    wide = pltpu.VMEM((tiles, PART * row_count, LANES), F32)
    given, low, high = call(
        first_kernel, "pack_half_of_shells_and_edges", (send, edge, edge), [place, polar_rows], [kernel], [wide],
        moved=4 << 20,
    )
    kept = call(
        second_kernel, "pack_other_half_of_shells", send, [place, polar_rows], [kernel], [wide],
        moved=4 << 20, unread=[low],
    )
    return given, kept, low, high


def smooth_lon(place, lon_halo, kernel, before, after, reach, blend):
    shells, row_count, col_count = kernel.shape
    tiles = col_count // LANES
    rows = pltpu.VMEM((row_count, LANES), F32)
    return call(
        lon_kernel,
        "smooth_along_longitude",
        (
            struct((shells, row_count, col_count), BF16),
            struct((row_count, row_count + 2 * LMAX), BF16),
            struct((shells * 8, shells * 8), BF16),
        ),
        [place, lon_halo],
        [kernel, before, after, reach, blend],
        [
            pltpu.VMEM((tiles + 1, shells * row_count, LANES), F32),
            pltpu.VMEM((tiles, shells * row_count, LANES), F32),
            rows,
            rows,
            rows,
        ],
        flops=1 << 32,
        moved=16 << 20,
    )


def hold(place, polar_rows, polar_shift, lon_halo, circles, after):
    sectors, held, block, _ = circles.shape
    return call(
        hold_kernel,
        "smooth_and_turn_polar_circles",
        struct(circles.shape, BF16),
        [place, polar_rows, polar_shift, lon_halo],
        [circles],
        [pltpu.VMEM((held, 2 * sectors * block + 2 * PART, LANES), BF16)],
        flops=1 << 30,
        moved=4 << 20,
        unread=[after],
    )


def smooth_lat(place, polar_rows, above, own, below, weight):
    row_count, frame_rows = weight.shape
    polar = polar_rows.shape[0] // 2
    return call(
        lat_kernel,
        "smooth_along_latitude",
        (struct(own.shape, F32), struct((row_count, polar), BF16)),
        [place, polar_rows],
        [above, own, below, weight],
        [pltpu.VMEM((polar, frame_rows), F32)],
        flops=1 << 30,
        moved=8 << 20,
    )


def finish(place, lat, mine, other, polar_weight, mix):
    shells, _, col_count = lat.shape
    polar = polar_weight.shape[1]
    return call(
        final_kernel,
        "add_polar_rows_and_blend",
        struct(lat.shape, BF16),
        [place],
        [lat, mine, other, polar_weight, mix],
        [pltpu.VMEM((col_count // LANES, shells * polar, LANES), F32), pltpu.VMEM(lat.shape, F32)],
        flops=1 << 31,
        moved=8 << 20,
    )


def per_device(kernel, lon_halo, lat_reach, polar_rows, polar_shift, blend):
    shells, row_count, col_count = kernel.shape
    sectors = lax.axis_size("sector")
    zones = lax.axis_size("zone")
    zone_id = lax.axis_index("zone").astype(jnp.int32)
    sector_id = lax.axis_index("sector").astype(jnp.int32)
    place = jnp.stack([zone_id, sector_id])
    last = zones - 1
    up = [(i, (i + 1) % sectors) for i in range(sectors)]
    down = [(j, i) for i, j in up]
    packed, kept, low, high = pack(place, polar_rows, kernel, sectors)
    given = lax.ppermute(packed, "zone", [(0, 1), (last, last - 1)])
    before = lax.ppermute(high, "sector", up)
    after = lax.ppermute(low, "sector", down)
    inner = (zone_id == 1) | (zone_id == last - 1)
    circles = lax.all_to_all(jnp.where(inner, given, kept), "sector", 0, 0, tiled=True)
    lon_smooth, lat_weight, mix = smooth_lon(place, lon_halo, kernel, before, after, lat_reach[:, None], blend)
    north = [(i, i + 1) for i in range(zones - 1)]
    south = [(j, i) for i, j in north]
    above = lax.ppermute(lon_smooth[:, row_count - LMAX :], "zone", north)
    below = lax.ppermute(lon_smooth[:, :LMAX], "zone", south)
    turned = hold(place, polar_rows, polar_shift, lon_halo, circles, lat_weight)
    mine = lax.all_to_all(turned, "sector", 0, 0, tiled=True)
    lat, polar_weight = smooth_lat(place, polar_rows, above, lon_smooth, below, lat_weight)
    mine, lat = lax.optimization_barrier((mine, lat))
    other = lax.ppermute(mine, "zone", [(0, 1), (1, 0), (last, last - 1), (last - 1, last)])
    return finish(place, lat, mine, other, polar_weight, mix)


def solution(mesh):
    in_specs = (P(None, "zone", "sector"), P(), P("zone"), P(), P(), P())
    out_specs = P(None, "zone", "sector")
    return jax.shard_map(
        per_device, mesh=mesh, in_specs=in_specs, out_specs=out_specs, check_vma=False
    )
```

```python
import jax
import jax.numpy as jnp
from jax import lax
from jax.experimental import pallas as pl
from jax.experimental.pallas import tpu as pltpu
from jax.sharding import PartitionSpec as P

HMAX = 48
LMAX = 32
LANES = 128
PART = 16
UNROLL = 8
F32 = jnp.float32
BF16 = jnp.bfloat16


def lanes_of(rows):
    return lax.broadcasted_iota(jnp.int32, (rows, LANES), 1)


def edge_kernel(x_ref, low_ref, high_ref, tile_ref, sems):
    shells, row_count, col_count = x_ref.shape
    half = shells // 2
    size = half * row_count
    lane = lanes_of(size)
    first = (0, col_count - LANES)
    copies = [
        pltpu.make_async_copy(x_ref.at[:, :, pl.ds(first[e], LANES)], tile_ref.at[e], sems.at[e]) for e in range(2)
    ]
    for copy in copies:
        copy.start()

    def part(e, shell):
        return tile_ref[e, shell : shell + half].reshape(size, LANES).astype(F32)

    copies[0].wait()
    low_ref[...] = jnp.where(lane < HMAX, part(0, 0), pltpu.roll(part(0, half), HMAX, 1)).astype(BF16)
    copies[1].wait()
    high_ref[...] = jnp.where(
        lane < HMAX, pltpu.roll(part(1, 0), HMAX, 1), pltpu.roll(part(1, half), 2 * HMAX, 1)
    ).astype(BF16)


def write_polar(half, place_ref, rows_ref, x_ref, send_ref, wide_ref):
    _, row_count, col_count = x_ref.shape
    tiles = col_count // LANES
    zone = place_ref[0]
    for t in range(tiles):
        wide_ref[t] = (
            x_ref[half * PART : (half + 1) * PART, :, t * LANES : (t + 1) * LANES]
            .reshape(PART * row_count, LANES)
            .astype(F32)
        )
    holders, held = send_ref.shape[0], send_ref.shape[1]
    cap = jnp.where(zone < 8, 0, holders * held)
    for k in range(holders):
        for r in range(held):
            row = jnp.clip(rows_ref[cap + k * held + r] - zone * row_count, 0, row_count - 1)
            for t in range(tiles):
                values = wide_ref[t, pl.ds(row, PART, stride=row_count), :]
                send_ref[k, r, t * PART : (t + 1) * PART, :] = values.astype(BF16)


def first_kernel(place_ref, rows_ref, x_ref, low_ref, send_ref, wide_ref):
    write_polar(1, place_ref, rows_ref, x_ref, send_ref, wide_ref)


def second_kernel(place_ref, rows_ref, x_ref, given_ref, send_ref, wide_ref):
    write_polar(0, place_ref, rows_ref, x_ref, send_ref, wide_ref)


def band_terms(half_f):
    rate = 4.5 / (half_f * half_f)
    tap = (lanes_of(half_f.shape[0]) - HMAX).astype(F32)
    terms = jnp.where(jnp.abs(tap) <= half_f, jnp.exp(-rate * (tap * tap)), 0.0)
    return rate, jnp.broadcast_to(1.0 / jnp.sum(terms, axis=1, keepdims=True), half_f.shape)


def lon_kernel(place_ref, halo_ref, x_ref, before_ref, after_ref, reach_ref, blend_ref,
               out_ref, weight_ref, mix_ref, wide_ref, done_ref, half_ref, rate_ref, scale_ref):
    shells, row_count, col_count = x_ref.shape
    total = shells * row_count
    size = total // 2
    tiles = col_count // LANES
    zone = place_ref[0]
    for i in range(row_count):
        half_ref[i : i + 1, :] = jnp.full((1, LANES), halo_ref[zone * row_count + i], jnp.int32).astype(F32)
    rate_ref[...], scale_ref[...] = band_terms(half_ref[...])
    lane = lanes_of(size)
    for part in range(2):
        rows = pl.ds(part * size, size)
        shell = slice(part * (shells // 2), (part + 1) * (shells // 2))
        edge = before_ref[...].astype(F32)
        previous = edge if part == 0 else pltpu.roll(edge, LANES - HMAX, 1)
        for t in range(tiles):
            turned = pltpu.roll(
                x_ref[shell, :, t * LANES : (t + 1) * LANES].reshape(size, LANES).astype(F32), HMAX, 1
            )
            wide_ref[t, rows, :] = jnp.where(lane < HMAX, previous, turned)
            previous = turned
        edge = after_ref[...].astype(F32)
        edge = pltpu.roll(edge, HMAX, 1) if part == 0 else edge
        wide_ref[tiles, rows, :] = jnp.where(lane < HMAX, previous, jnp.where(lane < 2 * HMAX, edge, 0.0))
    depth = 2 * LANES
    offset = (lanes_of(depth) - lax.broadcasted_iota(jnp.int32, (depth, LANES), 0) + HMAX).astype(F32)
    square = offset * offset
    distance = jnp.abs(offset)

    def some_rows(block, carry):
        for u in range(UNROLL):
            i = block * UNROLL + u
            line = pl.ds(i, 1)
            band = jnp.where(distance <= half_ref[line, :], jnp.exp(-rate_ref[line, :] * square), 0.0)
            band = (band * scale_ref[line, :]).astype(BF16)
            values = [wide_ref[t, pl.ds(i, shells, stride=row_count), :].astype(BF16) for t in range(tiles + 1)]
            stacked = jnp.concatenate(
                [jnp.concatenate(values[:tiles], axis=0), jnp.concatenate(values[1:], axis=0)], axis=1
            )
            result = jnp.dot(stacked, band, preferred_element_type=F32)
            for t in range(tiles):
                done_ref[t, pl.ds(i, shells, stride=row_count), :] = result[t * shells : (t + 1) * shells]
        return carry

    lax.fori_loop(0, row_count // UNROLL, some_rows, 0)
    for t in range(tiles):
        out_ref[:, :, t * LANES : (t + 1) * LANES] = done_ref[t].astype(BF16).reshape(shells, row_count, LANES)
    frame_rows = weight_ref.shape[1]
    reach = reach_ref[...]
    column = lax.broadcasted_iota(jnp.int32, (row_count, frame_rows), 1)
    away = column - LMAX - lax.broadcasted_iota(jnp.int32, (row_count, frame_rows), 0)
    source = zone * row_count - LMAX + column
    valid = (jnp.abs(away) <= reach) & (source >= 0) & (source < halo_ref.shape[0])
    reach_f = reach.astype(F32)
    away_f = away.astype(F32)
    weights = jnp.where(valid, jnp.exp(-(4.5 / (reach_f * reach_f)) * (away_f * away_f)), 0.0)
    weight_ref[...] = (weights / jnp.sum(weights, axis=1, keepdims=True)).astype(BF16)
    length = mix_ref.shape[0]
    group = length // shells
    spread = (
        lax.broadcasted_iota(jnp.int32, (length, shells), 0) // group
        == lax.broadcasted_iota(jnp.int32, (length, shells), 1)
    ).astype(F32).astype(BF16)
    tall = jnp.dot(spread, blend_ref[...], preferred_element_type=F32).astype(BF16)
    full = lax.dot_general(tall, spread, (((1,), (1,)), ((), ())), preferred_element_type=F32)
    same = (
        lax.broadcasted_iota(jnp.int32, (length, length), 0) % group
        == lax.broadcasted_iota(jnp.int32, (length, length), 1) % group
    )
    mix_ref[...] = jnp.where(same, full, 0.0).astype(BF16)


def hold_kernel(place_ref, rows_ref, shift_ref, halo_ref, x_ref, after_ref, out_ref, circle_ref):
    sectors, held, block, _ = x_ref.shape
    zone, sector = place_ref[0], place_ref[1]
    cap = jnp.where(zone < 8, 0, sectors * held)
    length = sectors * block
    full_lon = length // PART * LANES
    depth = 3 * LANES
    for r in range(held):
        for copy in range(2):
            circle_ref[r, copy * length : (copy + 1) * length, :] = x_ref[:, r].reshape(length, LANES)
        circle_ref[r, 2 * length : 2 * length + 2 * PART, :] = circle_ref[r, 0 : 2 * PART, :]
    for r in range(held):
        entry = cap + sector * held + r
        half_f = jnp.full((1, LANES), halo_ref[rows_ref[entry]], jnp.int32).astype(F32)
        rate, scale = band_terms(half_f)
        start = lax.rem(2 * full_lon - shift_ref[entry] - HMAX, full_lon)
        first = start // LANES
        rest = start - first * LANES
        offset = (
            lanes_of(depth) - lax.broadcasted_iota(jnp.int32, (depth, LANES), 0) + (rest + HMAX)
        ).astype(F32)
        band = jnp.where(jnp.abs(offset) <= half_f, jnp.exp(-rate * (offset * offset)), 0.0) * scale
        values = jnp.concatenate(
            [circle_ref[r, pl.ds(pl.multiple_of((first + u) * PART, PART), length), :] for u in range(3)], axis=1
        )
        result = jnp.dot(values, band.astype(BF16), preferred_element_type=F32)
        out_ref[:, r] = result.astype(BF16).reshape(sectors, block, LANES)


def lat_kernel(place_ref, rows_ref, above_ref, own_ref, below_ref, weight_ref,
               out_ref, polar_weight_ref, pick_ref):
    shells, row_count, col_count = own_ref.shape
    frame_rows = weight_ref.shape[1]
    polar = pick_ref.shape[0]
    zone = place_ref[0]
    cap = jnp.where(zone < 8, 0, polar)
    lane = lanes_of(1)
    for p in range(polar):
        pick_ref[p : p + 1, :] = (lane == rows_ref[cap + p] - zone * row_count + LMAX).astype(F32)
    pick = pick_ref[...]
    weight = weight_ref[...]
    polar_weight_ref[...] = lax.dot_general(
        weight, pick.astype(BF16), (((1,), (1,)), ((), ())), preferred_element_type=F32
    ).astype(BF16)
    rest = (weight.astype(F32) * (1.0 - jnp.sum(pick, axis=0, keepdims=True))).astype(BF16)

    def some_shells(block, carry):
        for u in range(4):
            s = block * 4 + u
            values = jnp.concatenate([above_ref[s], own_ref[s], below_ref[s]], axis=0)
            out_ref[s] = jnp.dot(rest, values, preferred_element_type=F32)
        return carry

    lax.fori_loop(0, shells // 4, some_shells, 0)


def final_kernel(place_ref, mine_ref, other_ref, polar_weight_ref, mix_ref, lat_ref,
                 out_ref, polar_ref, sum_ref, sem):
    shells, row_count, col_count = lat_ref.shape
    holders, held = mine_ref.shape[:2]
    tiles = col_count // LANES
    polar = holders * held
    fetch = pltpu.make_async_copy(lat_ref, sum_ref, sem)
    fetch.start()
    zone = place_ref[0]
    outer = (zone == 0) | (zone == 15)
    mine_first = jnp.where(outer, 0, PART * polar)
    for ref, first in ((mine_ref, mine_first), (other_ref, PART * polar - mine_first)):
        for k in range(holders):
            for r in range(held):
                for t in range(tiles):
                    polar_ref[t, pl.ds(first + k * held + r, PART, stride=polar), :] = ref[
                        k, r, t * PART : (t + 1) * PART, :
                    ].astype(F32)
    weight = polar_weight_ref[...]
    fetch.wait()

    def some_shells(index, carry):
        for u in range(4):
            s = index * 4 + u
            base = pl.multiple_of(s * polar, PART)
            values = jnp.concatenate(
                [polar_ref[t, pl.ds(base, polar), :].astype(BF16) for t in range(tiles)], axis=1
            )
            sum_ref[s] += jnp.dot(weight, values, preferred_element_type=F32)
        return carry

    lax.fori_loop(0, shells // 4, some_shells, 0)
    group = mix_ref.shape[0] // shells
    mix = mix_ref[...]
    for g in range(row_count // (2 * group)):
        mixed = []
        for e in range(2):
            first = (2 * g + e) * group
            values = sum_ref[:, first : first + group, :].reshape(shells * group, col_count).astype(BF16)
            mixed.append(jnp.dot(mix, values, preferred_element_type=F32).reshape(shells, group, col_count))
        out_ref[:, 2 * g * group : 2 * (g + 1) * group, :] = jnp.concatenate(mixed, axis=1).astype(BF16)


def call(kernel, name, out_shape, scalars, arrays, scratch, flops=0, moved=0, direct=(), mib=16):
    smem = pl.BlockSpec(memory_space=pltpu.SMEM)
    vmem = pl.BlockSpec(memory_space=pltpu.VMEM)
    anywhere = pl.BlockSpec(memory_space=pl.ANY)
    many = isinstance(out_shape, tuple)
    return pl.pallas_call(
        kernel,
        out_shape=out_shape,
        in_specs=[smem] * len(scalars) + [vmem] * len(arrays) + [anywhere] * len(direct),
        out_specs=(vmem,) * len(out_shape) if many else vmem,
        scratch_shapes=scratch,
        compiler_params=pltpu.CompilerParams(vmem_limit_bytes=mib << 20),
        cost_estimate=pl.CostEstimate(flops=flops, bytes_accessed=moved, transcendentals=0),
        name=name,
    )(*scalars, *arrays, *direct)


struct = jax.ShapeDtypeStruct


def pack(place, polar_rows, kernel, sectors):
    shells, row_count, col_count = kernel.shape
    tiles = col_count // LANES
    held = polar_rows.shape[0] // 2 // sectors
    send = struct((sectors, held, tiles * PART, LANES), BF16)
    edge = struct((shells * row_count // 2, LANES), BF16)
    wide = pltpu.VMEM((tiles, PART * row_count, LANES), F32)
    tile = pltpu.VMEM((2, shells, row_count, LANES), BF16)
    low, high = call(
        edge_kernel, "cut_edges", (edge, edge), [], [], [tile, pltpu.SemaphoreType.DMA((2,))],
        moved=4 << 20, direct=[kernel],
    )
    given = call(
        first_kernel, "pack_half_of_shells", send, [place, polar_rows], [kernel], [wide],
        moved=4 << 20, direct=[low],
    )
    kept = call(
        second_kernel, "pack_other_half_of_shells", send, [place, polar_rows], [kernel], [wide],
        moved=4 << 20, direct=[given],
    )
    return given, kept, low, high


def smooth_lon(place, lon_halo, kernel, before, after, reach, blend):
    shells, row_count, col_count = kernel.shape
    tiles = col_count // LANES
    rows = pltpu.VMEM((row_count, LANES), F32)
    return call(
        lon_kernel,
        "smooth_along_longitude",
        (
            struct((shells, row_count, col_count), BF16),
            struct((row_count, row_count + 2 * LMAX), BF16),
            struct((shells * 8, shells * 8), BF16),
        ),
        [place, lon_halo],
        [kernel, before, after, reach, blend],
        [
            pltpu.VMEM((tiles + 1, shells * row_count, LANES), F32),
            pltpu.VMEM((tiles, shells * row_count, LANES), F32),
            rows,
            rows,
            rows,
        ],
        flops=1 << 32,
        moved=16 << 20,
        mib=20,
    )


def hold(place, polar_rows, polar_shift, lon_halo, circles, after):
    sectors, held, block, _ = circles.shape
    return call(
        hold_kernel,
        "smooth_and_turn_polar_circles",
        struct(circles.shape, BF16),
        [place, polar_rows, polar_shift, lon_halo],
        [circles],
        [pltpu.VMEM((held, 2 * sectors * block + 2 * PART, LANES), BF16)],
        flops=1 << 30,
        moved=4 << 20,
        direct=[after],
    )


def smooth_lat(place, polar_rows, above, own, below, weight):
    row_count, frame_rows = weight.shape
    polar = polar_rows.shape[0] // 2
    return call(
        lat_kernel,
        "smooth_along_latitude",
        (struct(own.shape, F32), struct((row_count, polar), BF16)),
        [place, polar_rows],
        [above, own, below, weight],
        [pltpu.VMEM((polar, frame_rows), F32)],
        flops=1 << 30,
        moved=8 << 20,
    )


def finish(place, lat, mine, other, polar_weight, mix):
    shells, _, col_count = lat.shape
    polar = polar_weight.shape[1]
    return call(
        final_kernel,
        "add_polar_rows_and_blend",
        struct(lat.shape, BF16),
        [place],
        [mine, other, polar_weight, mix],
        [
            pltpu.VMEM((col_count // LANES, shells * polar, LANES), F32),
            pltpu.VMEM(lat.shape, F32),
            pltpu.SemaphoreType.DMA,
        ],
        flops=1 << 31,
        moved=8 << 20,
        direct=[lat],
        mib=50,
    )


def per_device(kernel, lon_halo, lat_reach, polar_rows, polar_shift, blend):
    shells, row_count, col_count = kernel.shape
    sectors = lax.axis_size("sector")
    zones = lax.axis_size("zone")
    zone_id = lax.axis_index("zone").astype(jnp.int32)
    sector_id = lax.axis_index("sector").astype(jnp.int32)
    place = jnp.stack([zone_id, sector_id])
    last = zones - 1
    up = [(i, (i + 1) % sectors) for i in range(sectors)]
    down = [(j, i) for i, j in up]
    packed, kept, low, high = pack(place, polar_rows, kernel, sectors)
    given = lax.ppermute(packed, "zone", [(0, 1), (last, last - 1)])
    before = lax.ppermute(high, "sector", up)
    after = lax.ppermute(low, "sector", down)
    inner = (zone_id == 1) | (zone_id == last - 1)
    parts, before, after = lax.optimization_barrier((jnp.where(inner, given, kept), before, after))
    circles = lax.all_to_all(parts, "sector", 0, 0, tiled=True)
    lon_smooth, lat_weight, mix = smooth_lon(place, lon_halo, kernel, before, after, lat_reach[:, None], blend)
    north = [(i, i + 1) for i in range(zones - 1)]
    south = [(j, i) for i, j in north]
    above = lax.ppermute(lon_smooth[:, row_count - LMAX :], "zone", north)
    below = lax.ppermute(lon_smooth[:, :LMAX], "zone", south)
    turned = hold(place, polar_rows, polar_shift, lon_halo, circles, lat_weight)
    mine = lax.all_to_all(turned, "sector", 0, 0, tiled=True)
    lat, polar_weight = smooth_lat(place, polar_rows, above, lon_smooth, below, lat_weight)
    mine, lat = lax.optimization_barrier((mine, lat))
    other = lax.ppermute(mine, "zone", [(0, 1), (1, 0), (last, last - 1), (last - 1, last)])
    return finish(place, lat, mine, other, polar_weight, mix)


def solution(mesh):
    in_specs = (P(None, "zone", "sector"), P(), P("zone"), P(), P(), P())
    out_specs = P(None, "zone", "sector")
    return jax.shard_map(
        per_device, mesh=mesh, in_specs=in_specs, out_specs=out_specs, check_vma=False
    )
```

```python
import jax
import jax.numpy as jnp
from jax import lax
from jax.experimental import pallas as pl
from jax.experimental.pallas import tpu as pltpu
from jax.sharding import PartitionSpec as P

HMAX = 48
LMAX = 32
LANES = 128
PART = 16
UNROLL = 8
F32 = jnp.float32
BF16 = jnp.bfloat16


def lanes_of(rows):
    return lax.broadcasted_iota(jnp.int32, (rows, LANES), 1)


def edge_kernel(place_ref, x_ref, near_ref, far_ref, tile_ref, sems):
    shells, row_count, col_count = x_ref.shape
    half = shells // 2
    size = half * row_count
    lane = lanes_of(size)
    first = (0, col_count - LANES)
    copies = [
        pltpu.make_async_copy(x_ref.at[:, :, pl.ds(first[e], LANES)], tile_ref.at[e], sems.at[e]) for e in range(2)
    ]
    for copy in copies:
        copy.start()

    def part(e, shell):
        return tile_ref[e, shell : shell + half].reshape(size, LANES).astype(F32)

    even = lax.rem(place_ref[1], 2) == 0
    copies[0].wait()
    low = jnp.where(lane < HMAX, part(0, 0), pltpu.roll(part(0, half), HMAX, 1))
    copies[1].wait()
    high = jnp.where(lane < HMAX, pltpu.roll(part(1, 0), HMAX, 1), pltpu.roll(part(1, half), 2 * HMAX, 1))
    near_ref[...] = jnp.where(even, high, low).astype(BF16)
    far_ref[...] = jnp.where(even, low, high).astype(BF16)


def write_polar(half, place_ref, rows_ref, x_ref, send_ref, wide_ref):
    _, row_count, col_count = x_ref.shape
    tiles = col_count // LANES
    zone = place_ref[0]
    for t in range(tiles):
        wide_ref[t] = (
            x_ref[half * PART : (half + 1) * PART, :, t * LANES : (t + 1) * LANES]
            .reshape(PART * row_count, LANES)
            .astype(F32)
        )
    holders, held = send_ref.shape[0], send_ref.shape[1]
    cap = jnp.where(zone < 8, 0, holders * held)
    for k in range(holders):
        for r in range(held):
            row = jnp.clip(rows_ref[cap + k * held + r] - zone * row_count, 0, row_count - 1)
            for t in range(tiles):
                values = wide_ref[t, pl.ds(row, PART, stride=row_count), :]
                send_ref[k, r, t * PART : (t + 1) * PART, :] = values.astype(BF16)


def first_kernel(place_ref, rows_ref, x_ref, far_ref, send_ref, wide_ref):
    write_polar(1, place_ref, rows_ref, x_ref, send_ref, wide_ref)


def second_kernel(place_ref, rows_ref, x_ref, given_ref, send_ref, wide_ref):
    write_polar(0, place_ref, rows_ref, x_ref, send_ref, wide_ref)


def band_terms(half_f):
    rate = 4.5 / (half_f * half_f)
    tap = (lanes_of(half_f.shape[0]) - HMAX).astype(F32)
    terms = jnp.where(jnp.abs(tap) <= half_f, jnp.exp(-rate * (tap * tap)), 0.0)
    return rate, jnp.broadcast_to(1.0 / jnp.sum(terms, axis=1, keepdims=True), half_f.shape)


def lon_kernel(place_ref, halo_ref, x_ref, near_ref, far_ref, reach_ref, blend_ref,
               out_ref, near_rows_ref, far_rows_ref, weight_ref, mix_ref, wide_ref, done_ref, half_ref, rate_ref, scale_ref):
    shells, row_count, col_count = x_ref.shape
    total = shells * row_count
    size = total // 2
    tiles = col_count // LANES
    zone = place_ref[0]
    for i in range(row_count):
        half_ref[i : i + 1, :] = jnp.full((1, LANES), halo_ref[zone * row_count + i], jnp.int32).astype(F32)
    rate_ref[...], scale_ref[...] = band_terms(half_ref[...])
    lane = lanes_of(size)
    even = lax.rem(place_ref[1], 2) == 0
    near = near_ref[...].astype(F32)
    far = far_ref[...].astype(F32)
    before = jnp.where(even, far, near)
    after = jnp.where(even, near, far)
    for part in range(2):
        rows = pl.ds(part * size, size)
        shell = slice(part * (shells // 2), (part + 1) * (shells // 2))
        previous = before if part == 0 else pltpu.roll(before, LANES - HMAX, 1)
        for t in range(tiles):
            turned = pltpu.roll(
                x_ref[shell, :, t * LANES : (t + 1) * LANES].reshape(size, LANES).astype(F32), HMAX, 1
            )
            wide_ref[t, rows, :] = jnp.where(lane < HMAX, previous, turned)
            previous = turned
        edge = pltpu.roll(after, HMAX, 1) if part == 0 else after
        wide_ref[tiles, rows, :] = jnp.where(lane < HMAX, previous, jnp.where(lane < 2 * HMAX, edge, 0.0))
    depth = 2 * LANES
    offset = (lanes_of(depth) - lax.broadcasted_iota(jnp.int32, (depth, LANES), 0) + HMAX).astype(F32)
    square = offset * offset
    distance = jnp.abs(offset)

    def some_rows(block, carry):
        for u in range(UNROLL):
            i = block * UNROLL + u
            line = pl.ds(i, 1)
            band = jnp.where(distance <= half_ref[line, :], jnp.exp(-rate_ref[line, :] * square), 0.0)
            band = (band * scale_ref[line, :]).astype(BF16)
            values = [wide_ref[t, pl.ds(i, shells, stride=row_count), :].astype(BF16) for t in range(tiles + 1)]
            stacked = jnp.concatenate(
                [jnp.concatenate(values[:tiles], axis=0), jnp.concatenate(values[1:], axis=0)], axis=1
            )
            result = jnp.dot(stacked, band, preferred_element_type=F32)
            for t in range(tiles):
                done_ref[t, pl.ds(i, shells, stride=row_count), :] = result[t * shells : (t + 1) * shells]
        return carry

    lax.fori_loop(0, row_count // UNROLL, some_rows, 0)
    for t in range(tiles):
        out_ref[:, :, t * LANES : (t + 1) * LANES] = done_ref[t].astype(BF16).reshape(shells, row_count, LANES)
    odd = lax.rem(zone, 2)
    last = row_count - LMAX
    near_rows_ref[...] = out_ref[:, pl.ds(pl.multiple_of((1 - odd) * last, LMAX), LMAX), :]
    far_rows_ref[...] = out_ref[:, pl.ds(pl.multiple_of(odd * last, LMAX), LMAX), :]
    frame_rows = weight_ref.shape[1]
    reach = reach_ref[...]
    column = lax.broadcasted_iota(jnp.int32, (row_count, frame_rows), 1)
    away = column - LMAX - lax.broadcasted_iota(jnp.int32, (row_count, frame_rows), 0)
    source = zone * row_count - LMAX + column
    valid = (jnp.abs(away) <= reach) & (source >= 0) & (source < halo_ref.shape[0])
    reach_f = reach.astype(F32)
    away_f = away.astype(F32)
    weights = jnp.where(valid, jnp.exp(-(4.5 / (reach_f * reach_f)) * (away_f * away_f)), 0.0)
    weight_ref[...] = (weights / jnp.sum(weights, axis=1, keepdims=True)).astype(BF16)
    length = mix_ref.shape[0]
    group = length // shells
    spread = (
        lax.broadcasted_iota(jnp.int32, (length, shells), 0) // group
        == lax.broadcasted_iota(jnp.int32, (length, shells), 1)
    ).astype(F32).astype(BF16)
    tall = jnp.dot(spread, blend_ref[...], preferred_element_type=F32).astype(BF16)
    full = lax.dot_general(tall, spread, (((1,), (1,)), ((), ())), preferred_element_type=F32)
    same = (
        lax.broadcasted_iota(jnp.int32, (length, length), 0) % group
        == lax.broadcasted_iota(jnp.int32, (length, length), 1) % group
    )
    mix_ref[...] = jnp.where(same, full, 0.0).astype(BF16)


def hold_kernel(place_ref, rows_ref, shift_ref, halo_ref, x_ref, after_ref, out_ref, circle_ref):
    sectors, held, block, _ = x_ref.shape
    zone, sector = place_ref[0], place_ref[1]
    cap = jnp.where(zone < 8, 0, sectors * held)
    length = sectors * block
    full_lon = length // PART * LANES
    depth = 3 * LANES
    for r in range(held):
        for copy in range(2):
            circle_ref[r, copy * length : (copy + 1) * length, :] = x_ref[:, r].reshape(length, LANES)
        circle_ref[r, 2 * length : 2 * length + 2 * PART, :] = circle_ref[r, 0 : 2 * PART, :]
    for r in range(held):
        entry = cap + sector * held + r
        half_f = jnp.full((1, LANES), halo_ref[rows_ref[entry]], jnp.int32).astype(F32)
        rate, scale = band_terms(half_f)
        start = lax.rem(2 * full_lon - shift_ref[entry] - HMAX, full_lon)
        first = start // LANES
        rest = start - first * LANES
        offset = (
            lanes_of(depth) - lax.broadcasted_iota(jnp.int32, (depth, LANES), 0) + (rest + HMAX)
        ).astype(F32)
        band = jnp.where(jnp.abs(offset) <= half_f, jnp.exp(-rate * (offset * offset)), 0.0) * scale
        values = jnp.concatenate(
            [circle_ref[r, pl.ds(pl.multiple_of((first + u) * PART, PART), length), :] for u in range(3)], axis=1
        )
        result = jnp.dot(values, band.astype(BF16), preferred_element_type=F32)
        out_ref[:, r] = result.astype(BF16).reshape(sectors, block, LANES)


def lat_kernel(place_ref, rows_ref, near_ref, own_ref, far_ref, weight_ref,
               out_ref, polar_weight_ref, pick_ref):
    shells, row_count, col_count = own_ref.shape
    frame_rows = weight_ref.shape[1]
    polar = pick_ref.shape[0]
    zone = place_ref[0]
    cap = jnp.where(zone < 8, 0, polar)
    lane = lanes_of(1)
    for p in range(polar):
        pick_ref[p : p + 1, :] = (lane == rows_ref[cap + p] - zone * row_count + LMAX).astype(F32)
    pick = pick_ref[...]
    weight = weight_ref[...]
    polar_weight_ref[...] = lax.dot_general(
        weight, pick.astype(BF16), (((1,), (1,)), ((), ())), preferred_element_type=F32
    ).astype(BF16)
    rest = weight.astype(F32) * (1.0 - jnp.sum(pick, axis=0, keepdims=True))
    wide = lanes_of(row_count)
    turned = jnp.where(
        wide < LMAX,
        pltpu.roll(rest, LMAX, 1),
        jnp.where(wide < frame_rows - LMAX, rest, pltpu.roll(rest, frame_rows - LMAX, 1)),
    )
    rest = jnp.where(lax.rem(zone, 2) == 0, turned, rest).astype(BF16)

    def some_shells(block, carry):
        for u in range(4):
            s = block * 4 + u
            values = jnp.concatenate([near_ref[s], own_ref[s], far_ref[s]], axis=0)
            out_ref[s] = jnp.dot(rest, values, preferred_element_type=F32)
        return carry

    lax.fori_loop(0, shells // 4, some_shells, 0)


def final_kernel(place_ref, mine_ref, other_ref, polar_weight_ref, mix_ref, lat_ref,
                 out_ref, polar_ref, sum_ref, stage_ref, sem, sems):
    shells, row_count, col_count = lat_ref.shape
    holders, held = mine_ref.shape[:2]
    tiles = col_count // LANES
    polar = holders * held
    fetch = pltpu.make_async_copy(lat_ref, sum_ref, sem)
    fetch.start()
    zone = place_ref[0]
    outer = (zone == 0) | (zone == 15)
    mine_first = jnp.where(outer, 0, PART * polar)
    for ref, first in ((mine_ref, mine_first), (other_ref, PART * polar - mine_first)):
        for k in range(holders):
            for r in range(held):
                for t in range(tiles):
                    polar_ref[t, pl.ds(first + k * held + r, PART, stride=polar), :] = ref[
                        k, r, t * PART : (t + 1) * PART, :
                    ].astype(F32)
    weight = polar_weight_ref[...]
    fetch.wait()

    def some_shells(index, carry):
        for u in range(4):
            s = index * 4 + u
            base = pl.multiple_of(s * polar, PART)
            values = jnp.concatenate(
                [polar_ref[t, pl.ds(base, polar), :].astype(BF16) for t in range(tiles)], axis=1
            )
            sum_ref[s] += jnp.dot(weight, values, preferred_element_type=F32)
        return carry

    lax.fori_loop(0, shells // 4, some_shells, 0)
    group = mix_ref.shape[0] // shells
    mix = mix_ref[...]
    stores = []
    for g in range(row_count // (2 * group)):
        mixed = []
        for e in range(2):
            first = (2 * g + e) * group
            values = sum_ref[:, first : first + group, :].reshape(shells * group, col_count).astype(BF16)
            mixed.append(jnp.dot(mix, values, preferred_element_type=F32).reshape(shells, group, col_count))
        rows = pl.ds(2 * g * group, 2 * group)
        stage_ref[:, rows, :] = jnp.concatenate(mixed, axis=1).astype(BF16)
        stores.append(pltpu.make_async_copy(stage_ref.at[:, rows], out_ref.at[:, rows], sems.at[g]))
        stores[-1].start()
    for store in stores:
        store.wait()


def call(kernel, name, out_shape, scalars, arrays, scratch, flops=0, moved=0, direct=(), far=False, mib=16):
    smem = pl.BlockSpec(memory_space=pltpu.SMEM)
    vmem = pl.BlockSpec(memory_space=pltpu.VMEM)
    anywhere = pl.BlockSpec(memory_space=pl.ANY)
    many = isinstance(out_shape, tuple)
    return pl.pallas_call(
        kernel,
        out_shape=out_shape,
        in_specs=[smem] * len(scalars) + [vmem] * len(arrays) + [anywhere] * len(direct),
        out_specs=(vmem,) * len(out_shape) if many else anywhere if far else vmem,
        scratch_shapes=scratch,
        compiler_params=pltpu.CompilerParams(vmem_limit_bytes=mib << 20),
        cost_estimate=pl.CostEstimate(flops=flops, bytes_accessed=moved, transcendentals=0),
        name=name,
    )(*scalars, *arrays, *direct)


struct = jax.ShapeDtypeStruct


def pack(place, polar_rows, kernel, sectors):
    shells, row_count, col_count = kernel.shape
    tiles = col_count // LANES
    held = polar_rows.shape[0] // 2 // sectors
    send = struct((sectors, held, tiles * PART, LANES), BF16)
    edge = struct((shells * row_count // 2, LANES), BF16)
    wide = pltpu.VMEM((tiles, PART * row_count, LANES), F32)
    tile = pltpu.VMEM((2, shells, row_count, LANES), BF16)
    near, far = call(
        edge_kernel, "cut_edges", (edge, edge), [place], [], [tile, pltpu.SemaphoreType.DMA((2,))],
        moved=4 << 20, direct=[kernel],
    )
    given = call(
        first_kernel, "pack_half_of_shells", send, [place, polar_rows], [kernel], [wide],
        moved=4 << 20, direct=[far],
    )
    kept = call(
        second_kernel, "pack_other_half_of_shells", send, [place, polar_rows], [kernel], [wide],
        moved=4 << 20, direct=[given],
    )
    return given, kept, near, far


def smooth_lon(place, lon_halo, kernel, near, far, reach, blend):
    shells, row_count, col_count = kernel.shape
    tiles = col_count // LANES
    rows = pltpu.VMEM((row_count, LANES), F32)
    return call(
        lon_kernel,
        "smooth_along_longitude",
        (
            struct((shells, row_count, col_count), BF16),
            struct((shells, LMAX, col_count), BF16),
            struct((shells, LMAX, col_count), BF16),
            struct((row_count, row_count + 2 * LMAX), BF16),
            struct((shells * 8, shells * 8), BF16),
        ),
        [place, lon_halo],
        [kernel, near, far, reach, blend],
        [
            pltpu.VMEM((tiles + 1, shells * row_count, LANES), F32),
            pltpu.VMEM((tiles, shells * row_count, LANES), F32),
            rows,
            rows,
            rows,
        ],
        flops=1 << 32,
        moved=16 << 20,
        mib=20,
    )


def hold(place, polar_rows, polar_shift, lon_halo, circles, after):
    sectors, held, block, _ = circles.shape
    return call(
        hold_kernel,
        "smooth_and_turn_polar_circles",
        struct(circles.shape, BF16),
        [place, polar_rows, polar_shift, lon_halo],
        [circles],
        [pltpu.VMEM((held, 2 * sectors * block + 2 * PART, LANES), BF16)],
        flops=1 << 30,
        moved=4 << 20,
        direct=[after],
    )


def smooth_lat(place, polar_rows, near, own, far, weight):
    row_count, frame_rows = weight.shape
    polar = polar_rows.shape[0] // 2
    return call(
        lat_kernel,
        "smooth_along_latitude",
        (struct(own.shape, F32), struct((row_count, polar), BF16)),
        [place, polar_rows],
        [near, own, far, weight],
        [pltpu.VMEM((polar, frame_rows), F32)],
        flops=1 << 30,
        moved=8 << 20,
    )


def finish(place, lat, mine, other, polar_weight, mix):
    shells, _, col_count = lat.shape
    polar = polar_weight.shape[1]
    return call(
        final_kernel,
        "add_polar_rows_and_blend",
        struct(lat.shape, BF16),
        [place],
        [mine, other, polar_weight, mix],
        [
            pltpu.VMEM((col_count // LANES, shells * polar, LANES), F32),
            pltpu.VMEM(lat.shape, F32),
            pltpu.VMEM(lat.shape, BF16),
            pltpu.SemaphoreType.DMA,
            pltpu.SemaphoreType.DMA((4,)),
        ],
        flops=1 << 31,
        moved=8 << 20,
        far=True,
        direct=[lat],
        mib=50,
    )


def per_device(kernel, lon_halo, lat_reach, polar_rows, polar_shift, blend):
    shells, row_count, col_count = kernel.shape
    sectors = lax.axis_size("sector")
    zones = lax.axis_size("zone")
    zone_id = lax.axis_index("zone").astype(jnp.int32)
    sector_id = lax.axis_index("sector").astype(jnp.int32)
    place = jnp.stack([zone_id, sector_id])
    last = zones - 1
    packed, kept, near, far = pack(place, polar_rows, kernel, sectors)
    given = lax.ppermute(packed, "zone", [(0, 1), (last, last - 1)])
    far = lax.ppermute(far, "sector", [(i, (i + 1 if i % 2 else i - 1) % sectors) for i in range(sectors)])
    near = lax.ppermute(near, "sector", [(i, i ^ 1) for i in range(sectors)])
    inner = (zone_id == 1) | (zone_id == last - 1)
    parts, near, far = lax.optimization_barrier((jnp.where(inner, given, kept), near, far))
    circles = lax.all_to_all(parts, "sector", 0, 0, tiled=True)
    lon_smooth, near_rows, far_rows, lat_weight, mix = smooth_lon(
        place, lon_halo, kernel, near, far, lat_reach[:, None], blend
    )
    far_rows = lax.ppermute(
        far_rows, "zone", [(i, i + 1 if i % 2 else i - 1) for i in range(1, zones - 1)]
    )
    near_rows = lax.ppermute(near_rows, "zone", [(i, i ^ 1) for i in range(zones)])
    turned = hold(place, polar_rows, polar_shift, lon_halo, circles, lat_weight)
    turned, near_rows, far_rows = lax.optimization_barrier((turned, near_rows, far_rows))
    mine = lax.all_to_all(turned, "sector", 0, 0, tiled=True)
    lat, polar_weight = smooth_lat(place, polar_rows, near_rows, lon_smooth, far_rows, lat_weight)
    mine, lat = lax.optimization_barrier((mine, lat))
    other = lax.ppermute(mine, "zone", [(0, 1), (1, 0), (last, last - 1), (last - 1, last)])
    return finish(place, lat, mine, other, polar_weight, mix)


def solution(mesh):
    in_specs = (P(None, "zone", "sector"), P(), P("zone"), P(), P(), P())
    out_specs = P(None, "zone", "sector")
    return jax.shard_map(
        per_device, mesh=mesh, in_specs=in_specs, out_specs=out_specs, check_vma=False
    )
```

```python
import jax
import jax.numpy as jnp
from jax import lax
from jax.experimental import pallas as pl
from jax.experimental.pallas import tpu as pltpu
from jax.sharding import PartitionSpec as P

HMAX = 48
LMAX = 32
LANES = 128
PART = 16
UNROLL = 8
F32 = jnp.float32
BF16 = jnp.bfloat16


def lanes_of(rows):
    return lax.broadcasted_iota(jnp.int32, (rows, LANES), 1)


def edge_kernel(place_ref, x_ref, near_ref, far_ref, tile_ref, sems):
    shells, row_count, col_count = x_ref.shape
    half = shells // 2
    size = half * row_count
    lane = lanes_of(size)
    first = (0, col_count - LANES)
    copies = [
        pltpu.make_async_copy(x_ref.at[:, :, pl.ds(first[e], LANES)], tile_ref.at[e], sems.at[e]) for e in range(2)
    ]
    for copy in copies:
        copy.start()

    def part(e, shell):
        return tile_ref[e, shell : shell + half].reshape(size, LANES).astype(F32)

    even = lax.rem(place_ref[1], 2) == 0
    copies[0].wait()
    low = jnp.where(lane < HMAX, part(0, 0), pltpu.roll(part(0, half), HMAX, 1))
    copies[1].wait()
    high = jnp.where(lane < HMAX, pltpu.roll(part(1, 0), HMAX, 1), pltpu.roll(part(1, half), 2 * HMAX, 1))
    near_ref[...] = jnp.where(even, high, low).astype(BF16)
    far_ref[...] = jnp.where(even, low, high).astype(BF16)


def write_polar(half, place_ref, rows_ref, x_ref, send_ref, wide_ref):
    _, row_count, col_count = x_ref.shape
    tiles = col_count // LANES
    zone = place_ref[0]
    for t in range(tiles):
        wide_ref[t] = (
            x_ref[half * PART : (half + 1) * PART, :, t * LANES : (t + 1) * LANES]
            .reshape(PART * row_count, LANES)
            .astype(F32)
        )
    holders, held = send_ref.shape[0], send_ref.shape[1]
    cap = jnp.where(zone < 8, 0, holders * held)
    for k in range(holders):
        for r in range(held):
            row = jnp.clip(rows_ref[cap + k * held + r] - zone * row_count, 0, row_count - 1)
            for t in range(tiles):
                values = wide_ref[t, pl.ds(row, PART, stride=row_count), :]
                send_ref[k, r, t * PART : (t + 1) * PART, :] = values.astype(BF16)


def first_kernel(place_ref, rows_ref, x_ref, far_ref, send_ref, wide_ref):
    write_polar(1, place_ref, rows_ref, x_ref, send_ref, wide_ref)


def second_kernel(place_ref, rows_ref, x_ref, given_ref, send_ref, wide_ref):
    write_polar(0, place_ref, rows_ref, x_ref, send_ref, wide_ref)


def band_terms(half_f):
    rate = 4.5 / (half_f * half_f)
    tap = (lanes_of(half_f.shape[0]) - HMAX).astype(F32)
    terms = jnp.where(jnp.abs(tap) <= half_f, jnp.exp(-rate * (tap * tap)), 0.0)
    return rate, jnp.broadcast_to(1.0 / jnp.sum(terms, axis=1, keepdims=True), half_f.shape)


def lon_kernel(place_ref, halo_ref, x_ref, near_ref, far_ref, reach_ref, blend_ref,
               out_ref, near_rows_ref, far_rows_ref, weight_ref, mix_ref, wide_ref, done_ref, half_ref, rate_ref, scale_ref):
    shells, row_count, col_count = x_ref.shape
    total = shells * row_count
    size = total // 2
    tiles = col_count // LANES
    zone = place_ref[0]
    for i in range(row_count):
        half_ref[i : i + 1, :] = jnp.full((1, LANES), halo_ref[zone * row_count + i], jnp.int32).astype(F32)
    rate_ref[...], scale_ref[...] = band_terms(half_ref[...])
    lane = lanes_of(size)
    even = lax.rem(place_ref[1], 2) == 0
    near = near_ref[...].astype(F32)
    far = far_ref[...].astype(F32)
    before = jnp.where(even, far, near)
    after = jnp.where(even, near, far)
    for part in range(2):
        rows = pl.ds(part * size, size)
        shell = slice(part * (shells // 2), (part + 1) * (shells // 2))
        previous = before if part == 0 else pltpu.roll(before, LANES - HMAX, 1)
        for t in range(tiles):
            turned = pltpu.roll(
                x_ref[shell, :, t * LANES : (t + 1) * LANES].reshape(size, LANES).astype(F32), HMAX, 1
            )
            wide_ref[t, rows, :] = jnp.where(lane < HMAX, previous, turned)
            previous = turned
        edge = pltpu.roll(after, HMAX, 1) if part == 0 else after
        wide_ref[tiles, rows, :] = jnp.where(lane < HMAX, previous, jnp.where(lane < 2 * HMAX, edge, 0.0))
    depth = 2 * LANES
    offset = (lanes_of(depth) - lax.broadcasted_iota(jnp.int32, (depth, LANES), 0) + HMAX).astype(F32)
    square = offset * offset
    distance = jnp.abs(offset)

    def some_rows(block, carry):
        for u in range(UNROLL):
            i = block * UNROLL + u
            line = pl.ds(i, 1)
            band = jnp.where(distance <= half_ref[line, :], jnp.exp(-rate_ref[line, :] * square), 0.0)
            band = (band * scale_ref[line, :]).astype(BF16)
            values = [wide_ref[t, pl.ds(i, shells, stride=row_count), :].astype(BF16) for t in range(tiles + 1)]
            stacked = jnp.concatenate(
                [jnp.concatenate(values[:tiles], axis=0), jnp.concatenate(values[1:], axis=0)], axis=1
            )
            result = jnp.dot(stacked, band, preferred_element_type=F32)
            for t in range(tiles):
                done_ref[t, pl.ds(i, shells, stride=row_count), :] = result[t * shells : (t + 1) * shells]
        return carry

    lax.fori_loop(0, row_count // UNROLL, some_rows, 0)
    for t in range(tiles):
        out_ref[:, :, t * LANES : (t + 1) * LANES] = done_ref[t].astype(BF16).reshape(shells, row_count, LANES)
    odd = lax.rem(zone, 2)
    last = row_count - LMAX
    near_rows_ref[...] = out_ref[:, pl.ds(pl.multiple_of((1 - odd) * last, LMAX), LMAX), :]
    far_rows_ref[...] = out_ref[:, pl.ds(pl.multiple_of(odd * last, LMAX), LMAX), :]
    frame_rows = weight_ref.shape[1]
    reach = reach_ref[...]
    column = lax.broadcasted_iota(jnp.int32, (row_count, frame_rows), 1)
    away = column - LMAX - lax.broadcasted_iota(jnp.int32, (row_count, frame_rows), 0)
    source = zone * row_count - LMAX + column
    valid = (jnp.abs(away) <= reach) & (source >= 0) & (source < halo_ref.shape[0])
    reach_f = reach.astype(F32)
    away_f = away.astype(F32)
    weights = jnp.where(valid, jnp.exp(-(4.5 / (reach_f * reach_f)) * (away_f * away_f)), 0.0)
    weight_ref[...] = (weights / jnp.sum(weights, axis=1, keepdims=True)).astype(BF16)
    length = mix_ref.shape[0]
    group = length // shells
    spread = (
        lax.broadcasted_iota(jnp.int32, (length, shells), 0) // group
        == lax.broadcasted_iota(jnp.int32, (length, shells), 1)
    ).astype(F32).astype(BF16)
    tall = jnp.dot(spread, blend_ref[...], preferred_element_type=F32).astype(BF16)
    full = lax.dot_general(tall, spread, (((1,), (1,)), ((), ())), preferred_element_type=F32)
    same = (
        lax.broadcasted_iota(jnp.int32, (length, length), 0) % group
        == lax.broadcasted_iota(jnp.int32, (length, length), 1) % group
    )
    mix_ref[...] = jnp.where(same, full, 0.0).astype(BF16)


def hold_kernel(place_ref, rows_ref, shift_ref, halo_ref, x_ref, after_ref, out_ref, circle_ref):
    sectors, held, block, _ = x_ref.shape
    zone, sector = place_ref[0], place_ref[1]
    cap = jnp.where(zone < 8, 0, sectors * held)
    length = sectors * block
    full_lon = length // PART * LANES
    depth = 3 * LANES
    for r in range(held):
        for copy in range(2):
            circle_ref[r, copy * length : (copy + 1) * length, :] = x_ref[:, r].reshape(length, LANES)
        circle_ref[r, 2 * length : 2 * length + 2 * PART, :] = circle_ref[r, 0 : 2 * PART, :]
    for r in range(held):
        entry = cap + sector * held + r
        half_f = jnp.full((1, LANES), halo_ref[rows_ref[entry]], jnp.int32).astype(F32)
        rate, scale = band_terms(half_f)
        start = lax.rem(2 * full_lon - shift_ref[entry] - HMAX, full_lon)
        first = start // LANES
        rest = start - first * LANES
        offset = (
            lanes_of(depth) - lax.broadcasted_iota(jnp.int32, (depth, LANES), 0) + (rest + HMAX)
        ).astype(F32)
        band = jnp.where(jnp.abs(offset) <= half_f, jnp.exp(-rate * (offset * offset)), 0.0) * scale
        values = jnp.concatenate(
            [circle_ref[r, pl.ds(pl.multiple_of((first + u) * PART, PART), length), :] for u in range(3)], axis=1
        )
        result = jnp.dot(values, band.astype(BF16), preferred_element_type=F32)
        out_ref[:, r] = result.astype(BF16).reshape(sectors, block, LANES)


def lat_kernel(place_ref, rows_ref, near_ref, own_ref, far_ref, weight_ref,
               out_ref, polar_weight_ref, pick_ref):
    shells, row_count, col_count = own_ref.shape
    frame_rows = weight_ref.shape[1]
    polar = pick_ref.shape[0]
    zone = place_ref[0]
    cap = jnp.where(zone < 8, 0, polar)
    lane = lanes_of(1)
    for p in range(polar):
        pick_ref[p : p + 1, :] = (lane == rows_ref[cap + p] - zone * row_count + LMAX).astype(F32)
    pick = pick_ref[...]
    weight = weight_ref[...]
    polar_weight_ref[...] = lax.dot_general(
        weight, pick.astype(BF16), (((1,), (1,)), ((), ())), preferred_element_type=F32
    ).astype(BF16)
    rest = weight.astype(F32) * (1.0 - jnp.sum(pick, axis=0, keepdims=True))
    wide = lanes_of(row_count)
    turned = jnp.where(
        wide < LMAX,
        pltpu.roll(rest, LMAX, 1),
        jnp.where(wide < frame_rows - LMAX, rest, pltpu.roll(rest, frame_rows - LMAX, 1)),
    )
    rest = jnp.where(lax.rem(zone, 2) == 0, turned, rest).astype(BF16)

    def some_shells(block, carry):
        for u in range(4):
            s = block * 4 + u
            values = jnp.concatenate([near_ref[s], own_ref[s], far_ref[s]], axis=0)
            out_ref[s] = jnp.dot(rest, values, preferred_element_type=F32)
        return carry

    lax.fori_loop(0, shells // 4, some_shells, 0)


def final_kernel(place_ref, mine_ref, other_ref, polar_weight_ref, mix_ref, lat_ref,
                 out_ref, polar_ref, sum_ref, stage_ref, sem, sems):
    shells, row_count, col_count = lat_ref.shape
    holders, held = mine_ref.shape[:2]
    tiles = col_count // LANES
    polar = holders * held
    fetch = pltpu.make_async_copy(lat_ref, sum_ref, sem)
    fetch.start()
    zone = place_ref[0]
    outer = (zone == 0) | (zone == 15)
    mine_first = jnp.where(outer, 0, PART * polar)
    for ref, first in ((mine_ref, mine_first), (other_ref, PART * polar - mine_first)):
        for k in range(holders):
            for r in range(held):
                for t in range(tiles):
                    polar_ref[t, pl.ds(first + k * held + r, PART, stride=polar), :] = ref[
                        k, r, t * PART : (t + 1) * PART, :
                    ].astype(F32)
    weight = polar_weight_ref[...]
    fetch.wait()

    def some_shells(index, carry):
        for u in range(4):
            s = index * 4 + u
            base = pl.multiple_of(s * polar, PART)
            values = jnp.concatenate(
                [polar_ref[t, pl.ds(base, polar), :].astype(BF16) for t in range(tiles)], axis=1
            )
            sum_ref[s] += jnp.dot(weight, values, preferred_element_type=F32)
        return carry

    lax.fori_loop(0, shells // 4, some_shells, 0)
    group = mix_ref.shape[0] // shells
    mix = mix_ref[...]
    stores = []
    for g in range(row_count // (2 * group)):
        mixed = []
        for e in range(2):
            first = (2 * g + e) * group
            values = sum_ref[:, first : first + group, :].reshape(shells * group, col_count).astype(BF16)
            mixed.append(jnp.dot(mix, values, preferred_element_type=F32).reshape(shells, group, col_count))
        rows = pl.ds(2 * g * group, 2 * group)
        stage_ref[:, rows, :] = jnp.concatenate(mixed, axis=1).astype(BF16)
        stores.append(pltpu.make_async_copy(stage_ref.at[:, rows], out_ref.at[:, rows], sems.at[g]))
        stores[-1].start()
    for store in stores:
        store.wait()


def call(kernel, name, out_shape, scalars, arrays, scratch, flops=0, moved=0, direct=(), far=False, mib=16):
    smem = pl.BlockSpec(memory_space=pltpu.SMEM)
    vmem = pl.BlockSpec(memory_space=pltpu.VMEM)
    anywhere = pl.BlockSpec(memory_space=pl.ANY)
    many = isinstance(out_shape, tuple)
    return pl.pallas_call(
        kernel,
        out_shape=out_shape,
        in_specs=[smem] * len(scalars) + [vmem] * len(arrays) + [anywhere] * len(direct),
        out_specs=(vmem,) * len(out_shape) if many else anywhere if far else vmem,
        scratch_shapes=scratch,
        compiler_params=pltpu.CompilerParams(vmem_limit_bytes=mib << 20),
        cost_estimate=pl.CostEstimate(flops=flops, bytes_accessed=moved, transcendentals=0),
        name=name,
    )(*scalars, *arrays, *direct)


struct = jax.ShapeDtypeStruct


def pack(place, polar_rows, kernel, sectors):
    shells, row_count, col_count = kernel.shape
    tiles = col_count // LANES
    held = polar_rows.shape[0] // 2 // sectors
    send = struct((sectors, held, tiles * PART, LANES), BF16)
    edge = struct((shells * row_count // 2, LANES), BF16)
    wide = pltpu.VMEM((tiles, PART * row_count, LANES), F32)
    tile = pltpu.VMEM((2, shells, row_count, LANES), BF16)
    near, far = call(
        edge_kernel, "cut_edges", (edge, edge), [place], [], [tile, pltpu.SemaphoreType.DMA((2,))],
        moved=4 << 20, direct=[kernel],
    )
    given = call(
        first_kernel, "pack_half_of_shells", send, [place, polar_rows], [kernel], [wide],
        moved=4 << 20, direct=[far],
    )
    kept = call(
        second_kernel, "pack_other_half_of_shells", send, [place, polar_rows], [kernel], [wide],
        moved=4 << 20, direct=[given],
    )
    return given, kept, near, far


def smooth_lon(place, lon_halo, kernel, near, far, reach, blend):
    shells, row_count, col_count = kernel.shape
    tiles = col_count // LANES
    rows = pltpu.VMEM((row_count, LANES), F32)
    return call(
        lon_kernel,
        "smooth_along_longitude",
        (
            struct((shells, row_count, col_count), BF16),
            struct((shells, LMAX, col_count), BF16),
            struct((shells, LMAX, col_count), BF16),
            struct((row_count, row_count + 2 * LMAX), BF16),
            struct((shells * 8, shells * 8), BF16),
        ),
        [place, lon_halo],
        [kernel, near, far, reach, blend],
        [
            pltpu.VMEM((tiles + 1, shells * row_count, LANES), F32),
            pltpu.VMEM((tiles, shells * row_count, LANES), F32),
            rows,
            rows,
            rows,
        ],
        flops=1 << 36,
        moved=16 << 20,
        mib=20,
    )


def hold(place, polar_rows, polar_shift, lon_halo, circles, after):
    sectors, held, block, _ = circles.shape
    return call(
        hold_kernel,
        "smooth_and_turn_polar_circles",
        struct(circles.shape, BF16),
        [place, polar_rows, polar_shift, lon_halo],
        [circles],
        [pltpu.VMEM((held, 2 * sectors * block + 2 * PART, LANES), BF16)],
        flops=1 << 30,
        moved=4 << 20,
        direct=[after],
    )


def smooth_lat(place, polar_rows, near, own, far, weight):
    row_count, frame_rows = weight.shape
    polar = polar_rows.shape[0] // 2
    return call(
        lat_kernel,
        "smooth_along_latitude",
        (struct(own.shape, F32), struct((row_count, polar), BF16)),
        [place, polar_rows],
        [near, own, far, weight],
        [pltpu.VMEM((polar, frame_rows), F32)],
        flops=1 << 36,
        moved=8 << 20,
    )


def finish(place, lat, mine, other, polar_weight, mix):
    shells, _, col_count = lat.shape
    polar = polar_weight.shape[1]
    return call(
        final_kernel,
        "add_polar_rows_and_blend",
        struct(lat.shape, BF16),
        [place],
        [mine, other, polar_weight, mix],
        [
            pltpu.VMEM((col_count // LANES, shells * polar, LANES), F32),
            pltpu.VMEM(lat.shape, F32),
            pltpu.VMEM(lat.shape, BF16),
            pltpu.SemaphoreType.DMA,
            pltpu.SemaphoreType.DMA((4,)),
        ],
        flops=1 << 31,
        moved=8 << 20,
        far=True,
        direct=[lat],
        mib=50,
    )


def per_device(kernel, lon_halo, lat_reach, polar_rows, polar_shift, blend):
    shells, row_count, col_count = kernel.shape
    sectors = lax.axis_size("sector")
    zones = lax.axis_size("zone")
    zone_id = lax.axis_index("zone").astype(jnp.int32)
    sector_id = lax.axis_index("sector").astype(jnp.int32)
    place = jnp.stack([zone_id, sector_id])
    last = zones - 1
    packed, kept, near, far = pack(place, polar_rows, kernel, sectors)
    given = lax.ppermute(packed, "zone", [(0, 1), (last, last - 1)])
    far = lax.ppermute(far, "sector", [(i, (i + 1 if i % 2 else i - 1) % sectors) for i in range(sectors)])
    near = lax.ppermute(near, "sector", [(i, i ^ 1) for i in range(sectors)])
    inner = (zone_id == 1) | (zone_id == last - 1)
    parts = jnp.where(inner, given, kept)
    circles = lax.all_to_all(parts, "sector", 0, 0, tiled=True)
    lon_smooth, near_rows, far_rows, lat_weight, mix = smooth_lon(
        place, lon_halo, kernel, near, far, lat_reach[:, None], blend
    )
    far_rows = lax.ppermute(
        far_rows, "zone", [(i, i + 1 if i % 2 else i - 1) for i in range(1, zones - 1)]
    )
    near_rows = lax.ppermute(near_rows, "zone", [(i, i ^ 1) for i in range(zones)])
    turned = hold(place, polar_rows, polar_shift, lon_halo, circles, lat_weight)
    mine = lax.all_to_all(turned, "sector", 0, 0, tiled=True)
    lat, polar_weight = smooth_lat(place, polar_rows, near_rows, lon_smooth, far_rows, lat_weight)
    mine, lat = lax.optimization_barrier((mine, lat))
    other = lax.ppermute(mine, "zone", [(0, 1), (1, 0), (last, last - 1), (last - 1, last)])
    return finish(place, lat, mine, other, polar_weight, mix)


def solution(mesh):
    in_specs = (P(None, "zone", "sector"), P(), P("zone"), P(), P(), P())
    out_specs = P(None, "zone", "sector")
    return jax.shard_map(
        per_device, mesh=mesh, in_specs=in_specs, out_specs=out_specs, check_vma=False
    )
```

```python
import jax
import jax.numpy as jnp
from jax import lax
from jax.experimental import pallas as pl
from jax.experimental.pallas import tpu as pltpu
from jax.sharding import PartitionSpec as P

HMAX = 48
LMAX = 32
LANES = 128
PART = 16
UNROLL = 8
F32 = jnp.float32
BF16 = jnp.bfloat16


def lanes_of(rows):
    return lax.broadcasted_iota(jnp.int32, (rows, LANES), 1)


def edge_kernel(x_ref, near_ref, far_ref, tile_ref, sems):
    shells, row_count, col_count = x_ref.shape
    half = shells // 2
    size = half * row_count
    lane = lanes_of(size)
    first = (0, col_count - LANES)
    copies = [
        pltpu.make_async_copy(x_ref.at[:, :, pl.ds(first[e], LANES)], tile_ref.at[e], sems.at[e]) for e in range(2)
    ]
    for copy in copies:
        copy.start()

    def part(e, shell):
        return tile_ref[e, shell : shell + half].reshape(size, LANES).astype(F32)

    even = lax.rem(lax.axis_index("sector"), 2) == 0
    copies[0].wait()
    low = jnp.where(lane < HMAX, part(0, 0), pltpu.roll(part(0, half), HMAX, 1))
    copies[1].wait()
    high = jnp.where(lane < HMAX, pltpu.roll(part(1, 0), HMAX, 1), pltpu.roll(part(1, half), 2 * HMAX, 1))
    near_ref[...] = jnp.where(even, high, low).astype(BF16)
    far_ref[...] = jnp.where(even, low, high).astype(BF16)


def write_polar(half, rows_ref, x_ref, send_ref, wide_ref):
    _, row_count, col_count = x_ref.shape
    tiles = col_count // LANES
    zone = lax.axis_index("zone")
    for t in range(tiles):
        wide_ref[t] = (
            x_ref[half * PART : (half + 1) * PART, :, t * LANES : (t + 1) * LANES]
            .reshape(PART * row_count, LANES)
            .astype(F32)
        )
    holders, held = send_ref.shape[0], send_ref.shape[1]
    cap = jnp.where(zone < 8, 0, holders * held)
    for k in range(holders):
        for r in range(held):
            row = jnp.clip(rows_ref[cap + k * held + r] - zone * row_count, 0, row_count - 1)
            for t in range(tiles):
                values = wide_ref[t, pl.ds(row, PART, stride=row_count), :]
                send_ref[k, r, t * PART : (t + 1) * PART, :] = values.astype(BF16)


def first_kernel(rows_ref, x_ref, far_ref, send_ref, wide_ref):
    write_polar(1, rows_ref, x_ref, send_ref, wide_ref)


def second_kernel(rows_ref, x_ref, given_ref, send_ref, wide_ref):
    write_polar(0, rows_ref, x_ref, send_ref, wide_ref)


def band_terms(half_f):
    rate = 4.5 / (half_f * half_f)
    tap = (lanes_of(half_f.shape[0]) - HMAX).astype(F32)
    terms = jnp.where(jnp.abs(tap) <= half_f, jnp.exp(-rate * (tap * tap)), 0.0)
    return rate, jnp.broadcast_to(1.0 / jnp.sum(terms, axis=1, keepdims=True), half_f.shape)


def lon_kernel(halo_ref, x_ref, near_ref, far_ref,
               out_ref, near_rows_ref, far_rows_ref, wide_ref, done_ref, half_ref, rate_ref, scale_ref):
    shells, row_count, col_count = x_ref.shape
    total = shells * row_count
    size = total // 2
    tiles = col_count // LANES
    zone = lax.axis_index("zone")
    for i in range(row_count):
        half_ref[i : i + 1, :] = jnp.full((1, LANES), halo_ref[zone * row_count + i], jnp.int32).astype(F32)
    rate_ref[...], scale_ref[...] = band_terms(half_ref[...])
    lane = lanes_of(size)
    even = lax.rem(lax.axis_index("sector"), 2) == 0
    near = near_ref[...].astype(F32)
    far = far_ref[...].astype(F32)
    before = jnp.where(even, far, near)
    after = jnp.where(even, near, far)
    for part in range(2):
        rows = pl.ds(part * size, size)
        shell = slice(part * (shells // 2), (part + 1) * (shells // 2))
        previous = before if part == 0 else pltpu.roll(before, LANES - HMAX, 1)
        for t in range(tiles):
            turned = pltpu.roll(
                x_ref[shell, :, t * LANES : (t + 1) * LANES].reshape(size, LANES).astype(F32), HMAX, 1
            )
            wide_ref[t, rows, :] = jnp.where(lane < HMAX, previous, turned)
            previous = turned
        edge = pltpu.roll(after, HMAX, 1) if part == 0 else after
        wide_ref[tiles, rows, :] = jnp.where(lane < HMAX, previous, jnp.where(lane < 2 * HMAX, edge, 0.0))
    depth = 2 * LANES
    offset = (lanes_of(depth) - lax.broadcasted_iota(jnp.int32, (depth, LANES), 0) + HMAX).astype(F32)
    square = offset * offset
    distance = jnp.abs(offset)

    def some_rows(block, carry):
        for u in range(UNROLL):
            i = block * UNROLL + u
            line = pl.ds(i, 1)
            band = jnp.where(distance <= half_ref[line, :], jnp.exp(-rate_ref[line, :] * square), 0.0)
            band = (band * scale_ref[line, :]).astype(BF16)
            values = [wide_ref[t, pl.ds(i, shells, stride=row_count), :].astype(BF16) for t in range(tiles + 1)]
            stacked = jnp.concatenate(
                [jnp.concatenate(values[:tiles], axis=0), jnp.concatenate(values[1:], axis=0)], axis=1
            )
            result = jnp.dot(stacked, band, preferred_element_type=F32)
            for t in range(tiles):
                done_ref[t, pl.ds(i, shells, stride=row_count), :] = result[t * shells : (t + 1) * shells]
        return carry

    lax.fori_loop(0, row_count // UNROLL, some_rows, 0)
    for t in range(tiles):
        out_ref[:, :, t * LANES : (t + 1) * LANES] = done_ref[t].astype(BF16).reshape(shells, row_count, LANES)
    odd = lax.rem(zone, 2)
    last = row_count - LMAX
    near_rows_ref[...] = out_ref[:, pl.ds(pl.multiple_of((1 - odd) * last, LMAX), LMAX), :]
    far_rows_ref[...] = out_ref[:, pl.ds(pl.multiple_of(odd * last, LMAX), LMAX), :]


def hold_kernel(table_ref, x_ref, after_ref, out_ref, circle_ref):
    sectors, held, block, _ = x_ref.shape
    zone, sector = lax.axis_index("zone"), lax.axis_index("sector")
    polar = 2 * sectors * held
    cap = jnp.where(zone < 8, 0, sectors * held)
    length = sectors * block
    full_lon = length // PART * LANES
    depth = 3 * LANES
    for r in range(held):
        for copy in range(2):
            circle_ref[r, copy * length : (copy + 1) * length, :] = x_ref[:, r].reshape(length, LANES)
        circle_ref[r, 2 * length : 2 * length + 2 * PART, :] = circle_ref[r, 0 : 2 * PART, :]
    for r in range(held):
        entry = cap + sector * held + r
        half_f = jnp.full((1, LANES), table_ref[2 * polar + table_ref[entry]], jnp.int32).astype(F32)
        rate, scale = band_terms(half_f)
        start = lax.rem(2 * full_lon - table_ref[polar + entry] - HMAX, full_lon)
        first = start // LANES
        rest = start - first * LANES
        offset = (
            lanes_of(depth) - lax.broadcasted_iota(jnp.int32, (depth, LANES), 0) + (rest + HMAX)
        ).astype(F32)
        band = jnp.where(jnp.abs(offset) <= half_f, jnp.exp(-rate * (offset * offset)), 0.0) * scale
        values = jnp.concatenate(
            [circle_ref[r, pl.ds(pl.multiple_of((first + u) * PART, PART), length), :] for u in range(3)], axis=1
        )
        result = jnp.dot(values, band.astype(BF16), preferred_element_type=F32)
        out_ref[:, r] = result.astype(BF16).reshape(sectors, block, LANES)


def lat_kernel(rows_ref, near_ref, own_ref, far_ref, reach_ref, blend_ref,
               out_ref, polar_weight_ref, mix_ref, pick_ref):
    shells, row_count, col_count = own_ref.shape
    frame_rows = row_count + 2 * LMAX
    polar = pick_ref.shape[0]
    zone = lax.axis_index("zone")
    cap = jnp.where(zone < 8, 0, polar)
    lane = lanes_of(1)
    for p in range(polar):
        pick_ref[p : p + 1, :] = (lane == rows_ref[cap + p] - zone * row_count + LMAX).astype(F32)
    pick = pick_ref[...]
    zones = lax.axis_size("zone")
    reach = reach_ref[...]
    column = lax.broadcasted_iota(jnp.int32, (row_count, frame_rows), 1)
    away = column - LMAX - lax.broadcasted_iota(jnp.int32, (row_count, frame_rows), 0)
    source = zone * row_count - LMAX + column
    valid = (jnp.abs(away) <= reach) & (source >= 0) & (source < zones * row_count)
    reach_f = reach.astype(F32)
    away_f = away.astype(F32)
    weights = jnp.where(valid, jnp.exp(-(4.5 / (reach_f * reach_f)) * (away_f * away_f)), 0.0)
    weight = (weights / jnp.sum(weights, axis=1, keepdims=True)).astype(BF16)
    length = mix_ref.shape[0]
    group = length // shells
    spread = (
        lax.broadcasted_iota(jnp.int32, (length, shells), 0) // group
        == lax.broadcasted_iota(jnp.int32, (length, shells), 1)
    ).astype(F32).astype(BF16)
    tall = jnp.dot(spread, blend_ref[...], preferred_element_type=F32).astype(BF16)
    full = lax.dot_general(tall, spread, (((1,), (1,)), ((), ())), preferred_element_type=F32)
    same = (
        lax.broadcasted_iota(jnp.int32, (length, length), 0) % group
        == lax.broadcasted_iota(jnp.int32, (length, length), 1) % group
    )
    mix_ref[...] = jnp.where(same, full, 0.0).astype(BF16)
    polar_weight_ref[...] = lax.dot_general(
        weight, pick.astype(BF16), (((1,), (1,)), ((), ())), preferred_element_type=F32
    ).astype(BF16)
    rest = weight.astype(F32) * (1.0 - jnp.sum(pick, axis=0, keepdims=True))
    wide = lanes_of(row_count)
    turned = jnp.where(
        wide < LMAX,
        pltpu.roll(rest, LMAX, 1),
        jnp.where(wide < frame_rows - LMAX, rest, pltpu.roll(rest, frame_rows - LMAX, 1)),
    )
    rest = jnp.where(lax.rem(zone, 2) == 0, turned, rest).astype(BF16)

    def some_shells(block, carry):
        for u in range(4):
            s = block * 4 + u
            values = jnp.concatenate([near_ref[s], own_ref[s], far_ref[s]], axis=0)
            out_ref[s] = jnp.dot(rest, values, preferred_element_type=F32)
        return carry

    lax.fori_loop(0, shells // 4, some_shells, 0)


def final_kernel(mine_ref, other_ref, polar_weight_ref, mix_ref, lat_ref,
                 out_ref, polar_ref, sum_ref, stage_ref, sem, sems):
    shells, row_count, col_count = lat_ref.shape
    holders, held = mine_ref.shape[:2]
    tiles = col_count // LANES
    polar = holders * held
    fetch = pltpu.make_async_copy(lat_ref, sum_ref, sem)
    fetch.start()
    zone = lax.axis_index("zone")
    outer = (zone == 0) | (zone == 15)
    mine_first = jnp.where(outer, 0, PART * polar)
    for ref, first in ((mine_ref, mine_first), (other_ref, PART * polar - mine_first)):
        for k in range(holders):
            for r in range(held):
                for t in range(tiles):
                    polar_ref[t, pl.ds(first + k * held + r, PART, stride=polar), :] = ref[
                        k, r, t * PART : (t + 1) * PART, :
                    ].astype(F32)
    weight = polar_weight_ref[...]
    fetch.wait()

    def some_shells(index, carry):
        for u in range(4):
            s = index * 4 + u
            base = pl.multiple_of(s * polar, PART)
            values = jnp.concatenate(
                [polar_ref[t, pl.ds(base, polar), :].astype(BF16) for t in range(tiles)], axis=1
            )
            sum_ref[s] += jnp.dot(weight, values, preferred_element_type=F32)
        return carry

    lax.fori_loop(0, shells // 4, some_shells, 0)
    group = mix_ref.shape[0] // shells
    mix = mix_ref[...]
    stores = []
    for g in range(row_count // (2 * group)):
        mixed = []
        for e in range(2):
            first = (2 * g + e) * group
            values = sum_ref[:, first : first + group, :].reshape(shells * group, col_count).astype(BF16)
            mixed.append(jnp.dot(mix, values, preferred_element_type=F32).reshape(shells, group, col_count))
        rows = pl.ds(2 * g * group, 2 * group)
        stage_ref[:, rows, :] = jnp.concatenate(mixed, axis=1).astype(BF16)
        stores.append(pltpu.make_async_copy(stage_ref.at[:, rows], out_ref.at[:, rows], sems.at[g]))
        stores[-1].start()
    for store in stores:
        store.wait()


def call(kernel, name, out_shape, scalars, arrays, scratch, flops=0, moved=0, direct=(), far=False, mib=16):
    smem = pl.BlockSpec(memory_space=pltpu.SMEM)
    vmem = pl.BlockSpec(memory_space=pltpu.VMEM)
    anywhere = pl.BlockSpec(memory_space=pl.ANY)
    many = isinstance(out_shape, tuple)
    return pl.pallas_call(
        kernel,
        out_shape=out_shape,
        in_specs=[smem] * len(scalars) + [vmem] * len(arrays) + [anywhere] * len(direct),
        out_specs=(vmem,) * len(out_shape) if many else anywhere if far else vmem,
        scratch_shapes=scratch,
        compiler_params=pltpu.CompilerParams(vmem_limit_bytes=mib << 20),
        cost_estimate=pl.CostEstimate(flops=flops, bytes_accessed=moved, transcendentals=0),
        name=name,
    )(*scalars, *arrays, *direct)


struct = jax.ShapeDtypeStruct


def pack(polar_rows, kernel, sectors):
    shells, row_count, col_count = kernel.shape
    tiles = col_count // LANES
    held = polar_rows.shape[0] // 2 // sectors
    send = struct((sectors, held, tiles * PART, LANES), BF16)
    edge = struct((shells * row_count // 2, LANES), BF16)
    wide = pltpu.VMEM((tiles, PART * row_count, LANES), F32)
    tile = pltpu.VMEM((2, shells, row_count, LANES), BF16)
    near, far = call(
        edge_kernel, "cut_edges", (edge, edge), [], [], [tile, pltpu.SemaphoreType.DMA((2,))],
        moved=4 << 20, direct=[kernel],
    )
    given = call(
        first_kernel, "pack_half_of_shells", send, [polar_rows], [kernel], [wide],
        moved=4 << 20, direct=[far],
    )
    kept = call(
        second_kernel, "pack_other_half_of_shells", send, [polar_rows], [kernel], [wide],
        moved=4 << 20, direct=[given],
    )
    return given, kept, near, far


def smooth_lon(lon_halo, kernel, near, far):
    shells, row_count, col_count = kernel.shape
    tiles = col_count // LANES
    rows = pltpu.VMEM((row_count, LANES), F32)
    return call(
        lon_kernel,
        "smooth_along_longitude",
        (
            struct((shells, row_count, col_count), BF16),
            struct((shells, LMAX, col_count), BF16),
            struct((shells, LMAX, col_count), BF16),
        ),
        [lon_halo],
        [kernel, near, far],
        [
            pltpu.VMEM((tiles + 1, shells * row_count, LANES), F32),
            pltpu.VMEM((tiles, shells * row_count, LANES), F32),
            rows,
            rows,
            rows,
        ],
        flops=1 << 36,
        moved=16 << 20,
        mib=20,
    )


def hold(table, circles, after):
    sectors, held, block, _ = circles.shape
    return call(
        hold_kernel,
        "smooth_and_turn_polar_circles",
        struct(circles.shape, BF16),
        [table],
        [circles],
        [pltpu.VMEM((held, 2 * sectors * block + 2 * PART, LANES), BF16)],
        flops=1 << 30,
        moved=4 << 20,
        direct=[after],
    )


def smooth_lat(polar_rows, near, own, far, reach, blend):
    shells, row_count, _ = own.shape
    frame_rows = row_count + 2 * LMAX
    polar = polar_rows.shape[0] // 2
    return call(
        lat_kernel,
        "smooth_along_latitude",
        (
            struct(own.shape, F32),
            struct((row_count, polar), BF16),
            struct((shells * 8, shells * 8), BF16),
        ),
        [polar_rows],
        [near, own, far, reach, blend],
        [pltpu.VMEM((polar, frame_rows), F32)],
        flops=1 << 36,
        moved=8 << 20,
    )


def finish(lat, mine, other, polar_weight, mix):
    shells, _, col_count = lat.shape
    polar = polar_weight.shape[1]
    return call(
        final_kernel,
        "add_polar_rows_and_blend",
        struct(lat.shape, BF16),
        [],
        [mine, other, polar_weight, mix],
        [
            pltpu.VMEM((col_count // LANES, shells * polar, LANES), F32),
            pltpu.VMEM(lat.shape, F32),
            pltpu.VMEM(lat.shape, BF16),
            pltpu.SemaphoreType.DMA,
            pltpu.SemaphoreType.DMA((4,)),
        ],
        flops=1 << 31,
        moved=8 << 20,
        far=True,
        direct=[lat],
        mib=50,
    )


def per_device(kernel, lon_halo, lat_reach, polar_rows, polar_shift, blend):
    shells, row_count, col_count = kernel.shape
    sectors = lax.axis_size("sector")
    zones = lax.axis_size("zone")
    zone_id = lax.axis_index("zone")
    last = zones - 1
    packed, kept, near, far = pack(polar_rows, kernel, sectors)
    given = lax.ppermute(packed, "zone", [(0, 1), (last, last - 1)])
    far = lax.ppermute(far, "sector", [(i, (i + 1 if i % 2 else i - 1) % sectors) for i in range(sectors)])
    near = lax.ppermute(near, "sector", [(i, i ^ 1) for i in range(sectors)])
    inner = (zone_id == 1) | (zone_id == last - 1)
    parts = jnp.where(inner, given, kept)
    circles = lax.all_to_all(parts, "sector", 0, 0, tiled=True)
    lon_smooth, near_rows, far_rows = smooth_lon(lon_halo, kernel, near, far)
    turned = hold(jnp.concatenate([polar_rows, polar_shift, lon_halo]), circles, far_rows)
    far_rows = lax.ppermute(
        far_rows, "zone", [(i, i + 1 if i % 2 else i - 1) for i in range(1, zones - 1)]
    )
    near_rows = lax.ppermute(near_rows, "zone", [(i, i ^ 1) for i in range(zones)])
    mine = lax.all_to_all(turned, "sector", 0, 0, tiled=True)
    lat, polar_weight, mix = smooth_lat(
        polar_rows, near_rows, lon_smooth, far_rows, lat_reach[:, None], blend
    )
    mine, lat = lax.optimization_barrier((mine, lat))
    other = lax.ppermute(mine, "zone", [(0, 1), (1, 0), (last, last - 1), (last - 1, last)])
    return finish(lat, mine, other, polar_weight, mix)


def solution(mesh):
    in_specs = (P(None, "zone", "sector"), P(), P("zone"), P(), P(), P())
    out_specs = P(None, "zone", "sector")
    return jax.shard_map(
        per_device, mesh=mesh, in_specs=in_specs, out_specs=out_specs, check_vma=False
    )
```

```python
import jax
import jax.numpy as jnp
from jax import lax
from jax.experimental import pallas as pl
from jax.experimental.pallas import tpu as pltpu
from jax.sharding import PartitionSpec as P

HMAX = 48
LMAX = 32
LANES = 128
PART = 16
UNROLL = 8
PITCH = 65
F32 = jnp.float32
BF16 = jnp.bfloat16


def lanes_of(rows):
    return lax.broadcasted_iota(jnp.int32, (rows, LANES), 1)


def edge_kernel(x_ref, near_ref, far_ref, tile_ref, sems):
    shells, row_count, col_count = x_ref.shape
    half = shells // 2
    size = half * row_count
    lane = lanes_of(size)
    first = (0, col_count - LANES)
    copies = [
        pltpu.make_async_copy(x_ref.at[:, :, pl.ds(first[e], LANES)], tile_ref.at[e], sems.at[e]) for e in range(2)
    ]
    for copy in copies:
        copy.start()

    def part(e, shell):
        return tile_ref[e, shell : shell + half].reshape(size, LANES).astype(F32)

    even = lax.rem(lax.axis_index("sector"), 2) == 0
    copies[0].wait()
    low = jnp.where(lane < HMAX, part(0, 0), pltpu.roll(part(0, half), HMAX, 1))
    copies[1].wait()
    high = jnp.where(lane < HMAX, pltpu.roll(part(1, 0), HMAX, 1), pltpu.roll(part(1, half), 2 * HMAX, 1))
    near_ref[...] = jnp.where(even, high, low).astype(BF16)
    far_ref[...] = jnp.where(even, low, high).astype(BF16)


def write_polar(half, rows_ref, x_ref, send_ref, wide_ref):
    _, row_count, col_count = x_ref.shape
    tiles = col_count // LANES
    zone = lax.axis_index("zone")
    for t in range(tiles):
        for s in range(PART):
            wide_ref[t, s * PITCH : s * PITCH + row_count, :] = x_ref[
                half * PART + s, :, t * LANES : (t + 1) * LANES
            ].astype(F32)
    holders, held = send_ref.shape[0], send_ref.shape[1]
    cap = jnp.where(zone < 8, 0, holders * held)
    for k in range(holders):
        for r in range(held):
            row = jnp.clip(rows_ref[cap + k * held + r] - zone * row_count, 0, row_count - 1)
            for t in range(tiles):
                values = wide_ref[t, pl.ds(row, PART, stride=PITCH), :]
                send_ref[k, r, t * PART : (t + 1) * PART, :] = values.astype(BF16)


def first_kernel(rows_ref, x_ref, far_ref, send_ref, wide_ref):
    write_polar(1, rows_ref, x_ref, send_ref, wide_ref)


def second_kernel(rows_ref, x_ref, given_ref, send_ref, wide_ref):
    write_polar(0, rows_ref, x_ref, send_ref, wide_ref)


def band_terms(half_f):
    rate = 4.5 / (half_f * half_f)
    tap = (lanes_of(half_f.shape[0]) - HMAX).astype(F32)
    terms = jnp.where(jnp.abs(tap) <= half_f, jnp.exp(-rate * (tap * tap)), 0.0)
    return rate, jnp.broadcast_to(1.0 / jnp.sum(terms, axis=1, keepdims=True), half_f.shape)


def lon_kernel(halo_ref, x_ref, near_ref, far_ref,
               out_ref, near_rows_ref, far_rows_ref, wide_ref, done_ref, half_ref, rate_ref, scale_ref):
    shells, row_count, col_count = x_ref.shape
    total = shells * row_count
    size = total // 2
    tiles = col_count // LANES
    zone = lax.axis_index("zone")
    for i in range(row_count):
        half_ref[i : i + 1, :] = jnp.full((1, LANES), halo_ref[zone * row_count + i], jnp.int32).astype(F32)
    rate_ref[...], scale_ref[...] = band_terms(half_ref[...])
    lane = lanes_of(size)
    even = lax.rem(lax.axis_index("sector"), 2) == 0
    near = near_ref[...].astype(F32)
    far = far_ref[...].astype(F32)
    before = jnp.where(even, far, near)
    after = jnp.where(even, near, far)

    def keep(t, part, values):
        for s in range(shells // 2):
            first = (part * (shells // 2) + s) * PITCH
            wide_ref[t, first : first + row_count, :] = values[s * row_count : (s + 1) * row_count]

    for part in range(2):
        shell = slice(part * (shells // 2), (part + 1) * (shells // 2))
        previous = before if part == 0 else pltpu.roll(before, LANES - HMAX, 1)
        for t in range(tiles):
            turned = pltpu.roll(
                x_ref[shell, :, t * LANES : (t + 1) * LANES].reshape(size, LANES).astype(F32), HMAX, 1
            )
            keep(t, part, jnp.where(lane < HMAX, previous, turned))
            previous = turned
        edge = pltpu.roll(after, HMAX, 1) if part == 0 else after
        keep(tiles, part, jnp.where(lane < HMAX, previous, jnp.where(lane < 2 * HMAX, edge, 0.0)))
    depth = 2 * LANES
    offset = (lanes_of(depth) - lax.broadcasted_iota(jnp.int32, (depth, LANES), 0) + HMAX).astype(F32)
    square = offset * offset
    distance = jnp.abs(offset)

    def some_rows(block, carry):
        for u in range(UNROLL):
            i = block * UNROLL + u
            line = pl.ds(i, 1)
            band = jnp.where(distance <= half_ref[line, :], jnp.exp(-rate_ref[line, :] * square), 0.0)
            band = (band * scale_ref[line, :]).astype(BF16)
            values = [wide_ref[t, pl.ds(i, shells, stride=PITCH), :].astype(BF16) for t in range(tiles + 1)]
            stacked = jnp.concatenate(
                [jnp.concatenate(values[:tiles], axis=0), jnp.concatenate(values[1:], axis=0)], axis=1
            )
            result = jnp.dot(stacked, band, preferred_element_type=F32)
            for t in range(tiles):
                done_ref[t, pl.ds(i, shells, stride=PITCH), :] = result[t * shells : (t + 1) * shells]
        return carry

    lax.fori_loop(0, row_count // UNROLL, some_rows, 0)
    for t in range(tiles):
        for s in range(shells):
            out_ref[s, :, t * LANES : (t + 1) * LANES] = done_ref[t, s * PITCH : s * PITCH + row_count, :].astype(BF16)
    odd = lax.rem(zone, 2)
    last = row_count - LMAX
    near_rows_ref[...] = out_ref[:, pl.ds(pl.multiple_of((1 - odd) * last, LMAX), LMAX), :]
    far_rows_ref[...] = out_ref[:, pl.ds(pl.multiple_of(odd * last, LMAX), LMAX), :]


def hold_kernel(table_ref, x_ref, after_ref, out_ref, circle_ref):
    sectors, held, block, _ = x_ref.shape
    zone, sector = lax.axis_index("zone"), lax.axis_index("sector")
    polar = 2 * sectors * held
    cap = jnp.where(zone < 8, 0, sectors * held)
    length = sectors * block
    full_lon = length // PART * LANES
    depth = 3 * LANES
    for r in range(held):
        for copy in range(2):
            circle_ref[r, copy * length : (copy + 1) * length, :] = x_ref[:, r].reshape(length, LANES)
        circle_ref[r, 2 * length : 2 * length + 2 * PART, :] = circle_ref[r, 0 : 2 * PART, :]
    for r in range(held):
        entry = cap + sector * held + r
        half_f = jnp.full((1, LANES), table_ref[2 * polar + table_ref[entry]], jnp.int32).astype(F32)
        rate, scale = band_terms(half_f)
        start = lax.rem(2 * full_lon - table_ref[polar + entry] - HMAX, full_lon)
        first = start // LANES
        rest = start - first * LANES
        offset = (
            lanes_of(depth) - lax.broadcasted_iota(jnp.int32, (depth, LANES), 0) + (rest + HMAX)
        ).astype(F32)
        band = jnp.where(jnp.abs(offset) <= half_f, jnp.exp(-rate * (offset * offset)), 0.0) * scale
        values = jnp.concatenate(
            [circle_ref[r, pl.ds(pl.multiple_of((first + u) * PART, PART), length), :] for u in range(3)], axis=1
        )
        result = jnp.dot(values, band.astype(BF16), preferred_element_type=F32)
        out_ref[:, r] = result.astype(BF16).reshape(sectors, block, LANES)


def lat_kernel(rows_ref, near_ref, own_ref, far_ref, reach_ref, blend_ref,
               out_ref, polar_weight_ref, mix_ref, pick_ref):
    shells, row_count, col_count = own_ref.shape
    frame_rows = row_count + 2 * LMAX
    polar = pick_ref.shape[0]
    zone = lax.axis_index("zone")
    cap = jnp.where(zone < 8, 0, polar)
    lane = lanes_of(1)
    for p in range(polar):
        pick_ref[p : p + 1, :] = (lane == rows_ref[cap + p] - zone * row_count + LMAX).astype(F32)
    pick = pick_ref[...]
    zones = lax.axis_size("zone")
    reach = reach_ref[...]
    column = lax.broadcasted_iota(jnp.int32, (row_count, frame_rows), 1)
    away = column - LMAX - lax.broadcasted_iota(jnp.int32, (row_count, frame_rows), 0)
    source = zone * row_count - LMAX + column
    valid = (jnp.abs(away) <= reach) & (source >= 0) & (source < zones * row_count)
    reach_f = reach.astype(F32)
    away_f = away.astype(F32)
    weights = jnp.where(valid, jnp.exp(-(4.5 / (reach_f * reach_f)) * (away_f * away_f)), 0.0)
    weight = (weights / jnp.sum(weights, axis=1, keepdims=True)).astype(BF16)
    length = mix_ref.shape[0]
    group = length // shells
    spread = (
        lax.broadcasted_iota(jnp.int32, (length, shells), 0) // group
        == lax.broadcasted_iota(jnp.int32, (length, shells), 1)
    ).astype(F32).astype(BF16)
    tall = jnp.dot(spread, blend_ref[...], preferred_element_type=F32).astype(BF16)
    full = lax.dot_general(tall, spread, (((1,), (1,)), ((), ())), preferred_element_type=F32)
    same = (
        lax.broadcasted_iota(jnp.int32, (length, length), 0) % group
        == lax.broadcasted_iota(jnp.int32, (length, length), 1) % group
    )
    mix_ref[...] = jnp.where(same, full, 0.0).astype(BF16)
    polar_weight_ref[...] = lax.dot_general(
        weight, pick.astype(BF16), (((1,), (1,)), ((), ())), preferred_element_type=F32
    ).astype(BF16)
    rest = weight.astype(F32) * (1.0 - jnp.sum(pick, axis=0, keepdims=True))
    wide = lanes_of(row_count)
    turned = jnp.where(
        wide < LMAX,
        pltpu.roll(rest, LMAX, 1),
        jnp.where(wide < frame_rows - LMAX, rest, pltpu.roll(rest, frame_rows - LMAX, 1)),
    )
    rest = jnp.where(lax.rem(zone, 2) == 0, turned, rest).astype(BF16)

    def some_shells(block, carry):
        for u in range(4):
            s = block * 4 + u
            values = jnp.concatenate([near_ref[s], own_ref[s], far_ref[s]], axis=0)
            out_ref[s] = jnp.dot(rest, values, preferred_element_type=F32)
        return carry

    lax.fori_loop(0, shells // 4, some_shells, 0)


def final_kernel(mine_ref, other_ref, polar_weight_ref, mix_ref, lat_ref,
                 out_ref, polar_ref, sum_ref, stage_ref, sem, sems):
    shells, row_count, col_count = lat_ref.shape
    holders, held = mine_ref.shape[:2]
    tiles = col_count // LANES
    polar = holders * held
    fetch = pltpu.make_async_copy(lat_ref, sum_ref, sem)
    fetch.start()
    zone = lax.axis_index("zone")
    outer = (zone == 0) | (zone == 15)
    mine_first = jnp.where(outer, 0, PART * (polar + 1))
    for ref, first in ((mine_ref, mine_first), (other_ref, PART * (polar + 1) - mine_first)):
        for k in range(holders):
            for r in range(held):
                for t in range(tiles):
                    polar_ref[t, pl.ds(first + k * held + r, PART, stride=polar + 1), :] = ref[
                        k, r, t * PART : (t + 1) * PART, :
                    ].astype(F32)
    weight = polar_weight_ref[...]
    fetch.wait()

    def some_shells(index, carry):
        for u in range(4):
            s = index * 4 + u
            base = s * (polar + 1)
            values = jnp.concatenate(
                [polar_ref[t, pl.ds(base, polar), :].astype(BF16) for t in range(tiles)], axis=1
            )
            sum_ref[s] += jnp.dot(weight, values, preferred_element_type=F32)
        return carry

    lax.fori_loop(0, shells // 4, some_shells, 0)
    group = mix_ref.shape[0] // shells
    mix = mix_ref[...]
    stores = []
    for g in range(row_count // (2 * group)):
        mixed = []
        for e in range(2):
            first = (2 * g + e) * group
            values = sum_ref[:, first : first + group, :].reshape(shells * group, col_count).astype(BF16)
            mixed.append(jnp.dot(mix, values, preferred_element_type=F32).reshape(shells, group, col_count))
        rows = pl.ds(2 * g * group, 2 * group)
        stage_ref[:, rows, :] = jnp.concatenate(mixed, axis=1).astype(BF16)
        stores.append(pltpu.make_async_copy(stage_ref.at[:, rows], out_ref.at[:, rows], sems.at[g]))
        stores[-1].start()
    for store in stores:
        store.wait()


def call(kernel, name, out_shape, scalars, arrays, scratch, flops=0, moved=0, direct=(), far=False, mib=16):
    smem = pl.BlockSpec(memory_space=pltpu.SMEM)
    vmem = pl.BlockSpec(memory_space=pltpu.VMEM)
    anywhere = pl.BlockSpec(memory_space=pl.ANY)
    many = isinstance(out_shape, tuple)
    return pl.pallas_call(
        kernel,
        out_shape=out_shape,
        in_specs=[smem] * len(scalars) + [vmem] * len(arrays) + [anywhere] * len(direct),
        out_specs=(vmem,) * len(out_shape) if many else anywhere if far else vmem,
        scratch_shapes=scratch,
        compiler_params=pltpu.CompilerParams(vmem_limit_bytes=mib << 20),
        cost_estimate=pl.CostEstimate(flops=flops, bytes_accessed=moved, transcendentals=0),
        name=name,
    )(*scalars, *arrays, *direct)


struct = jax.ShapeDtypeStruct


def pack(polar_rows, kernel, sectors):
    shells, row_count, col_count = kernel.shape
    tiles = col_count // LANES
    held = polar_rows.shape[0] // 2 // sectors
    send = struct((sectors, held, tiles * PART, LANES), BF16)
    edge = struct((shells * row_count // 2, LANES), BF16)
    wide = pltpu.VMEM((tiles, PART * PITCH, LANES), F32)
    tile = pltpu.VMEM((2, shells, row_count, LANES), BF16)
    near, far = call(
        edge_kernel, "cut_edges", (edge, edge), [], [], [tile, pltpu.SemaphoreType.DMA((2,))],
        moved=4 << 20, direct=[kernel],
    )
    given = call(
        first_kernel, "pack_half_of_shells", send, [polar_rows], [kernel], [wide],
        moved=4 << 20, direct=[far],
    )
    kept = call(
        second_kernel, "pack_other_half_of_shells", send, [polar_rows], [kernel], [wide],
        moved=4 << 20, direct=[given],
    )
    return given, kept, near, far


def smooth_lon(lon_halo, kernel, near, far):
    shells, row_count, col_count = kernel.shape
    tiles = col_count // LANES
    rows = pltpu.VMEM((row_count, LANES), F32)
    return call(
        lon_kernel,
        "smooth_along_longitude",
        (
            struct((shells, row_count, col_count), BF16),
            struct((shells, LMAX, col_count), BF16),
            struct((shells, LMAX, col_count), BF16),
        ),
        [lon_halo],
        [kernel, near, far],
        [
            pltpu.VMEM((tiles + 1, shells * PITCH, LANES), F32),
            pltpu.VMEM((tiles, shells * PITCH, LANES), F32),
            rows,
            rows,
            rows,
        ],
        flops=1 << 36,
        moved=16 << 20,
        mib=20,
    )


def hold(table, circles, after):
    sectors, held, block, _ = circles.shape
    return call(
        hold_kernel,
        "smooth_and_turn_polar_circles",
        struct(circles.shape, BF16),
        [table],
        [circles],
        [pltpu.VMEM((held, 2 * sectors * block + 2 * PART, LANES), BF16)],
        flops=1 << 30,
        moved=4 << 20,
        direct=[after],
    )


def smooth_lat(polar_rows, near, own, far, reach, blend):
    shells, row_count, _ = own.shape
    frame_rows = row_count + 2 * LMAX
    polar = polar_rows.shape[0] // 2
    return call(
        lat_kernel,
        "smooth_along_latitude",
        (
            struct(own.shape, F32),
            struct((row_count, polar), BF16),
            struct((shells * 8, shells * 8), BF16),
        ),
        [polar_rows],
        [near, own, far, reach, blend],
        [pltpu.VMEM((polar, frame_rows), F32)],
        flops=1 << 36,
        moved=8 << 20,
    )


def finish(lat, mine, other, polar_weight, mix):
    shells, _, col_count = lat.shape
    polar = polar_weight.shape[1]
    return call(
        final_kernel,
        "add_polar_rows_and_blend",
        struct(lat.shape, BF16),
        [],
        [mine, other, polar_weight, mix],
        [
            pltpu.VMEM((col_count // LANES, shells * (polar + 1), LANES), F32),
            pltpu.VMEM(lat.shape, F32),
            pltpu.VMEM(lat.shape, BF16),
            pltpu.SemaphoreType.DMA,
            pltpu.SemaphoreType.DMA((4,)),
        ],
        flops=1 << 31,
        moved=8 << 20,
        far=True,
        direct=[lat],
        mib=50,
    )


def per_device(kernel, lon_halo, lat_reach, polar_rows, polar_shift, blend):
    shells, row_count, col_count = kernel.shape
    sectors = lax.axis_size("sector")
    zones = lax.axis_size("zone")
    zone_id = lax.axis_index("zone")
    last = zones - 1
    packed, kept, near, far = pack(polar_rows, kernel, sectors)
    given = lax.ppermute(packed, "zone", [(0, 1), (last, last - 1)])
    far = lax.ppermute(far, "sector", [(i, (i + 1 if i % 2 else i - 1) % sectors) for i in range(sectors)])
    near = lax.ppermute(near, "sector", [(i, i ^ 1) for i in range(sectors)])
    inner = (zone_id == 1) | (zone_id == last - 1)
    parts = jnp.where(inner, given, kept)
    circles = lax.all_to_all(parts, "sector", 0, 0, tiled=True)
    lon_smooth, near_rows, far_rows = smooth_lon(lon_halo, kernel, near, far)
    turned = hold(jnp.concatenate([polar_rows, polar_shift, lon_halo]), circles, far_rows)
    far_rows = lax.ppermute(
        far_rows, "zone", [(i, i + 1 if i % 2 else i - 1) for i in range(1, zones - 1)]
    )
    near_rows = lax.ppermute(near_rows, "zone", [(i, i ^ 1) for i in range(zones)])
    mine = lax.all_to_all(turned, "sector", 0, 0, tiled=True)
    lat, polar_weight, mix = smooth_lat(
        polar_rows, near_rows, lon_smooth, far_rows, lat_reach[:, None], blend
    )
    mine, lat = lax.optimization_barrier((mine, lat))
    other = lax.ppermute(mine, "zone", [(0, 1), (1, 0), (last, last - 1), (last - 1, last)])
    return finish(lat, mine, other, polar_weight, mix)


def solution(mesh):
    in_specs = (P(None, "zone", "sector"), P(), P("zone"), P(), P(), P())
    out_specs = P(None, "zone", "sector")
    return jax.shard_map(
        per_device, mesh=mesh, in_specs=in_specs, out_specs=out_specs, check_vma=False
    )
```

```python
import jax
import jax.numpy as jnp
from jax import lax
from jax.experimental import pallas as pl
from jax.experimental.pallas import tpu as pltpu
from jax.sharding import PartitionSpec as P

HMAX = 48
LMAX = 32
LANES = 128
PART = 16
UNROLL = 8
PITCH = 65
F32 = jnp.float32
BF16 = jnp.bfloat16


def lanes_of(rows):
    return lax.broadcasted_iota(jnp.int32, (rows, LANES), 1)


def write_edges(x_ref, near_ref, far_ref):
    shells, row_count, col_count = x_ref.shape
    half = shells // 2
    size = half * row_count
    lane = lanes_of(size)

    def part(column, shell):
        return x_ref[shell : shell + half, :, column : column + LANES].reshape(size, LANES).astype(F32)

    last = col_count - LANES
    even = lax.rem(lax.axis_index("sector"), 2) == 0
    low = jnp.where(lane < HMAX, part(0, 0), pltpu.roll(part(0, half), HMAX, 1))
    high = jnp.where(lane < HMAX, pltpu.roll(part(last, 0), HMAX, 1), pltpu.roll(part(last, half), 2 * HMAX, 1))
    near_ref[...] = jnp.where(even, high, low).astype(BF16)
    far_ref[...] = jnp.where(even, low, high).astype(BF16)


def write_polar(half, rows_ref, x_ref, send_ref, wide_ref):
    _, row_count, col_count = x_ref.shape
    tiles = col_count // LANES
    zone = lax.axis_index("zone")
    for t in range(tiles):
        for s in range(PART):
            wide_ref[t, s * PITCH : s * PITCH + row_count, :] = x_ref[
                half * PART + s, :, t * LANES : (t + 1) * LANES
            ].astype(F32)
    holders, held = send_ref.shape[0], send_ref.shape[1]
    cap = jnp.where(zone < 8, 0, holders * held)
    for k in range(holders):
        for r in range(held):
            row = jnp.clip(rows_ref[cap + k * held + r] - zone * row_count, 0, row_count - 1)
            for t in range(tiles):
                values = wide_ref[t, pl.ds(row, PART, stride=PITCH), :]
                send_ref[k, r, t * PART : (t + 1) * PART, :] = values.astype(BF16)


def first_kernel(x_ref, far_rows_ref, send_ref, near_ref, far_ref, wide_ref, held_ref, rows_ref, sems):
    fetch = pltpu.make_async_copy(far_rows_ref, rows_ref, sems.at[2])
    fetch.start()
    copies = []
    for half in (1, 0):
        shells = pl.ds(half * PART, PART)
        copies.append(pltpu.make_async_copy(x_ref.at[shells], held_ref.at[shells], sems.at[half]))
        copies[-1].start()
    fetch.wait()
    copies[0].wait()
    write_polar(1, rows_ref, held_ref, send_ref, wide_ref)
    copies[1].wait()
    write_edges(held_ref, near_ref, far_ref)


def second_kernel(rows_ref, x_ref, given_ref, send_ref, wide_ref, sem):
    zone = lax.axis_index("zone")
    inner = (zone == 1) | (zone == lax.axis_size("zone") - 2)

    @pl.when(inner)
    def _():
        copy = pltpu.make_async_copy(given_ref, send_ref, sem)
        copy.start()
        copy.wait()

    @pl.when(jnp.logical_not(inner))
    def _():
        write_polar(0, rows_ref, x_ref, send_ref, wide_ref)


def band_terms(half_f):
    rate = 4.5 / (half_f * half_f)
    tap = (lanes_of(half_f.shape[0]) - HMAX).astype(F32)
    terms = jnp.where(jnp.abs(tap) <= half_f, jnp.exp(-rate * (tap * tap)), 0.0)
    return rate, jnp.broadcast_to(1.0 / jnp.sum(terms, axis=1, keepdims=True), half_f.shape)


def lon_kernel(halo_ref, x_ref, near_ref, far_ref,
               out_ref, near_rows_ref, far_rows_ref, wide_ref, done_ref, half_ref, rate_ref, scale_ref):
    shells, row_count, col_count = x_ref.shape
    total = shells * row_count
    size = total // 2
    tiles = col_count // LANES
    zone = lax.axis_index("zone")
    for i in range(row_count):
        half_ref[i : i + 1, :] = jnp.full((1, LANES), halo_ref[zone * row_count + i], jnp.int32).astype(F32)
    rate_ref[...], scale_ref[...] = band_terms(half_ref[...])
    lane = lanes_of(size)
    even = lax.rem(lax.axis_index("sector"), 2) == 0
    near = near_ref[...].astype(F32)
    far = far_ref[...].astype(F32)
    before = jnp.where(even, far, near)
    after = jnp.where(even, near, far)

    def keep(t, part, values):
        for s in range(shells // 2):
            first = (part * (shells // 2) + s) * PITCH
            wide_ref[t, first : first + row_count, :] = values[s * row_count : (s + 1) * row_count]

    for part in range(2):
        shell = slice(part * (shells // 2), (part + 1) * (shells // 2))
        previous = before if part == 0 else pltpu.roll(before, LANES - HMAX, 1)
        for t in range(tiles):
            turned = pltpu.roll(
                x_ref[shell, :, t * LANES : (t + 1) * LANES].reshape(size, LANES).astype(F32), HMAX, 1
            )
            keep(t, part, jnp.where(lane < HMAX, previous, turned))
            previous = turned
        edge = pltpu.roll(after, HMAX, 1) if part == 0 else after
        keep(tiles, part, jnp.where(lane < HMAX, previous, jnp.where(lane < 2 * HMAX, edge, 0.0)))
    depth = 2 * LANES
    offset = (lanes_of(depth) - lax.broadcasted_iota(jnp.int32, (depth, LANES), 0) + HMAX).astype(F32)
    square = offset * offset
    distance = jnp.abs(offset)

    def some_rows(block, carry):
        for u in range(UNROLL):
            i = block * UNROLL + u
            line = pl.ds(i, 1)
            band = jnp.where(distance <= half_ref[line, :], jnp.exp(-rate_ref[line, :] * square), 0.0)
            band = (band * scale_ref[line, :]).astype(BF16)
            values = [wide_ref[t, pl.ds(i, shells, stride=PITCH), :].astype(BF16) for t in range(tiles + 1)]
            stacked = jnp.concatenate(
                [jnp.concatenate(values[:tiles], axis=0), jnp.concatenate(values[1:], axis=0)], axis=1
            )
            result = jnp.dot(stacked, band, preferred_element_type=F32)
            for t in range(tiles):
                done_ref[t, pl.ds(i, shells, stride=PITCH), :] = result[t * shells : (t + 1) * shells]
        return carry

    lax.fori_loop(0, row_count // UNROLL, some_rows, 0)
    for t in range(tiles):
        for s in range(shells):
            out_ref[s, :, t * LANES : (t + 1) * LANES] = done_ref[t, s * PITCH : s * PITCH + row_count, :].astype(BF16)
    odd = lax.rem(zone, 2)
    last = row_count - LMAX
    near_rows_ref[...] = out_ref[:, pl.ds(pl.multiple_of((1 - odd) * last, LMAX), LMAX), :]
    far_rows_ref[...] = out_ref[:, pl.ds(pl.multiple_of(odd * last, LMAX), LMAX), :]


def hold_kernel(table_ref, x_ref, after_ref, out_ref, circle_ref):
    sectors, held, block, _ = x_ref.shape
    zone, sector = lax.axis_index("zone"), lax.axis_index("sector")
    polar = 2 * sectors * held
    cap = jnp.where(zone < 8, 0, sectors * held)
    length = sectors * block
    full_lon = length // PART * LANES
    depth = 3 * LANES
    for r in range(held):
        for copy in range(2):
            circle_ref[r, copy * length : (copy + 1) * length, :] = x_ref[:, r].reshape(length, LANES)
        circle_ref[r, 2 * length : 2 * length + 2 * PART, :] = circle_ref[r, 0 : 2 * PART, :]
    for r in range(held):
        entry = cap + sector * held + r
        half_f = jnp.full((1, LANES), table_ref[2 * polar + table_ref[entry]], jnp.int32).astype(F32)
        rate, scale = band_terms(half_f)
        start = lax.rem(2 * full_lon - table_ref[polar + entry] - HMAX, full_lon)
        first = start // LANES
        rest = start - first * LANES
        offset = (
            lanes_of(depth) - lax.broadcasted_iota(jnp.int32, (depth, LANES), 0) + (rest + HMAX)
        ).astype(F32)
        band = jnp.where(jnp.abs(offset) <= half_f, jnp.exp(-rate * (offset * offset)), 0.0) * scale
        values = jnp.concatenate(
            [circle_ref[r, pl.ds(pl.multiple_of((first + u) * PART, PART), length), :] for u in range(3)], axis=1
        )
        result = jnp.dot(values, band.astype(BF16), preferred_element_type=F32)
        out_ref[:, r] = result.astype(BF16).reshape(sectors, block, LANES)


def lat_kernel(rows_ref, near_ref, own_ref, far_ref, reach_ref, blend_ref,
               out_ref, polar_weight_ref, mix_ref, pick_ref):
    shells, row_count, col_count = own_ref.shape
    frame_rows = row_count + 2 * LMAX
    polar = pick_ref.shape[0]
    zone = lax.axis_index("zone")
    cap = jnp.where(zone < 8, 0, polar)
    lane = lanes_of(1)
    for p in range(polar):
        pick_ref[p : p + 1, :] = (lane == rows_ref[cap + p] - zone * row_count + LMAX).astype(F32)
    pick = pick_ref[...]
    zones = lax.axis_size("zone")
    reach = reach_ref[...]
    column = lax.broadcasted_iota(jnp.int32, (row_count, frame_rows), 1)
    away = column - LMAX - lax.broadcasted_iota(jnp.int32, (row_count, frame_rows), 0)
    source = zone * row_count - LMAX + column
    valid = (jnp.abs(away) <= reach) & (source >= 0) & (source < zones * row_count)
    reach_f = reach.astype(F32)
    away_f = away.astype(F32)
    weights = jnp.where(valid, jnp.exp(-(4.5 / (reach_f * reach_f)) * (away_f * away_f)), 0.0)
    weight = (weights / jnp.sum(weights, axis=1, keepdims=True)).astype(BF16)
    length = mix_ref.shape[0]
    group = length // shells
    spread = (
        lax.broadcasted_iota(jnp.int32, (length, shells), 0) // group
        == lax.broadcasted_iota(jnp.int32, (length, shells), 1)
    ).astype(F32).astype(BF16)
    tall = jnp.dot(spread, blend_ref[...], preferred_element_type=F32).astype(BF16)
    full = lax.dot_general(tall, spread, (((1,), (1,)), ((), ())), preferred_element_type=F32)
    same = (
        lax.broadcasted_iota(jnp.int32, (length, length), 0) % group
        == lax.broadcasted_iota(jnp.int32, (length, length), 1) % group
    )
    mix_ref[...] = jnp.where(same, full, 0.0).astype(BF16)
    polar_weight_ref[...] = lax.dot_general(
        weight, pick.astype(BF16), (((1,), (1,)), ((), ())), preferred_element_type=F32
    ).astype(BF16)
    rest = weight.astype(F32) * (1.0 - jnp.sum(pick, axis=0, keepdims=True))
    wide = lanes_of(row_count)
    turned = jnp.where(
        wide < LMAX,
        pltpu.roll(rest, LMAX, 1),
        jnp.where(wide < frame_rows - LMAX, rest, pltpu.roll(rest, frame_rows - LMAX, 1)),
    )
    rest = jnp.where(lax.rem(zone, 2) == 0, turned, rest).astype(BF16)

    def some_shells(block, carry):
        for u in range(4):
            s = block * 4 + u
            values = jnp.concatenate([near_ref[s], own_ref[s], far_ref[s]], axis=0)
            out_ref[s] = jnp.dot(rest, values, preferred_element_type=F32)
        return carry

    lax.fori_loop(0, shells // 4, some_shells, 0)


def own_part():
    zone = lax.axis_index("zone")
    return jnp.where((zone == 0) | (zone == lax.axis_size("zone") - 1), 0, 1)


def add_polar(part, source_ref, weight_ref, lat_ref, polar_ref, sum_ref, sem, put):
    holders, held = source_ref.shape[:2]
    tiles = polar_ref.shape[0]
    polar = holders * held
    pitch = polar + 1
    fetch = pltpu.make_async_copy(lat_ref.at[pl.ds(part * PART, PART)], sum_ref, sem)
    fetch.start()
    for k in range(holders):
        for r in range(held):
            for t in range(tiles):
                polar_ref[t, pl.ds(k * held + r, PART, stride=pitch), :] = source_ref[
                    k, r, t * PART : (t + 1) * PART, :
                ].astype(F32)
    weight = weight_ref[...]
    fetch.wait()

    def some_shells(index, carry):
        for u in range(4):
            s = index * 4 + u
            values = jnp.concatenate(
                [polar_ref[t, pl.ds(s * pitch, polar), :].astype(BF16) for t in range(tiles)], axis=1
            )
            put(s, sum_ref[s] + jnp.dot(weight, values, preferred_element_type=F32))
        return carry

    lax.fori_loop(0, PART // 4, some_shells, 0)


def own_kernel(mine_ref, weight_ref, lat_ref, out_ref, polar_ref, sum_ref, sem):
    def put(s, values):
        out_ref[s] = values.astype(BF16)

    add_polar(own_part(), mine_ref, weight_ref, lat_ref, polar_ref, sum_ref, sem, put)


def final_kernel(other_ref, own_ref, weight_ref, mix_ref, lat_ref, out_ref,
                 polar_ref, sum_ref, full_ref, stage_ref, sem, sems):
    shells, row_count, col_count = lat_ref.shape
    part = own_part()

    def put(s, values):
        full_ref[(1 - part) * PART + s] = values

    add_polar(1 - part, other_ref, weight_ref, lat_ref, polar_ref, sum_ref, sem, put)
    for s in range(PART):
        full_ref[part * PART + s] = own_ref[s].astype(F32)
    group = mix_ref.shape[0] // shells
    mix = mix_ref[...]
    stores = []
    for g in range(row_count // (2 * group)):
        mixed = []
        for e in range(2):
            first = (2 * g + e) * group
            values = full_ref[:, first : first + group, :].reshape(shells * group, col_count).astype(BF16)
            mixed.append(jnp.dot(mix, values, preferred_element_type=F32).reshape(shells, group, col_count))
        rows = pl.ds(2 * g * group, 2 * group)
        stage_ref[:, rows, :] = jnp.concatenate(mixed, axis=1).astype(BF16)
        stores.append(pltpu.make_async_copy(stage_ref.at[:, rows], out_ref.at[:, rows], sems.at[g]))
        stores[-1].start()
    for store in stores:
        store.wait()


def call(kernel, name, out_shape, scalars, arrays, scratch, flops=0, moved=0, direct=(), far=False, mib=16):
    smem = pl.BlockSpec(memory_space=pltpu.SMEM)
    vmem = pl.BlockSpec(memory_space=pltpu.VMEM)
    anywhere = pl.BlockSpec(memory_space=pl.ANY)
    many = isinstance(out_shape, tuple)
    return pl.pallas_call(
        kernel,
        out_shape=out_shape,
        in_specs=[smem] * len(scalars) + [vmem] * len(arrays) + [anywhere] * len(direct),
        out_specs=(vmem,) * len(out_shape) if many else anywhere if far else vmem,
        scratch_shapes=scratch,
        compiler_params=pltpu.CompilerParams(vmem_limit_bytes=mib << 20),
        cost_estimate=pl.CostEstimate(flops=flops, bytes_accessed=moved, transcendentals=0),
        name=name,
    )(*scalars, *arrays, *direct)


struct = jax.ShapeDtypeStruct


def pack_first(polar_rows, kernel, sectors):
    shells, row_count, col_count = kernel.shape
    tiles = col_count // LANES
    held = polar_rows.shape[0] // 2 // sectors
    edge = struct((shells * row_count // 2, LANES), BF16)
    return call(
        first_kernel,
        "pack_half_of_shells_and_edges",
        (struct((sectors, held, tiles * PART, LANES), BF16), edge, edge),
        [],
        [],
        [
            pltpu.VMEM((tiles, PART * PITCH, LANES), F32),
            pltpu.VMEM(kernel.shape, BF16),
            pltpu.SMEM(polar_rows.shape, jnp.int32),
            pltpu.SemaphoreType.DMA((3,)),
        ],
        moved=4 << 20,
        direct=[kernel, polar_rows],
        mib=52,
    )


def pack_second(polar_rows, kernel, given):
    _, row_count, col_count = kernel.shape
    return call(
        second_kernel,
        "pack_other_half_or_take_given",
        struct(given.shape, BF16),
        [polar_rows],
        [kernel],
        [pltpu.VMEM((col_count // LANES, PART * PITCH, LANES), F32), pltpu.SemaphoreType.DMA],
        moved=4 << 20,
        direct=[given],
    )


def smooth_lon(lon_halo, kernel, near, far):
    shells, row_count, col_count = kernel.shape
    tiles = col_count // LANES
    rows = pltpu.VMEM((row_count, LANES), F32)
    return call(
        lon_kernel,
        "smooth_along_longitude",
        (
            struct((shells, row_count, col_count), BF16),
            struct((shells, LMAX, col_count), BF16),
            struct((shells, LMAX, col_count), BF16),
        ),
        [lon_halo],
        [kernel, near, far],
        [
            pltpu.VMEM((tiles + 1, shells * PITCH, LANES), F32),
            pltpu.VMEM((tiles, shells * PITCH, LANES), F32),
            rows,
            rows,
            rows,
        ],
        flops=1 << 36,
        moved=16 << 20,
        mib=20,
    )


def hold(table, circles, after):
    sectors, held, block, _ = circles.shape
    return call(
        hold_kernel,
        "smooth_and_turn_polar_circles",
        struct(circles.shape, BF16),
        [table],
        [circles],
        [pltpu.VMEM((held, 2 * sectors * block + 2 * PART, LANES), BF16)],
        flops=1 << 30,
        moved=4 << 20,
        direct=[after],
    )


def smooth_lat(polar_rows, near, own, far, reach, blend):
    shells, row_count, _ = own.shape
    frame_rows = row_count + 2 * LMAX
    polar = polar_rows.shape[0] // 2
    return call(
        lat_kernel,
        "smooth_along_latitude",
        (
            struct(own.shape, F32),
            struct((row_count, polar), BF16),
            struct((shells * 8, shells * 8), BF16),
        ),
        [polar_rows],
        [near, own, far, reach, blend],
        [pltpu.VMEM((polar, frame_rows), F32)],
        flops=1 << 36,
        moved=8 << 20,
    )


def add_own(lat, mine, polar_weight):
    shells, row_count, col_count = lat.shape
    half = (PART, row_count, col_count)
    return call(
        own_kernel,
        "add_polar_rows_of_own_shells",
        struct(half, BF16),
        [],
        [mine, polar_weight],
        [
            pltpu.VMEM((col_count // LANES, PART * (polar_weight.shape[1] + 1), LANES), F32),
            pltpu.VMEM(half, F32),
            pltpu.SemaphoreType.DMA,
        ],
        flops=1 << 30,
        moved=4 << 20,
        direct=[lat],
        mib=50,
    )


def finish(lat, other, own, polar_weight, mix):
    shells, row_count, col_count = lat.shape
    return call(
        final_kernel,
        "add_polar_rows_and_blend",
        struct(lat.shape, BF16),
        [],
        [other, own, polar_weight, mix],
        [
            pltpu.VMEM((col_count // LANES, PART * (polar_weight.shape[1] + 1), LANES), F32),
            pltpu.VMEM((PART, row_count, col_count), F32),
            pltpu.VMEM(lat.shape, F32),
            pltpu.VMEM(lat.shape, BF16),
            pltpu.SemaphoreType.DMA,
            pltpu.SemaphoreType.DMA((4,)),
        ],
        flops=1 << 31,
        moved=8 << 20,
        far=True,
        direct=[lat],
        mib=50,
    )


def per_device(kernel, lon_halo, lat_reach, polar_rows, polar_shift, blend):
    shells, row_count, col_count = kernel.shape
    sectors = lax.axis_size("sector")
    zones = lax.axis_size("zone")
    last = zones - 1
    packed, near, far = pack_first(polar_rows, kernel, sectors)
    given = lax.ppermute(packed, "zone", [(0, 1), (last, last - 1)])
    far = lax.ppermute(far, "sector", [(i, (i + 1 if i % 2 else i - 1) % sectors) for i in range(sectors)])
    near = lax.ppermute(near, "sector", [(i, i ^ 1) for i in range(sectors)])
    parts = pack_second(polar_rows, kernel, given)
    circles = lax.all_to_all(parts, "sector", 0, 0, tiled=True)
    lon_smooth, near_rows, far_rows = smooth_lon(lon_halo, kernel, near, far)
    turned = hold(jnp.concatenate([polar_rows, polar_shift, lon_halo]), circles, far_rows)
    far_rows = lax.ppermute(
        far_rows, "zone", [(i, i + 1 if i % 2 else i - 1) for i in range(1, zones - 1)]
    )
    near_rows = lax.ppermute(near_rows, "zone", [(i, i ^ 1) for i in range(zones)])
    mine = lax.all_to_all(turned, "sector", 0, 0, tiled=True)
    lat, polar_weight, mix = smooth_lat(
        polar_rows, near_rows, lon_smooth, far_rows, lat_reach[:, None], blend
    )
    mine, lat = lax.optimization_barrier((mine, lat))
    other = lax.ppermute(mine, "zone", [(0, 1), (1, 0), (last, last - 1), (last - 1, last)])
    own = add_own(lat, mine, polar_weight)
    return finish(lat, other, own, polar_weight, mix)


def solution(mesh):
    in_specs = (P(None, "zone", "sector"), P(), P("zone"), P(), P(), P())
    out_specs = P(None, "zone", "sector")
    return jax.shard_map(
        per_device, mesh=mesh, in_specs=in_specs, out_specs=out_specs, check_vma=False
    )
```

```python
import jax
import jax.numpy as jnp
from jax import lax
from jax.experimental import pallas as pl
from jax.experimental.pallas import tpu as pltpu
from jax.sharding import PartitionSpec as P

HMAX = 48
LMAX = 32
LANES = 128
PART = 16
UNROLL = 8
PITCH = 65
SETS = 3
F32 = jnp.float32
BF16 = jnp.bfloat16


def lanes_of(rows):
    return lax.broadcasted_iota(jnp.int32, (rows, LANES), 1)


def write_edges(x_ref, near_ref, far_ref):
    shells, row_count, col_count = x_ref.shape
    half = shells // 2
    size = half * row_count
    lane = lanes_of(size)

    def part(column, shell):
        return x_ref[shell : shell + half, :, column : column + LANES].reshape(size, LANES).astype(F32)

    last = col_count - LANES
    even = lax.rem(lax.axis_index("sector"), 2) == 0
    low = jnp.where(lane < HMAX, part(0, 0), pltpu.roll(part(0, half), HMAX, 1))
    high = jnp.where(lane < HMAX, pltpu.roll(part(last, 0), HMAX, 1), pltpu.roll(part(last, half), 2 * HMAX, 1))
    near_ref[...] = jnp.where(even, high, low).astype(BF16)
    far_ref[...] = jnp.where(even, low, high).astype(BF16)


def from_pole(zone):
    return jnp.minimum(zone, lax.axis_size("zone") - 1 - zone)


def write_polar(half, holders, rows_ref, x_ref, wide_ref, store):
    _, row_count, col_count = x_ref.shape
    tiles = col_count // LANES
    zone = lax.axis_index("zone")
    for t in range(tiles):
        for s in range(PART):
            wide_ref[t, s * PITCH : s * PITCH + row_count, :] = x_ref[
                half * PART + s, :, t * LANES : (t + 1) * LANES
            ].astype(F32)
    cap = jnp.where(zone < 8, 0, SETS * holders)
    for r in range(SETS):
        for k in range(holders):
            row = jnp.clip(rows_ref[cap + r * holders + k] - zone * row_count, 0, row_count - 1)
            for t in range(tiles):
                store(r, k, t, wide_ref[t, pl.ds(row, PART, stride=PITCH), :].astype(BF16))


def first_kernel(x_ref, far_rows_ref, send_ref, near_ref, far_ref, wide_ref, held_ref, rows_ref, sems):
    fetch = pltpu.make_async_copy(far_rows_ref, rows_ref, sems.at[2])
    fetch.start()
    copies = []
    for half in (1, 0):
        shells = pl.ds(half * PART, PART)
        copies.append(pltpu.make_async_copy(x_ref.at[shells], held_ref.at[shells], sems.at[half]))
        copies[-1].start()
    fetch.wait()
    copies[0].wait()

    def store(r, k, t, values):
        send_ref[r, k, t * PART : (t + 1) * PART, :] = values

    write_polar(1, send_ref.shape[1], rows_ref, held_ref, wide_ref, store)
    copies[1].wait()
    write_edges(held_ref, near_ref, far_ref)


def second_kernel(rows_ref, x_ref, given_ref, stay_ref, right_ref, left_ref, wide_ref, sems):
    outs = (stay_ref, right_ref, left_ref)
    inner = from_pole(lax.axis_index("zone")) == 1

    @pl.when(inner)
    def _():
        copies = [pltpu.make_async_copy(given_ref.at[r], outs[r], sems.at[r]) for r in range(SETS)]
        for copy in copies:
            copy.start()
        for copy in copies:
            copy.wait()

    @pl.when(jnp.logical_not(inner))
    def _():
        def store(r, k, t, values):
            outs[r][k, t * PART : (t + 1) * PART, :] = values

        write_polar(0, stay_ref.shape[0], rows_ref, x_ref, wide_ref, store)


def band_terms(half_f):
    rate = 4.5 / (half_f * half_f)
    tap = (lanes_of(half_f.shape[0]) - HMAX).astype(F32)
    terms = jnp.where(jnp.abs(tap) <= half_f, jnp.exp(-rate * (tap * tap)), 0.0)
    return rate, jnp.broadcast_to(1.0 / jnp.sum(terms, axis=1, keepdims=True), half_f.shape)


def lon_kernel(halo_ref, x_ref, near_ref, far_ref, after_ref, table_ref, reach_ref,
               out_ref, near_rows_ref, far_rows_ref, wide_ref, done_ref, half_ref, rate_ref, scale_ref):
    shells, row_count, col_count = x_ref.shape
    total = shells * row_count
    size = total // 2
    tiles = col_count // LANES
    zone = lax.axis_index("zone")
    for i in range(row_count):
        half_ref[i : i + 1, :] = jnp.full((1, LANES), halo_ref[zone * row_count + i], jnp.int32).astype(F32)
    rate_ref[...], scale_ref[...] = band_terms(half_ref[...])
    lane = lanes_of(size)
    even = lax.rem(lax.axis_index("sector"), 2) == 0
    near = near_ref[...].astype(F32)
    far = far_ref[...].astype(F32)
    before = jnp.where(even, far, near)
    after = jnp.where(even, near, far)

    def keep(t, part, values):
        for s in range(shells // 2):
            first = (part * (shells // 2) + s) * PITCH
            wide_ref[t, first : first + row_count, :] = values[s * row_count : (s + 1) * row_count]

    for part in range(2):
        shell = slice(part * (shells // 2), (part + 1) * (shells // 2))
        previous = before if part == 0 else pltpu.roll(before, LANES - HMAX, 1)
        for t in range(tiles):
            turned = pltpu.roll(
                x_ref[shell, :, t * LANES : (t + 1) * LANES].reshape(size, LANES).astype(F32), HMAX, 1
            )
            keep(t, part, jnp.where(lane < HMAX, previous, turned))
            previous = turned
        edge = pltpu.roll(after, HMAX, 1) if part == 0 else after
        keep(tiles, part, jnp.where(lane < HMAX, previous, jnp.where(lane < 2 * HMAX, edge, 0.0)))
    depth = 2 * LANES
    offset = (lanes_of(depth) - lax.broadcasted_iota(jnp.int32, (depth, LANES), 0) + HMAX).astype(F32)
    square = offset * offset
    distance = jnp.abs(offset)

    def some_rows(block, carry):
        for u in range(UNROLL):
            i = block * UNROLL + u
            line = pl.ds(i, 1)
            band = jnp.where(distance <= half_ref[line, :], jnp.exp(-rate_ref[line, :] * square), 0.0)
            band = (band * scale_ref[line, :]).astype(BF16)
            values = [wide_ref[t, pl.ds(i, shells, stride=PITCH), :].astype(BF16) for t in range(tiles + 1)]
            stacked = jnp.concatenate(
                [jnp.concatenate(values[:tiles], axis=0), jnp.concatenate(values[1:], axis=0)], axis=1
            )
            result = jnp.dot(stacked, band, preferred_element_type=F32)
            for t in range(tiles):
                done_ref[t, pl.ds(i, shells, stride=PITCH), :] = result[t * shells : (t + 1) * shells]
        return carry

    lax.fori_loop(0, row_count // UNROLL, some_rows, 0)
    for t in range(tiles):
        for s in range(shells):
            out_ref[s, :, t * LANES : (t + 1) * LANES] = done_ref[t, s * PITCH : s * PITCH + row_count, :].astype(BF16)
    odd = lax.rem(zone, 2)
    last = row_count - LMAX
    near_rows_ref[...] = out_ref[:, pl.ds(pl.multiple_of((1 - odd) * last, LMAX), LMAX), :]
    far_rows_ref[...] = out_ref[:, pl.ds(pl.multiple_of(odd * last, LMAX), LMAX), :]


def hold_kernel(table_ref, x_ref, after_ref, out_ref, circle_ref):
    sectors, block, _ = x_ref.shape
    zone, sector = lax.axis_index("zone"), lax.axis_index("sector")
    polar = 2 * sectors * SETS
    length = sectors * block
    full_lon = length // PART * LANES
    depth = 3 * LANES
    for copy in range(2):
        circle_ref[copy * length : (copy + 1) * length, :] = x_ref[...].reshape(length, LANES)
    circle_ref[2 * length : 2 * length + 2 * PART, :] = circle_ref[0 : 2 * PART, :]
    chip = from_pole(zone) // 2
    kept = jnp.where(chip == 1, 1, jnp.where(chip == 3, 2, 0))
    entry = jnp.where(zone < 8, 0, sectors * SETS) + kept * sectors + sector
    half_f = jnp.full((1, LANES), table_ref[2 * polar + table_ref[entry]], jnp.int32).astype(F32)
    rate, scale = band_terms(half_f)
    start = lax.rem(2 * full_lon - table_ref[polar + entry] - HMAX, full_lon)
    first = start // LANES
    rest = start - first * LANES
    offset = (lanes_of(depth) - lax.broadcasted_iota(jnp.int32, (depth, LANES), 0) + (rest + HMAX)).astype(F32)
    band = jnp.where(jnp.abs(offset) <= half_f, jnp.exp(-rate * (offset * offset)), 0.0) * scale
    values = jnp.concatenate(
        [circle_ref[pl.ds(pl.multiple_of((first + u) * PART, PART), length), :] for u in range(3)], axis=1
    )
    result = jnp.dot(values, band.astype(BF16), preferred_element_type=F32)
    out_ref[...] = result.astype(BF16).reshape(sectors, block, LANES)


def lat_kernel(rows_ref, near_ref, own_ref, far_ref, reach_ref, blend_ref,
               out_ref, polar_weight_ref, mix_ref, pick_ref):
    shells, row_count, col_count = own_ref.shape
    frame_rows = row_count + 2 * LMAX
    polar = pick_ref.shape[0]
    zone = lax.axis_index("zone")
    cap = jnp.where(zone < 8, 0, polar)
    lane = lanes_of(1)
    for p in range(polar):
        pick_ref[p : p + 1, :] = (lane == rows_ref[cap + p] - zone * row_count + LMAX).astype(F32)
    pick = pick_ref[...]
    zones = lax.axis_size("zone")
    reach = reach_ref[...]
    column = lax.broadcasted_iota(jnp.int32, (row_count, frame_rows), 1)
    away = column - LMAX - lax.broadcasted_iota(jnp.int32, (row_count, frame_rows), 0)
    source = zone * row_count - LMAX + column
    valid = (jnp.abs(away) <= reach) & (source >= 0) & (source < zones * row_count)
    reach_f = reach.astype(F32)
    away_f = away.astype(F32)
    weights = jnp.where(valid, jnp.exp(-(4.5 / (reach_f * reach_f)) * (away_f * away_f)), 0.0)
    weight = (weights / jnp.sum(weights, axis=1, keepdims=True)).astype(BF16)
    length = mix_ref.shape[0]
    group = length // shells
    spread = (
        lax.broadcasted_iota(jnp.int32, (length, shells), 0) // group
        == lax.broadcasted_iota(jnp.int32, (length, shells), 1)
    ).astype(F32).astype(BF16)
    tall = jnp.dot(spread, blend_ref[...], preferred_element_type=F32).astype(BF16)
    full = lax.dot_general(tall, spread, (((1,), (1,)), ((), ())), preferred_element_type=F32)
    same = (
        lax.broadcasted_iota(jnp.int32, (length, length), 0) % group
        == lax.broadcasted_iota(jnp.int32, (length, length), 1) % group
    )
    mix_ref[...] = jnp.where(same, full, 0.0).astype(BF16)
    polar_weight_ref[...] = lax.dot_general(
        weight, pick.astype(BF16), (((1,), (1,)), ((), ())), preferred_element_type=F32
    ).astype(BF16)
    rest = weight.astype(F32) * (1.0 - jnp.sum(pick, axis=0, keepdims=True))
    wide = lanes_of(row_count)
    turned = jnp.where(
        wide < LMAX,
        pltpu.roll(rest, LMAX, 1),
        jnp.where(wide < frame_rows - LMAX, rest, pltpu.roll(rest, frame_rows - LMAX, 1)),
    )
    rest = jnp.where(lax.rem(zone, 2) == 0, turned, rest).astype(BF16)

    def some_shells(block, carry):
        for u in range(4):
            s = block * 4 + u
            values = jnp.concatenate([near_ref[s], own_ref[s], far_ref[s]], axis=0)
            out_ref[s] = jnp.dot(rest, values, preferred_element_type=F32)
        return carry

    lax.fori_loop(0, shells // 4, some_shells, 0)


def own_part():
    return jnp.where(from_pole(lax.axis_index("zone")) == 0, 0, 1)


def add_polar(part, source_refs, weight_ref, lat_ref, polar_ref, sum_ref, sem, put):
    holders = source_refs[0].shape[0]
    tiles = polar_ref.shape[0]
    polar = holders * SETS
    pitch = polar + 1
    fetch = pltpu.make_async_copy(lat_ref.at[pl.ds(part * PART, PART)], sum_ref, sem)
    fetch.start()
    for r in range(SETS):
        for k in range(holders):
            for t in range(tiles):
                polar_ref[t, pl.ds(r * holders + k, PART, stride=pitch), :] = source_refs[r][
                    k, t * PART : (t + 1) * PART, :
                ].astype(F32)
    weight = weight_ref[...]
    fetch.wait()

    def some_shells(index, carry):
        for u in range(4):
            s = index * 4 + u
            values = jnp.concatenate(
                [polar_ref[t, pl.ds(s * pitch, polar), :].astype(BF16) for t in range(tiles)], axis=1
            )
            put(s, sum_ref[s] + jnp.dot(weight, values, preferred_element_type=F32))
        return carry

    lax.fori_loop(0, PART // 4, some_shells, 0)


def own_kernel(stay_ref, right_ref, left_ref, weight_ref, lat_ref, out_ref, polar_ref, sum_ref, sem):
    def put(s, values):
        out_ref[s] = values.astype(BF16)

    add_polar(own_part(), (stay_ref, right_ref, left_ref), weight_ref, lat_ref, polar_ref, sum_ref, sem, put)


def final_kernel(stay_ref, right_ref, left_ref, own_ref, weight_ref, mix_ref, lat_ref, out_ref,
                 polar_ref, sum_ref, full_ref, stage_ref, sem, sems):
    shells, row_count, col_count = lat_ref.shape
    part = own_part()

    def put(s, values):
        full_ref[(1 - part) * PART + s] = values

    add_polar(1 - part, (stay_ref, right_ref, left_ref), weight_ref, lat_ref, polar_ref, sum_ref, sem, put)
    for s in range(PART):
        full_ref[part * PART + s] = own_ref[s].astype(F32)
    group = mix_ref.shape[0] // shells
    mix = mix_ref[...]
    stores = []
    for g in range(row_count // (2 * group)):
        mixed = []
        for e in range(2):
            first = (2 * g + e) * group
            values = full_ref[:, first : first + group, :].reshape(shells * group, col_count).astype(BF16)
            mixed.append(jnp.dot(mix, values, preferred_element_type=F32).reshape(shells, group, col_count))
        rows = pl.ds(2 * g * group, 2 * group)
        stage_ref[:, rows, :] = jnp.concatenate(mixed, axis=1).astype(BF16)
        stores.append(pltpu.make_async_copy(stage_ref.at[:, rows], out_ref.at[:, rows], sems.at[g]))
        stores[-1].start()
    for store in stores:
        store.wait()


def call(kernel, name, out_shape, scalars, arrays, scratch, flops=0, moved=0, direct=(), far=False, mib=16):
    smem = pl.BlockSpec(memory_space=pltpu.SMEM)
    vmem = pl.BlockSpec(memory_space=pltpu.VMEM)
    anywhere = pl.BlockSpec(memory_space=pl.ANY)
    many = isinstance(out_shape, tuple)
    return pl.pallas_call(
        kernel,
        out_shape=out_shape,
        in_specs=[smem] * len(scalars) + [vmem] * len(arrays) + [anywhere] * len(direct),
        out_specs=(vmem,) * len(out_shape) if many else anywhere if far else vmem,
        scratch_shapes=scratch,
        compiler_params=pltpu.CompilerParams(vmem_limit_bytes=mib << 20),
        cost_estimate=pl.CostEstimate(flops=flops, bytes_accessed=moved, transcendentals=0),
        name=name,
    )(*scalars, *arrays, *direct)


struct = jax.ShapeDtypeStruct


def pack_first(polar_rows, kernel, sectors):
    shells, row_count, col_count = kernel.shape
    tiles = col_count // LANES
    edge = struct((shells * row_count // 2, LANES), BF16)
    return call(
        first_kernel,
        "pack_half_of_shells_and_edges",
        (struct((SETS, sectors, tiles * PART, LANES), BF16), edge, edge),
        [],
        [],
        [
            pltpu.VMEM((tiles, PART * PITCH, LANES), F32),
            pltpu.VMEM(kernel.shape, BF16),
            pltpu.SMEM(polar_rows.shape, jnp.int32),
            pltpu.SemaphoreType.DMA((3,)),
        ],
        moved=4 << 20,
        direct=[kernel, polar_rows],
        mib=52,
    )


def pack_second(polar_rows, kernel, given):
    _, row_count, col_count = kernel.shape
    return call(
        second_kernel,
        "pack_other_half_or_take_given",
        (struct(given.shape[1:], BF16),) * SETS,
        [polar_rows],
        [kernel],
        [pltpu.VMEM((col_count // LANES, PART * PITCH, LANES), F32), pltpu.SemaphoreType.DMA((SETS,))],
        moved=4 << 20,
        direct=[given],
    )


def smooth_lon(lon_halo, kernel, near, far, *after):
    shells, row_count, col_count = kernel.shape
    tiles = col_count // LANES
    rows = pltpu.VMEM((row_count, LANES), F32)
    return call(
        lon_kernel,
        "smooth_along_longitude",
        (
            struct((shells, row_count, col_count), BF16),
            struct((shells, LMAX, col_count), BF16),
            struct((shells, LMAX, col_count), BF16),
        ),
        [lon_halo],
        [kernel, near, far],
        [
            pltpu.VMEM((tiles + 1, shells * PITCH, LANES), F32),
            pltpu.VMEM((tiles, shells * PITCH, LANES), F32),
            rows,
            rows,
            rows,
        ],
        flops=1 << 36,
        moved=16 << 20,
        direct=after,
        mib=20,
    )


def hold(table, circles, after):
    sectors, block, _ = circles.shape
    return call(
        hold_kernel,
        "smooth_and_turn_polar_circles",
        struct(circles.shape, BF16),
        [table],
        [circles],
        [pltpu.VMEM((2 * sectors * block + 2 * PART, LANES), BF16)],
        flops=1 << 36,
        moved=4 << 20,
        direct=[after],
    )


def smooth_lat(polar_rows, near, own, far, reach, blend):
    shells, row_count, _ = own.shape
    frame_rows = row_count + 2 * LMAX
    polar = polar_rows.shape[0] // 2
    return call(
        lat_kernel,
        "smooth_along_latitude",
        (
            struct(own.shape, F32),
            struct((row_count, polar), BF16),
            struct((shells * 8, shells * 8), BF16),
        ),
        [polar_rows],
        [near, own, far, reach, blend],
        [pltpu.VMEM((polar, frame_rows), F32)],
        flops=1 << 36,
        moved=8 << 20,
    )


def add_own(lat, mine, polar_weight):
    shells, row_count, col_count = lat.shape
    half = (PART, row_count, col_count)
    return call(
        own_kernel,
        "add_polar_rows_of_own_shells",
        struct(half, BF16),
        [],
        [*mine, polar_weight],
        [
            pltpu.VMEM((col_count // LANES, PART * (polar_weight.shape[1] + 1), LANES), F32),
            pltpu.VMEM(half, F32),
            pltpu.SemaphoreType.DMA,
        ],
        flops=1 << 30,
        moved=4 << 20,
        direct=[lat],
        mib=50,
    )


def finish(lat, other, own, polar_weight, mix):
    shells, row_count, col_count = lat.shape
    return call(
        final_kernel,
        "add_polar_rows_and_blend",
        struct(lat.shape, BF16),
        [],
        [*other, own, polar_weight, mix],
        [
            pltpu.VMEM((col_count // LANES, PART * (polar_weight.shape[1] + 1), LANES), F32),
            pltpu.VMEM((PART, row_count, col_count), F32),
            pltpu.VMEM(lat.shape, F32),
            pltpu.VMEM(lat.shape, BF16),
            pltpu.SemaphoreType.DMA,
            pltpu.SemaphoreType.DMA((4,)),
        ],
        flops=1 << 31,
        moved=8 << 20,
        far=True,
        direct=[lat],
        mib=50,
    )


def per_device(kernel, lon_halo, lat_reach, polar_rows, polar_shift, blend):
    shells, row_count, col_count = kernel.shape
    sectors = lax.axis_size("sector")
    zones = lax.axis_size("zone")
    last = zones - 1
    packed, near, far = pack_first(polar_rows, kernel, sectors)
    given = lax.ppermute(packed, "zone", [(0, 1), (last, last - 1)])
    far = lax.ppermute(far, "sector", [(i, (i + 1 if i % 2 else i - 1) % sectors) for i in range(sectors)])
    near = lax.ppermute(near, "sector", [(i, i ^ 1) for i in range(sectors)])
    stay, right, left = pack_second(polar_rows, kernel, given)
    to_right = [(0, 2), (1, 3), (last, last - 2), (last - 1, last - 3)]
    to_left = [(0, 6), (1, 7), (last, last - 6), (last - 1, last - 7)]
    right = lax.ppermute(right, "zone", to_right)
    left = lax.ppermute(left, "zone", to_left)
    away = from_pole(lax.axis_index("zone"))
    parts = jnp.where((away == 2) | (away == 3), right, jnp.where((away == 6) | (away == 7), left, stay))
    circles = lax.all_to_all(parts, "sector", 0, 0, tiled=True)
    table = jnp.concatenate([polar_rows, polar_shift, lon_halo])
    reach = lat_reach[:, None]
    lon_smooth, near_rows, far_rows = smooth_lon(lon_halo, kernel, near, far, parts, table, reach)
    turned = hold(table, circles, far_rows)
    far_rows = lax.ppermute(
        far_rows, "zone", [(i, i + 1 if i % 2 else i - 1) for i in range(1, zones - 1)]
    )
    near_rows = lax.ppermute(near_rows, "zone", [(i, i ^ 1) for i in range(zones)])
    mine = lax.all_to_all(turned, "sector", 0, 0, tiled=True)
    lat, polar_weight, mix = smooth_lat(
        polar_rows, near_rows, lon_smooth, far_rows, reach, blend
    )
    mine, lat = lax.optimization_barrier((mine, lat))
    right = lax.ppermute(mine, "zone", [(j, i) for i, j in to_right])
    left = lax.ppermute(mine, "zone", [(j, i) for i, j in to_left])
    mine = (mine, right, left)
    swap = [(0, 1), (1, 0), (last, last - 1), (last - 1, last)]
    other = tuple(lax.ppermute(part, "zone", swap) for part in mine)
    own = add_own(lat, mine, polar_weight)
    return finish(lat, other, own, polar_weight, mix)


def solution(mesh):
    in_specs = (P(None, "zone", "sector"), P(), P("zone"), P(), P(), P())
    out_specs = P(None, "zone", "sector")
    return jax.shard_map(
        per_device, mesh=mesh, in_specs=in_specs, out_specs=out_specs, check_vma=False
    )
```

```python
import jax
import jax.numpy as jnp
from jax import lax
from jax.experimental import pallas as pl
from jax.experimental.pallas import tpu as pltpu
from jax.sharding import PartitionSpec as P

HMAX = 48
LMAX = 32
LANES = 128
PART = 16
UNROLL = 8
PITCH = 65
F32 = jnp.float32
BF16 = jnp.bfloat16


def lanes_of(rows):
    return lax.broadcasted_iota(jnp.int32, (rows, LANES), 1)


def write_edges(x_ref, near_ref, far_ref):
    shells, row_count, col_count = x_ref.shape
    half = shells // 2
    size = half * row_count
    lane = lanes_of(size)

    def part(column, shell):
        return x_ref[shell : shell + half, :, column : column + LANES].reshape(size, LANES).astype(F32)

    last = col_count - LANES
    even = lax.rem(lax.axis_index("sector"), 2) == 0
    low = jnp.where(lane < HMAX, part(0, 0), pltpu.roll(part(0, half), HMAX, 1))
    high = jnp.where(lane < HMAX, pltpu.roll(part(last, 0), HMAX, 1), pltpu.roll(part(last, half), 2 * HMAX, 1))
    near_ref[...] = jnp.where(even, high, low).astype(BF16)
    far_ref[...] = jnp.where(even, low, high).astype(BF16)


def write_polar(half, rows_ref, x_ref, send_ref, wide_ref):
    _, row_count, col_count = x_ref.shape
    tiles = col_count // LANES
    zone = lax.axis_index("zone")
    for t in range(tiles):
        for s in range(PART):
            wide_ref[t, s * PITCH : s * PITCH + row_count, :] = x_ref[
                half * PART + s, :, t * LANES : (t + 1) * LANES
            ].astype(F32)
    holders, held = send_ref.shape[0], send_ref.shape[1]
    cap = jnp.where(zone < 8, 0, holders * held)
    for k in range(holders):
        for r in range(held):
            row = jnp.clip(rows_ref[cap + k * held + r] - zone * row_count, 0, row_count - 1)
            for t in range(tiles):
                values = wide_ref[t, pl.ds(row, PART, stride=PITCH), :]
                send_ref[k, r, t * PART : (t + 1) * PART, :] = values.astype(BF16)


def first_kernel(x_ref, far_rows_ref, send_ref, near_ref, far_ref, kept_ref,
                 wide_ref, held_ref, stage_ref, rows_ref, sems):
    fetch = pltpu.make_async_copy(far_rows_ref, rows_ref, sems.at[2])
    fetch.start()
    copies = []
    for half in (1, 0):
        shells = pl.ds(half * PART, PART)
        copies.append(pltpu.make_async_copy(x_ref.at[shells], held_ref.at[shells], sems.at[half]))
        copies[-1].start()
    fetch.wait()
    copies[0].wait()
    write_polar(1, rows_ref, held_ref, send_ref, wide_ref)
    copies[1].wait()
    write_polar(0, rows_ref, held_ref, stage_ref, wide_ref)
    store = pltpu.make_async_copy(stage_ref, kept_ref, sems.at[3])
    store.start()
    write_edges(held_ref, near_ref, far_ref)
    store.wait()


def second_kernel(given_ref, kept_ref, out_ref, sem):
    zone = lax.axis_index("zone")

    @pl.when((zone == 1) | (zone == lax.axis_size("zone") - 2))
    def _():
        copy = pltpu.make_async_copy(given_ref, out_ref, sem)
        copy.start()
        copy.wait()


def band_terms(half_f):
    rate = 4.5 / (half_f * half_f)
    tap = (lanes_of(half_f.shape[0]) - HMAX).astype(F32)
    terms = jnp.where(jnp.abs(tap) <= half_f, jnp.exp(-rate * (tap * tap)), 0.0)
    return rate, jnp.broadcast_to(1.0 / jnp.sum(terms, axis=1, keepdims=True), half_f.shape)


def lon_kernel(halo_ref, x_ref, near_ref, far_ref,
               out_ref, near_rows_ref, far_rows_ref, wide_ref, done_ref, half_ref, rate_ref, scale_ref):
    shells, row_count, col_count = x_ref.shape
    total = shells * row_count
    size = total // 2
    tiles = col_count // LANES
    zone = lax.axis_index("zone")
    for i in range(row_count):
        half_ref[i : i + 1, :] = jnp.full((1, LANES), halo_ref[zone * row_count + i], jnp.int32).astype(F32)
    rate_ref[...], scale_ref[...] = band_terms(half_ref[...])
    lane = lanes_of(size)
    even = lax.rem(lax.axis_index("sector"), 2) == 0
    near = near_ref[...].astype(F32)
    far = far_ref[...].astype(F32)
    before = jnp.where(even, far, near)
    after = jnp.where(even, near, far)

    def keep(t, part, values):
        for s in range(shells // 2):
            first = (part * (shells // 2) + s) * PITCH
            wide_ref[t, first : first + row_count, :] = values[s * row_count : (s + 1) * row_count]

    for part in range(2):
        shell = slice(part * (shells // 2), (part + 1) * (shells // 2))
        previous = before if part == 0 else pltpu.roll(before, LANES - HMAX, 1)
        for t in range(tiles):
            turned = pltpu.roll(
                x_ref[shell, :, t * LANES : (t + 1) * LANES].reshape(size, LANES).astype(F32), HMAX, 1
            )
            keep(t, part, jnp.where(lane < HMAX, previous, turned))
            previous = turned
        edge = pltpu.roll(after, HMAX, 1) if part == 0 else after
        keep(tiles, part, jnp.where(lane < HMAX, previous, jnp.where(lane < 2 * HMAX, edge, 0.0)))
    depth = 2 * LANES
    offset = (lanes_of(depth) - lax.broadcasted_iota(jnp.int32, (depth, LANES), 0) + HMAX).astype(F32)
    square = offset * offset
    distance = jnp.abs(offset)

    def some_rows(block, carry):
        for u in range(UNROLL):
            i = block * UNROLL + u
            line = pl.ds(i, 1)
            band = jnp.where(distance <= half_ref[line, :], jnp.exp(-rate_ref[line, :] * square), 0.0)
            band = (band * scale_ref[line, :]).astype(BF16)
            values = [wide_ref[t, pl.ds(i, shells, stride=PITCH), :].astype(BF16) for t in range(tiles + 1)]
            stacked = jnp.concatenate(
                [jnp.concatenate(values[:tiles], axis=0), jnp.concatenate(values[1:], axis=0)], axis=1
            )
            result = jnp.dot(stacked, band, preferred_element_type=F32)
            for t in range(tiles):
                done_ref[t, pl.ds(i, shells, stride=PITCH), :] = result[t * shells : (t + 1) * shells]
        return carry

    lax.fori_loop(0, row_count // UNROLL, some_rows, 0)
    for t in range(tiles):
        for s in range(shells):
            out_ref[s, :, t * LANES : (t + 1) * LANES] = done_ref[t, s * PITCH : s * PITCH + row_count, :].astype(BF16)
    odd = lax.rem(zone, 2)
    last = row_count - LMAX
    near_rows_ref[...] = out_ref[:, pl.ds(pl.multiple_of((1 - odd) * last, LMAX), LMAX), :]
    far_rows_ref[...] = out_ref[:, pl.ds(pl.multiple_of(odd * last, LMAX), LMAX), :]


def hold_kernel(table_ref, x_ref, after_ref, out_ref, circle_ref):
    sectors, held, block, _ = x_ref.shape
    zone, sector = lax.axis_index("zone"), lax.axis_index("sector")
    polar = 2 * sectors * held
    cap = jnp.where(zone < 8, 0, sectors * held)
    length = sectors * block
    full_lon = length // PART * LANES
    depth = 3 * LANES
    for r in range(held):
        for copy in range(2):
            circle_ref[r, copy * length : (copy + 1) * length, :] = x_ref[:, r].reshape(length, LANES)
        circle_ref[r, 2 * length : 2 * length + 2 * PART, :] = circle_ref[r, 0 : 2 * PART, :]
    for r in range(held):
        entry = cap + sector * held + r
        half_f = jnp.full((1, LANES), table_ref[2 * polar + table_ref[entry]], jnp.int32).astype(F32)
        rate, scale = band_terms(half_f)
        start = lax.rem(2 * full_lon - table_ref[polar + entry] - HMAX, full_lon)
        first = start // LANES
        rest = start - first * LANES
        offset = (
            lanes_of(depth) - lax.broadcasted_iota(jnp.int32, (depth, LANES), 0) + (rest + HMAX)
        ).astype(F32)
        band = jnp.where(jnp.abs(offset) <= half_f, jnp.exp(-rate * (offset * offset)), 0.0) * scale
        values = jnp.concatenate(
            [circle_ref[r, pl.ds(pl.multiple_of((first + u) * PART, PART), length), :] for u in range(3)], axis=1
        )
        result = jnp.dot(values, band.astype(BF16), preferred_element_type=F32)
        out_ref[:, r] = result.astype(BF16).reshape(sectors, block, LANES)


def lat_kernel(rows_ref, near_ref, own_ref, far_ref, reach_ref, blend_ref,
               out_ref, polar_weight_ref, mix_ref, pick_ref):
    shells, row_count, col_count = own_ref.shape
    frame_rows = row_count + 2 * LMAX
    polar = pick_ref.shape[0]
    zone = lax.axis_index("zone")
    cap = jnp.where(zone < 8, 0, polar)
    lane = lanes_of(1)
    for p in range(polar):
        pick_ref[p : p + 1, :] = (lane == rows_ref[cap + p] - zone * row_count + LMAX).astype(F32)
    pick = pick_ref[...]
    zones = lax.axis_size("zone")
    reach = reach_ref[...]
    column = lax.broadcasted_iota(jnp.int32, (row_count, frame_rows), 1)
    away = column - LMAX - lax.broadcasted_iota(jnp.int32, (row_count, frame_rows), 0)
    source = zone * row_count - LMAX + column
    valid = (jnp.abs(away) <= reach) & (source >= 0) & (source < zones * row_count)
    reach_f = reach.astype(F32)
    away_f = away.astype(F32)
    weights = jnp.where(valid, jnp.exp(-(4.5 / (reach_f * reach_f)) * (away_f * away_f)), 0.0)
    weight = (weights / jnp.sum(weights, axis=1, keepdims=True)).astype(BF16)
    length = mix_ref.shape[0]
    group = length // shells
    spread = (
        lax.broadcasted_iota(jnp.int32, (length, shells), 0) // group
        == lax.broadcasted_iota(jnp.int32, (length, shells), 1)
    ).astype(F32).astype(BF16)
    tall = jnp.dot(spread, blend_ref[...], preferred_element_type=F32).astype(BF16)
    full = lax.dot_general(tall, spread, (((1,), (1,)), ((), ())), preferred_element_type=F32)
    same = (
        lax.broadcasted_iota(jnp.int32, (length, length), 0) % group
        == lax.broadcasted_iota(jnp.int32, (length, length), 1) % group
    )
    mix_ref[...] = jnp.where(same, full, 0.0).astype(BF16)
    polar_weight_ref[...] = lax.dot_general(
        weight, pick.astype(BF16), (((1,), (1,)), ((), ())), preferred_element_type=F32
    ).astype(BF16)
    rest = weight.astype(F32) * (1.0 - jnp.sum(pick, axis=0, keepdims=True))
    wide = lanes_of(row_count)
    turned = jnp.where(
        wide < LMAX,
        pltpu.roll(rest, LMAX, 1),
        jnp.where(wide < frame_rows - LMAX, rest, pltpu.roll(rest, frame_rows - LMAX, 1)),
    )
    rest = jnp.where(lax.rem(zone, 2) == 0, turned, rest).astype(BF16)

    def some_shells(block, carry):
        for u in range(4):
            s = block * 4 + u
            values = jnp.concatenate([near_ref[s], own_ref[s], far_ref[s]], axis=0)
            out_ref[s] = jnp.dot(rest, values, preferred_element_type=F32)
        return carry

    lax.fori_loop(0, shells // 4, some_shells, 0)


def own_part():
    zone = lax.axis_index("zone")
    return jnp.where((zone == 0) | (zone == lax.axis_size("zone") - 1), 0, 1)


def add_polar(part, source_ref, weight_ref, lat_ref, polar_ref, sum_ref, sem, put):
    holders, held = source_ref.shape[:2]
    tiles = polar_ref.shape[0]
    polar = holders * held
    pitch = polar + 1
    fetch = pltpu.make_async_copy(lat_ref.at[pl.ds(part * PART, PART)], sum_ref, sem)
    fetch.start()
    for k in range(holders):
        for r in range(held):
            for t in range(tiles):
                polar_ref[t, pl.ds(k * held + r, PART, stride=pitch), :] = source_ref[
                    k, r, t * PART : (t + 1) * PART, :
                ].astype(F32)
    weight = weight_ref[...]
    fetch.wait()

    def some_shells(index, carry):
        for u in range(4):
            s = index * 4 + u
            values = jnp.concatenate(
                [polar_ref[t, pl.ds(s * pitch, polar), :].astype(BF16) for t in range(tiles)], axis=1
            )
            put(s, sum_ref[s] + jnp.dot(weight, values, preferred_element_type=F32))
        return carry

    lax.fori_loop(0, PART // 4, some_shells, 0)


def own_kernel(mine_ref, weight_ref, lat_ref, out_ref, polar_ref, sum_ref, sem):
    def put(s, values):
        out_ref[s] = values.astype(BF16)

    add_polar(own_part(), mine_ref, weight_ref, lat_ref, polar_ref, sum_ref, sem, put)


def final_kernel(other_ref, own_ref, weight_ref, mix_ref, lat_ref, out_ref,
                 polar_ref, sum_ref, full_ref, stage_ref, sem, sems):
    shells, row_count, col_count = lat_ref.shape
    part = own_part()

    def put(s, values):
        full_ref[(1 - part) * PART + s] = values

    add_polar(1 - part, other_ref, weight_ref, lat_ref, polar_ref, sum_ref, sem, put)
    for s in range(PART):
        full_ref[part * PART + s] = own_ref[s].astype(F32)
    group = mix_ref.shape[0] // shells
    mix = mix_ref[...]
    stores = []
    for g in range(row_count // (2 * group)):
        mixed = []
        for e in range(2):
            first = (2 * g + e) * group
            values = full_ref[:, first : first + group, :].reshape(shells * group, col_count).astype(BF16)
            mixed.append(jnp.dot(mix, values, preferred_element_type=F32).reshape(shells, group, col_count))
        rows = pl.ds(2 * g * group, 2 * group)
        stage_ref[:, rows, :] = jnp.concatenate(mixed, axis=1).astype(BF16)
        stores.append(pltpu.make_async_copy(stage_ref.at[:, rows], out_ref.at[:, rows], sems.at[g]))
        stores[-1].start()
    for store in stores:
        store.wait()


def call(kernel, name, out_shape, scalars, arrays, scratch, flops=0, moved=0, direct=(), far=False, mib=16):
    smem = pl.BlockSpec(memory_space=pltpu.SMEM)
    vmem = pl.BlockSpec(memory_space=pltpu.VMEM)
    anywhere = pl.BlockSpec(memory_space=pl.ANY)
    many = isinstance(out_shape, tuple)
    return pl.pallas_call(
        kernel,
        out_shape=out_shape,
        in_specs=[smem] * len(scalars) + [vmem] * len(arrays) + [anywhere] * len(direct),
        out_specs=(vmem,) * len(out_shape) if many else anywhere if far else vmem,
        scratch_shapes=scratch,
        compiler_params=pltpu.CompilerParams(vmem_limit_bytes=mib << 20),
        cost_estimate=pl.CostEstimate(flops=flops, bytes_accessed=moved, transcendentals=0),
        name=name,
    )(*scalars, *arrays, *direct)


struct = jax.ShapeDtypeStruct


def pack(polar_rows, kernel, sectors):
    shells, row_count, col_count = kernel.shape
    tiles = col_count // LANES
    held = polar_rows.shape[0] // 2 // sectors
    edge = struct((shells * row_count // 2, LANES), BF16)
    parts = struct((sectors, held, tiles * PART, LANES), BF16)
    vmem = pl.BlockSpec(memory_space=pltpu.VMEM)
    anywhere = pl.BlockSpec(memory_space=pl.ANY)
    return pl.pallas_call(
        first_kernel,
        out_shape=(parts, edge, edge, parts),
        in_specs=[anywhere, anywhere],
        out_specs=(vmem, vmem, vmem, anywhere),
        scratch_shapes=[
            pltpu.VMEM((tiles, PART * PITCH, LANES), F32),
            pltpu.VMEM(kernel.shape, BF16),
            pltpu.VMEM(parts.shape, BF16),
            pltpu.SMEM(polar_rows.shape, jnp.int32),
            pltpu.SemaphoreType.DMA((4,)),
        ],
        compiler_params=pltpu.CompilerParams(vmem_limit_bytes=52 << 20),
        cost_estimate=pl.CostEstimate(flops=0, bytes_accessed=4 << 20, transcendentals=0),
        name="pack_polar_rows_and_edges",
    )(kernel, polar_rows)


def take_given(given, kept):
    anywhere = pl.BlockSpec(memory_space=pl.ANY)
    return pl.pallas_call(
        second_kernel,
        out_shape=struct(kept.shape, BF16),
        in_specs=[anywhere, anywhere],
        out_specs=anywhere,
        scratch_shapes=[pltpu.SemaphoreType.DMA],
        input_output_aliases={1: 0},
        compiler_params=pltpu.CompilerParams(vmem_limit_bytes=4 << 20),
        name="take_given",
    )(given, kept)


def smooth_lon(lon_halo, kernel, near, far):
    shells, row_count, col_count = kernel.shape
    tiles = col_count // LANES
    rows = pltpu.VMEM((row_count, LANES), F32)
    return call(
        lon_kernel,
        "smooth_along_longitude",
        (
            struct((shells, row_count, col_count), BF16),
            struct((shells, LMAX, col_count), BF16),
            struct((shells, LMAX, col_count), BF16),
        ),
        [lon_halo],
        [kernel, near, far],
        [
            pltpu.VMEM((tiles + 1, shells * PITCH, LANES), F32),
            pltpu.VMEM((tiles, shells * PITCH, LANES), F32),
            rows,
            rows,
            rows,
        ],
        flops=1 << 36,
        moved=16 << 20,
        mib=20,
    )


def hold(table, circles, after):
    sectors, held, block, _ = circles.shape
    return call(
        hold_kernel,
        "smooth_and_turn_polar_circles",
        struct(circles.shape, BF16),
        [table],
        [circles],
        [pltpu.VMEM((held, 2 * sectors * block + 2 * PART, LANES), BF16)],
        flops=1 << 30,
        moved=4 << 20,
        direct=[after],
    )


def smooth_lat(polar_rows, near, own, far, reach, blend):
    shells, row_count, _ = own.shape
    frame_rows = row_count + 2 * LMAX
    polar = polar_rows.shape[0] // 2
    return call(
        lat_kernel,
        "smooth_along_latitude",
        (
            struct(own.shape, F32),
            struct((row_count, polar), BF16),
            struct((shells * 8, shells * 8), BF16),
        ),
        [polar_rows],
        [near, own, far, reach, blend],
        [pltpu.VMEM((polar, frame_rows), F32)],
        flops=1 << 36,
        moved=8 << 20,
    )


def add_own(lat, mine, polar_weight):
    shells, row_count, col_count = lat.shape
    half = (PART, row_count, col_count)
    return call(
        own_kernel,
        "add_polar_rows_of_own_shells",
        struct(half, BF16),
        [],
        [mine, polar_weight],
        [
            pltpu.VMEM((col_count // LANES, PART * (polar_weight.shape[1] + 1), LANES), F32),
            pltpu.VMEM(half, F32),
            pltpu.SemaphoreType.DMA,
        ],
        flops=1 << 30,
        moved=4 << 20,
        direct=[lat],
        mib=50,
    )


def finish(lat, other, own, polar_weight, mix):
    shells, row_count, col_count = lat.shape
    return call(
        final_kernel,
        "add_polar_rows_and_blend",
        struct(lat.shape, BF16),
        [],
        [other, own, polar_weight, mix],
        [
            pltpu.VMEM((col_count // LANES, PART * (polar_weight.shape[1] + 1), LANES), F32),
            pltpu.VMEM((PART, row_count, col_count), F32),
            pltpu.VMEM(lat.shape, F32),
            pltpu.VMEM(lat.shape, BF16),
            pltpu.SemaphoreType.DMA,
            pltpu.SemaphoreType.DMA((4,)),
        ],
        flops=1 << 31,
        moved=8 << 20,
        far=True,
        direct=[lat],
        mib=50,
    )


def per_device(kernel, lon_halo, lat_reach, polar_rows, polar_shift, blend):
    shells, row_count, col_count = kernel.shape
    sectors = lax.axis_size("sector")
    zones = lax.axis_size("zone")
    last = zones - 1
    packed, near, far, kept = pack(polar_rows, kernel, sectors)
    given = lax.ppermute(packed, "zone", [(0, 1), (last, last - 1)])
    far = lax.ppermute(far, "sector", [(i, (i + 1 if i % 2 else i - 1) % sectors) for i in range(sectors)])
    near = lax.ppermute(near, "sector", [(i, i ^ 1) for i in range(sectors)])
    parts = take_given(given, kept)
    circles = lax.all_to_all(parts, "sector", 0, 0, tiled=True)
    lon_smooth, near_rows, far_rows = smooth_lon(lon_halo, kernel, near, far)
    turned = hold(jnp.concatenate([polar_rows, polar_shift, lon_halo]), circles, far_rows)
    far_rows = lax.ppermute(
        far_rows, "zone", [(i, i + 1 if i % 2 else i - 1) for i in range(1, zones - 1)]
    )
    near_rows = lax.ppermute(near_rows, "zone", [(i, i ^ 1) for i in range(zones)])
    mine = lax.all_to_all(turned, "sector", 0, 0, tiled=True)
    lat, polar_weight, mix = smooth_lat(
        polar_rows, near_rows, lon_smooth, far_rows, lat_reach[:, None], blend
    )
    mine, lat = lax.optimization_barrier((mine, lat))
    other = lax.ppermute(mine, "zone", [(0, 1), (1, 0), (last, last - 1), (last - 1, last)])
    own = add_own(lat, mine, polar_weight)
    return finish(lat, other, own, polar_weight, mix)


def solution(mesh):
    in_specs = (P(None, "zone", "sector"), P(), P("zone"), P(), P(), P())
    out_specs = P(None, "zone", "sector")
    return jax.shard_map(
        per_device, mesh=mesh, in_specs=in_specs, out_specs=out_specs, check_vma=False
    )
```

```python
import jax
import jax.numpy as jnp
from jax import lax
from jax.experimental import pallas as pl
from jax.experimental.pallas import tpu as pltpu
from jax.sharding import PartitionSpec as P

HMAX = 48
LMAX = 32
LANES = 128
PART = 16
PIECES = 8
UNROLL = 8
PITCH = 65
F32 = jnp.float32
BF16 = jnp.bfloat16


def lanes_of(rows):
    return lax.broadcasted_iota(jnp.int32, (rows, LANES), 1)


def places(tile):
    first = tile * LANES // HMAX
    last = ((tile + 1) * LANES - 1) // HMAX
    return [(piece, piece * HMAX - tile * LANES) for piece in range(first, last + 1)]


def write_edges(x_ref, near_ref, far_ref):
    shells, row_count, col_count = x_ref.shape
    some = shells // PIECES
    size = some * row_count
    lane = lanes_of(size)
    last = col_count - LANES
    even = lax.rem(lax.axis_index("sector"), 2) == 0

    def packed(column, turn, tile):
        result = None
        for piece, place in places(tile):
            values = x_ref[piece * some : (piece + 1) * some, :, column : column + LANES].reshape(size, LANES)
            shift = (place + turn) % LANES
            values = values.astype(F32)
            values = pltpu.roll(values, shift, 1) if shift else values
            result = values if result is None else jnp.where(lane < place, result, values)
        return result

    for tile in range(PIECES * HMAX // LANES):
        low = packed(0, 0, tile)
        high = packed(last, HMAX, tile)
        rows = slice(tile * size, (tile + 1) * size)
        near_ref[rows, :] = jnp.where(even, high, low).astype(BF16)
        far_ref[rows, :] = jnp.where(even, low, high).astype(BF16)


def write_polar(half, rows_ref, x_ref, send_ref, wide_ref):
    _, row_count, col_count = x_ref.shape
    tiles = col_count // LANES
    zone = lax.axis_index("zone")
    for t in range(tiles):
        for s in range(PART):
            wide_ref[t, s * PITCH : s * PITCH + row_count, :] = x_ref[
                half * PART + s, :, t * LANES : (t + 1) * LANES
            ].astype(F32)
    holders, held = send_ref.shape[0], send_ref.shape[1]
    cap = jnp.where(zone < 8, 0, holders * held)
    for k in range(holders):
        for r in range(held):
            row = jnp.clip(rows_ref[cap + k * held + r] - zone * row_count, 0, row_count - 1)
            for t in range(tiles):
                values = wide_ref[t, pl.ds(row, PART, stride=PITCH), :]
                send_ref[k, r, t * PART : (t + 1) * PART, :] = values.astype(BF16)


def first_kernel(x_ref, far_rows_ref, send_ref, near_ref, far_ref, kept_ref,
                 wide_ref, held_ref, stage_ref, rows_ref, sems):
    fetch = pltpu.make_async_copy(far_rows_ref, rows_ref, sems.at[2])
    fetch.start()
    copies = []
    for half in (1, 0):
        shells = pl.ds(half * PART, PART)
        copies.append(pltpu.make_async_copy(x_ref.at[shells], held_ref.at[shells], sems.at[half]))
        copies[-1].start()
    fetch.wait()
    copies[0].wait()
    write_polar(1, rows_ref, held_ref, send_ref, wide_ref)
    copies[1].wait()
    write_polar(0, rows_ref, held_ref, stage_ref, wide_ref)
    store = pltpu.make_async_copy(stage_ref, kept_ref, sems.at[3])
    store.start()
    write_edges(held_ref, near_ref, far_ref)
    store.wait()


def second_kernel(given_ref, kept_ref, out_ref, sem):
    zone = lax.axis_index("zone")

    @pl.when((zone == 1) | (zone == lax.axis_size("zone") - 2))
    def _():
        copy = pltpu.make_async_copy(given_ref, out_ref, sem)
        copy.start()
        copy.wait()


def band_terms(half_f):
    rate = 4.5 / (half_f * half_f)
    tap = (lanes_of(half_f.shape[0]) - HMAX).astype(F32)
    terms = jnp.where(jnp.abs(tap) <= half_f, jnp.exp(-rate * (tap * tap)), 0.0)
    return rate, jnp.broadcast_to(1.0 / jnp.sum(terms, axis=1, keepdims=True), half_f.shape)


def lon_kernel(halo_ref, x_ref, near_ref, far_ref,
               out_ref, near_rows_ref, far_rows_ref, wide_ref, done_ref, half_ref, rate_ref, scale_ref):
    shells, row_count, col_count = x_ref.shape
    some = shells // PIECES
    size = some * row_count
    tiles = col_count // LANES
    zone = lax.axis_index("zone")
    for i in range(row_count):
        half_ref[i : i + 1, :] = jnp.full((1, LANES), halo_ref[zone * row_count + i], jnp.int32).astype(F32)
    rate_ref[...], scale_ref[...] = band_terms(half_ref[...])
    lane = lanes_of(size)
    even = lax.rem(lax.axis_index("sector"), 2) == 0

    def unpacked(piece, turn, first, second):
        result = None
        for tile in range(piece * HMAX // LANES, ((piece + 1) * HMAX - 1) // LANES + 1):
            rows = slice(tile * size, (tile + 1) * size)
            place = piece * HMAX - tile * LANES
            values = jnp.where(even, first[rows, :].astype(F32), second[rows, :].astype(F32))
            shift = (turn - place) % LANES
            values = pltpu.roll(values, shift, 1) if shift else values
            result = values if result is None else jnp.where(lane < turn - place, result, values)
        return result

    for piece in range(PIECES):
        shell = slice(piece * some, (piece + 1) * some)

        def keep(t, values):
            for s in range(some):
                first = (piece * some + s) * PITCH
                wide_ref[t, first : first + row_count, :] = values[s * row_count : (s + 1) * row_count]

        previous = unpacked(piece, 0, far_ref, near_ref)
        for t in range(tiles):
            turned = pltpu.roll(
                x_ref[shell, :, t * LANES : (t + 1) * LANES].reshape(size, LANES).astype(F32), HMAX, 1
            )
            keep(t, jnp.where(lane < HMAX, previous, turned))
            previous = turned
        after = unpacked(piece, HMAX, near_ref, far_ref)
        keep(tiles, jnp.where(lane < HMAX, previous, jnp.where(lane < 2 * HMAX, after, 0.0)))
    depth = 2 * LANES
    offset = (lanes_of(depth) - lax.broadcasted_iota(jnp.int32, (depth, LANES), 0) + HMAX).astype(F32)
    square = offset * offset
    distance = jnp.abs(offset)

    def some_rows(block, carry):
        for u in range(UNROLL):
            i = block * UNROLL + u
            line = pl.ds(i, 1)
            band = jnp.where(distance <= half_ref[line, :], jnp.exp(-rate_ref[line, :] * square), 0.0)
            band = (band * scale_ref[line, :]).astype(BF16)
            values = [wide_ref[t, pl.ds(i, shells, stride=PITCH), :].astype(BF16) for t in range(tiles + 1)]
            stacked = jnp.concatenate(
                [jnp.concatenate(values[:tiles], axis=0), jnp.concatenate(values[1:], axis=0)], axis=1
            )
            result = jnp.dot(stacked, band, preferred_element_type=F32)
            for t in range(tiles):
                done_ref[t, pl.ds(i, shells, stride=PITCH), :] = result[t * shells : (t + 1) * shells]
        return carry

    lax.fori_loop(0, row_count // UNROLL, some_rows, 0)
    for t in range(tiles):
        for s in range(shells):
            out_ref[s, :, t * LANES : (t + 1) * LANES] = done_ref[t, s * PITCH : s * PITCH + row_count, :].astype(BF16)
    odd = lax.rem(zone, 2)
    last = row_count - LMAX
    near_rows_ref[...] = out_ref[:, pl.ds(pl.multiple_of((1 - odd) * last, LMAX), LMAX), :]
    far_rows_ref[...] = out_ref[:, pl.ds(pl.multiple_of(odd * last, LMAX), LMAX), :]


def hold_kernel(table_ref, x_ref, after_ref, out_ref, circle_ref):
    sectors, held, block, _ = x_ref.shape
    zone, sector = lax.axis_index("zone"), lax.axis_index("sector")
    polar = 2 * sectors * held
    cap = jnp.where(zone < 8, 0, sectors * held)
    length = sectors * block
    full_lon = length // PART * LANES
    depth = 3 * LANES
    for r in range(held):
        for copy in range(2):
            circle_ref[r, copy * length : (copy + 1) * length, :] = x_ref[:, r].reshape(length, LANES)
        circle_ref[r, 2 * length : 2 * length + 2 * PART, :] = circle_ref[r, 0 : 2 * PART, :]
    for r in range(held):
        entry = cap + sector * held + r
        half_f = jnp.full((1, LANES), table_ref[2 * polar + table_ref[entry]], jnp.int32).astype(F32)
        rate, scale = band_terms(half_f)
        start = lax.rem(2 * full_lon - table_ref[polar + entry] - HMAX, full_lon)
        first = start // LANES
        rest = start - first * LANES
        offset = (
            lanes_of(depth) - lax.broadcasted_iota(jnp.int32, (depth, LANES), 0) + (rest + HMAX)
        ).astype(F32)
        band = jnp.where(jnp.abs(offset) <= half_f, jnp.exp(-rate * (offset * offset)), 0.0) * scale
        values = jnp.concatenate(
            [circle_ref[r, pl.ds(pl.multiple_of((first + u) * PART, PART), length), :] for u in range(3)], axis=1
        )
        result = jnp.dot(values, band.astype(BF16), preferred_element_type=F32)
        out_ref[:, r] = result.astype(BF16).reshape(sectors, block, LANES)


def lat_kernel(rows_ref, near_ref, own_ref, far_ref, reach_ref, blend_ref,
               out_ref, polar_weight_ref, mix_ref, pick_ref):
    shells, row_count, col_count = own_ref.shape
    frame_rows = row_count + 2 * LMAX
    polar = pick_ref.shape[0]
    zone = lax.axis_index("zone")
    cap = jnp.where(zone < 8, 0, polar)
    lane = lanes_of(1)
    for p in range(polar):
        pick_ref[p : p + 1, :] = (lane == rows_ref[cap + p] - zone * row_count + LMAX).astype(F32)
    pick = pick_ref[...]
    zones = lax.axis_size("zone")
    reach = reach_ref[...]
    column = lax.broadcasted_iota(jnp.int32, (row_count, frame_rows), 1)
    away = column - LMAX - lax.broadcasted_iota(jnp.int32, (row_count, frame_rows), 0)
    source = zone * row_count - LMAX + column
    valid = (jnp.abs(away) <= reach) & (source >= 0) & (source < zones * row_count)
    reach_f = reach.astype(F32)
    away_f = away.astype(F32)
    weights = jnp.where(valid, jnp.exp(-(4.5 / (reach_f * reach_f)) * (away_f * away_f)), 0.0)
    weight = (weights / jnp.sum(weights, axis=1, keepdims=True)).astype(BF16)
    length = mix_ref.shape[0]
    group = length // shells
    spread = (
        lax.broadcasted_iota(jnp.int32, (length, shells), 0) // group
        == lax.broadcasted_iota(jnp.int32, (length, shells), 1)
    ).astype(F32).astype(BF16)
    tall = jnp.dot(spread, blend_ref[...], preferred_element_type=F32).astype(BF16)
    full = lax.dot_general(tall, spread, (((1,), (1,)), ((), ())), preferred_element_type=F32)
    same = (
        lax.broadcasted_iota(jnp.int32, (length, length), 0) % group
        == lax.broadcasted_iota(jnp.int32, (length, length), 1) % group
    )
    mix_ref[...] = jnp.where(same, full, 0.0).astype(BF16)
    polar_weight_ref[...] = lax.dot_general(
        weight, pick.astype(BF16), (((1,), (1,)), ((), ())), preferred_element_type=F32
    ).astype(BF16)
    rest = weight.astype(F32) * (1.0 - jnp.sum(pick, axis=0, keepdims=True))
    wide = lanes_of(row_count)
    turned = jnp.where(
        wide < LMAX,
        pltpu.roll(rest, LMAX, 1),
        jnp.where(wide < frame_rows - LMAX, rest, pltpu.roll(rest, frame_rows - LMAX, 1)),
    )
    rest = jnp.where(lax.rem(zone, 2) == 0, turned, rest).astype(BF16)

    def some_shells(block, carry):
        for u in range(4):
            s = block * 4 + u
            values = jnp.concatenate([near_ref[s], own_ref[s], far_ref[s]], axis=0)
            out_ref[s] = jnp.dot(rest, values, preferred_element_type=F32)
        return carry

    lax.fori_loop(0, shells // 4, some_shells, 0)


def own_part():
    zone = lax.axis_index("zone")
    return jnp.where((zone == 0) | (zone == lax.axis_size("zone") - 1), 0, 1)


def add_polar(part, source_ref, weight_ref, lat_ref, polar_ref, sum_ref, sem, put):
    holders, held = source_ref.shape[:2]
    tiles = polar_ref.shape[0]
    polar = holders * held
    pitch = polar + 1
    fetch = pltpu.make_async_copy(lat_ref.at[pl.ds(part * PART, PART)], sum_ref, sem)
    fetch.start()
    for k in range(holders):
        for r in range(held):
            for t in range(tiles):
                polar_ref[t, pl.ds(k * held + r, PART, stride=pitch), :] = source_ref[
                    k, r, t * PART : (t + 1) * PART, :
                ].astype(F32)
    weight = weight_ref[...]
    fetch.wait()

    def some_shells(index, carry):
        for u in range(4):
            s = index * 4 + u
            values = jnp.concatenate(
                [polar_ref[t, pl.ds(s * pitch, polar), :].astype(BF16) for t in range(tiles)], axis=1
            )
            put(s, sum_ref[s] + jnp.dot(weight, values, preferred_element_type=F32))
        return carry

    lax.fori_loop(0, PART // 4, some_shells, 0)


def own_kernel(mine_ref, weight_ref, lat_ref, out_ref, polar_ref, sum_ref, sem):
    def put(s, values):
        out_ref[s] = values.astype(BF16)

    add_polar(own_part(), mine_ref, weight_ref, lat_ref, polar_ref, sum_ref, sem, put)


def final_kernel(other_ref, own_ref, weight_ref, mix_ref, lat_ref, out_ref,
                 polar_ref, sum_ref, full_ref, stage_ref, sem, sems):
    shells, row_count, col_count = lat_ref.shape
    part = own_part()

    def put(s, values):
        full_ref[(1 - part) * PART + s] = values

    add_polar(1 - part, other_ref, weight_ref, lat_ref, polar_ref, sum_ref, sem, put)
    for s in range(PART):
        full_ref[part * PART + s] = own_ref[s].astype(F32)
    group = mix_ref.shape[0] // shells
    mix = mix_ref[...]
    stores = []
    for g in range(row_count // (2 * group)):
        mixed = []
        for e in range(2):
            first = (2 * g + e) * group
            values = full_ref[:, first : first + group, :].reshape(shells * group, col_count).astype(BF16)
            mixed.append(jnp.dot(mix, values, preferred_element_type=F32).reshape(shells, group, col_count))
        rows = pl.ds(2 * g * group, 2 * group)
        stage_ref[:, rows, :] = jnp.concatenate(mixed, axis=1).astype(BF16)
        stores.append(pltpu.make_async_copy(stage_ref.at[:, rows], out_ref.at[:, rows], sems.at[g]))
        stores[-1].start()
    for store in stores:
        store.wait()


def call(kernel, name, out_shape, scalars, arrays, scratch, flops=0, moved=0, direct=(), far=False, mib=16):
    smem = pl.BlockSpec(memory_space=pltpu.SMEM)
    vmem = pl.BlockSpec(memory_space=pltpu.VMEM)
    anywhere = pl.BlockSpec(memory_space=pl.ANY)
    many = isinstance(out_shape, tuple)
    return pl.pallas_call(
        kernel,
        out_shape=out_shape,
        in_specs=[smem] * len(scalars) + [vmem] * len(arrays) + [anywhere] * len(direct),
        out_specs=(vmem,) * len(out_shape) if many else anywhere if far else vmem,
        scratch_shapes=scratch,
        compiler_params=pltpu.CompilerParams(vmem_limit_bytes=mib << 20),
        cost_estimate=pl.CostEstimate(flops=flops, bytes_accessed=moved, transcendentals=0),
        name=name,
    )(*scalars, *arrays, *direct)


struct = jax.ShapeDtypeStruct


def pack(polar_rows, kernel, sectors):
    shells, row_count, col_count = kernel.shape
    tiles = col_count // LANES
    held = polar_rows.shape[0] // 2 // sectors
    edge = struct((shells * row_count * HMAX // LANES, LANES), BF16)
    parts = struct((sectors, held, tiles * PART, LANES), BF16)
    vmem = pl.BlockSpec(memory_space=pltpu.VMEM)
    anywhere = pl.BlockSpec(memory_space=pl.ANY)
    return pl.pallas_call(
        first_kernel,
        out_shape=(parts, edge, edge, parts),
        in_specs=[anywhere, anywhere],
        out_specs=(vmem, vmem, vmem, anywhere),
        scratch_shapes=[
            pltpu.VMEM((tiles, PART * PITCH, LANES), F32),
            pltpu.VMEM(kernel.shape, BF16),
            pltpu.VMEM(parts.shape, BF16),
            pltpu.SMEM(polar_rows.shape, jnp.int32),
            pltpu.SemaphoreType.DMA((4,)),
        ],
        compiler_params=pltpu.CompilerParams(vmem_limit_bytes=52 << 20),
        cost_estimate=pl.CostEstimate(flops=0, bytes_accessed=4 << 20, transcendentals=0),
        name="pack_polar_rows_and_edges",
    )(kernel, polar_rows)


def take_given(given, kept):
    anywhere = pl.BlockSpec(memory_space=pl.ANY)
    return pl.pallas_call(
        second_kernel,
        out_shape=struct(kept.shape, BF16),
        in_specs=[anywhere, anywhere],
        out_specs=anywhere,
        scratch_shapes=[pltpu.SemaphoreType.DMA],
        input_output_aliases={1: 0},
        compiler_params=pltpu.CompilerParams(vmem_limit_bytes=4 << 20),
        name="take_given",
    )(given, kept)


def smooth_lon(lon_halo, kernel, near, far):
    shells, row_count, col_count = kernel.shape
    tiles = col_count // LANES
    rows = pltpu.VMEM((row_count, LANES), F32)
    return call(
        lon_kernel,
        "smooth_along_longitude",
        (
            struct((shells, row_count, col_count), BF16),
            struct((shells, LMAX, col_count), BF16),
            struct((shells, LMAX, col_count), BF16),
        ),
        [lon_halo],
        [kernel, near, far],
        [
            pltpu.VMEM((tiles + 1, shells * PITCH, LANES), F32),
            pltpu.VMEM((tiles, shells * PITCH, LANES), F32),
            rows,
            rows,
            rows,
        ],
        flops=1 << 36,
        moved=16 << 20,
        mib=20,
    )


def hold(table, circles, after):
    sectors, held, block, _ = circles.shape
    return call(
        hold_kernel,
        "smooth_and_turn_polar_circles",
        struct(circles.shape, BF16),
        [table],
        [circles],
        [pltpu.VMEM((held, 2 * sectors * block + 2 * PART, LANES), BF16)],
        flops=1 << 30,
        moved=4 << 20,
        direct=[after],
    )


def smooth_lat(polar_rows, near, own, far, reach, blend):
    shells, row_count, _ = own.shape
    frame_rows = row_count + 2 * LMAX
    polar = polar_rows.shape[0] // 2
    return call(
        lat_kernel,
        "smooth_along_latitude",
        (
            struct(own.shape, F32),
            struct((row_count, polar), BF16),
            struct((shells * 8, shells * 8), BF16),
        ),
        [polar_rows],
        [near, own, far, reach, blend],
        [pltpu.VMEM((polar, frame_rows), F32)],
        flops=1 << 36,
        moved=8 << 20,
    )


def add_own(lat, mine, polar_weight):
    shells, row_count, col_count = lat.shape
    half = (PART, row_count, col_count)
    return call(
        own_kernel,
        "add_polar_rows_of_own_shells",
        struct(half, BF16),
        [],
        [mine, polar_weight],
        [
            pltpu.VMEM((col_count // LANES, PART * (polar_weight.shape[1] + 1), LANES), F32),
            pltpu.VMEM(half, F32),
            pltpu.SemaphoreType.DMA,
        ],
        flops=1 << 30,
        moved=4 << 20,
        direct=[lat],
        mib=50,
    )


def finish(lat, other, own, polar_weight, mix):
    shells, row_count, col_count = lat.shape
    return call(
        final_kernel,
        "add_polar_rows_and_blend",
        struct(lat.shape, BF16),
        [],
        [other, own, polar_weight, mix],
        [
            pltpu.VMEM((col_count // LANES, PART * (polar_weight.shape[1] + 1), LANES), F32),
            pltpu.VMEM((PART, row_count, col_count), F32),
            pltpu.VMEM(lat.shape, F32),
            pltpu.VMEM(lat.shape, BF16),
            pltpu.SemaphoreType.DMA,
            pltpu.SemaphoreType.DMA((4,)),
        ],
        flops=1 << 31,
        moved=8 << 20,
        far=True,
        direct=[lat],
        mib=50,
    )


def per_device(kernel, lon_halo, lat_reach, polar_rows, polar_shift, blend):
    shells, row_count, col_count = kernel.shape
    sectors = lax.axis_size("sector")
    zones = lax.axis_size("zone")
    last = zones - 1
    packed, near, far, kept = pack(polar_rows, kernel, sectors)
    given = lax.ppermute(packed, "zone", [(0, 1), (last, last - 1)])
    far = lax.ppermute(far, "sector", [(i, (i + 1 if i % 2 else i - 1) % sectors) for i in range(sectors)])
    near = lax.ppermute(near, "sector", [(i, i ^ 1) for i in range(sectors)])
    parts = take_given(given, kept)
    circles = lax.all_to_all(parts, "sector", 0, 0, tiled=True)
    lon_smooth, near_rows, far_rows = smooth_lon(lon_halo, kernel, near, far)
    turned = hold(jnp.concatenate([polar_rows, polar_shift, lon_halo]), circles, far_rows)
    far_rows = lax.ppermute(
        far_rows, "zone", [(i, i + 1 if i % 2 else i - 1) for i in range(1, zones - 1)]
    )
    near_rows = lax.ppermute(near_rows, "zone", [(i, i ^ 1) for i in range(zones)])
    mine = lax.all_to_all(turned, "sector", 0, 0, tiled=True)
    lat, polar_weight, mix = smooth_lat(
        polar_rows, near_rows, lon_smooth, far_rows, lat_reach[:, None], blend
    )
    mine, lat = lax.optimization_barrier((mine, lat))
    other = lax.ppermute(mine, "zone", [(0, 1), (1, 0), (last, last - 1), (last - 1, last)])
    own = add_own(lat, mine, polar_weight)
    return finish(lat, other, own, polar_weight, mix)


def solution(mesh):
    in_specs = (P(None, "zone", "sector"), P(), P("zone"), P(), P(), P())
    out_specs = P(None, "zone", "sector")
    return jax.shard_map(
        per_device, mesh=mesh, in_specs=in_specs, out_specs=out_specs, check_vma=False
    )
```

```python
import jax
import jax.numpy as jnp
from jax import lax
from jax.experimental import pallas as pl
from jax.experimental.pallas import tpu as pltpu
from jax.sharding import PartitionSpec as P

HMAX = 48
LMAX = 32
LANES = 128
PART = 16
UNROLL = 8
PITCH = 65
F32 = jnp.float32
BF16 = jnp.bfloat16


def lanes_of(rows):
    return lax.broadcasted_iota(jnp.int32, (rows, LANES), 1)


def write_edges(x_ref, near_ref, far_ref):
    shells, row_count, col_count = x_ref.shape
    half = shells // 2
    size = half * row_count
    lane = lanes_of(size)

    def part(column, shell):
        return x_ref[shell : shell + half, :, column : column + LANES].reshape(size, LANES).astype(F32)

    last = col_count - LANES
    even = lax.rem(lax.axis_index("sector"), 2) == 0
    low = jnp.where(lane < HMAX, part(0, 0), pltpu.roll(part(0, half), HMAX, 1))
    high = jnp.where(lane < HMAX, pltpu.roll(part(last, 0), HMAX, 1), pltpu.roll(part(last, half), 2 * HMAX, 1))
    near_ref[...] = jnp.where(even, high, low).astype(BF16)
    far_ref[...] = jnp.where(even, low, high).astype(BF16)


def write_polar(half, rows_ref, x_ref, send_ref, wide_ref):
    _, row_count, col_count = x_ref.shape
    tiles = col_count // LANES
    zone = lax.axis_index("zone")
    for t in range(tiles):
        for s in range(PART):
            wide_ref[t, s * PITCH : s * PITCH + row_count, :] = x_ref[
                half * PART + s, :, t * LANES : (t + 1) * LANES
            ].astype(F32)
    holders, held = send_ref.shape[0], send_ref.shape[1]
    cap = jnp.where(zone < 8, 0, holders * held)
    for k in range(holders):
        for r in range(held):
            row = jnp.clip(rows_ref[cap + k * held + r] - zone * row_count, 0, row_count - 1)
            for t in range(tiles):
                values = wide_ref[t, pl.ds(row, PART, stride=PITCH), :]
                send_ref[k, r, t * PART : (t + 1) * PART, :] = values.astype(BF16)


def first_kernel(x_ref, far_rows_ref, send_ref, near_ref, far_ref, kept_ref,
                 wide_ref, held_ref, stage_ref, rows_ref, sems):
    fetch = pltpu.make_async_copy(far_rows_ref, rows_ref, sems.at[2])
    fetch.start()
    copies = []
    for half in (1, 0):
        shells = pl.ds(half * PART, PART)
        copies.append(pltpu.make_async_copy(x_ref.at[shells], held_ref.at[shells], sems.at[half]))
        copies[-1].start()
    fetch.wait()
    copies[0].wait()
    write_polar(1, rows_ref, held_ref, send_ref, wide_ref)
    copies[1].wait()
    write_polar(0, rows_ref, held_ref, stage_ref, wide_ref)
    store = pltpu.make_async_copy(stage_ref, kept_ref, sems.at[3])
    store.start()
    write_edges(held_ref, near_ref, far_ref)
    store.wait()


def second_kernel(given_ref, kept_ref, out_ref, sem):
    zone = lax.axis_index("zone")

    @pl.when((zone == 1) | (zone == lax.axis_size("zone") - 2))
    def _():
        copy = pltpu.make_async_copy(given_ref, out_ref, sem)
        copy.start()
        copy.wait()


def band_terms(half_f):
    rate = 4.5 / (half_f * half_f)
    tap = (lanes_of(half_f.shape[0]) - HMAX).astype(F32)
    terms = jnp.where(jnp.abs(tap) <= half_f, jnp.exp(-rate * (tap * tap)), 0.0)
    return rate, jnp.broadcast_to(1.0 / jnp.sum(terms, axis=1, keepdims=True), half_f.shape)


def lon_kernel(halo_ref, x_ref, near_ref, far_ref,
               out_ref, near_rows_ref, far_rows_ref, wide_ref, done_ref, half_ref, rate_ref, scale_ref):
    shells, row_count, col_count = x_ref.shape
    total = shells * row_count
    size = total // 2
    tiles = col_count // LANES
    zone = lax.axis_index("zone")
    for i in range(row_count):
        half_ref[i : i + 1, :] = jnp.full((1, LANES), halo_ref[zone * row_count + i], jnp.int32).astype(F32)
    rate_ref[...], scale_ref[...] = band_terms(half_ref[...])
    lane = lanes_of(size)
    even = lax.rem(lax.axis_index("sector"), 2) == 0
    near = near_ref[...].astype(F32)
    far = far_ref[...].astype(F32)
    before = jnp.where(even, far, near)
    after = jnp.where(even, near, far)

    def keep(t, part, values):
        for s in range(shells // 2):
            first = (part * (shells // 2) + s) * PITCH
            wide_ref[t, first : first + row_count, :] = values[s * row_count : (s + 1) * row_count]

    for part in range(2):
        shell = slice(part * (shells // 2), (part + 1) * (shells // 2))
        previous = before if part == 0 else pltpu.roll(before, LANES - HMAX, 1)
        for t in range(tiles):
            turned = pltpu.roll(
                x_ref[shell, :, t * LANES : (t + 1) * LANES].reshape(size, LANES).astype(F32), HMAX, 1
            )
            keep(t, part, jnp.where(lane < HMAX, previous, turned))
            previous = turned
        edge = pltpu.roll(after, HMAX, 1) if part == 0 else after
        keep(tiles, part, jnp.where(lane < HMAX, previous, jnp.where(lane < 2 * HMAX, edge, 0.0)))
    depth = 2 * LANES
    offset = (lanes_of(depth) - lax.broadcasted_iota(jnp.int32, (depth, LANES), 0) + HMAX).astype(F32)
    square = offset * offset
    distance = jnp.abs(offset)

    def some_rows(block, carry):
        for u in range(UNROLL):
            i = block * UNROLL + u
            line = pl.ds(i, 1)
            band = jnp.where(distance <= half_ref[line, :], jnp.exp(-rate_ref[line, :] * square), 0.0)
            band = (band * scale_ref[line, :]).astype(BF16)
            values = [wide_ref[t, pl.ds(i, shells, stride=PITCH), :].astype(BF16) for t in range(tiles + 1)]
            stacked = jnp.concatenate(
                [jnp.concatenate(values[:tiles], axis=0), jnp.concatenate(values[1:], axis=0)], axis=1
            )
            result = jnp.dot(stacked, band, preferred_element_type=F32)
            for t in range(tiles):
                done_ref[t, pl.ds(i, shells, stride=PITCH), :] = result[t * shells : (t + 1) * shells]
        return carry

    lax.fori_loop(0, row_count // UNROLL, some_rows, 0)
    for t in range(tiles):
        for s in range(shells):
            out_ref[s, :, t * LANES : (t + 1) * LANES] = done_ref[t, s * PITCH : s * PITCH + row_count, :].astype(BF16)
    odd = lax.rem(zone, 2)
    last = row_count - LMAX
    near_rows_ref[...] = out_ref[:, pl.ds(pl.multiple_of((1 - odd) * last, LMAX), LMAX), :]
    far_rows_ref[...] = out_ref[:, pl.ds(pl.multiple_of(odd * last, LMAX), LMAX), :]


def hold_kernel(table_ref, x_ref, after_ref, out_ref, circle_ref):
    sectors, held, block, _ = x_ref.shape
    zone, sector = lax.axis_index("zone"), lax.axis_index("sector")
    polar = 2 * sectors * held
    cap = jnp.where(zone < 8, 0, sectors * held)
    length = sectors * block
    full_lon = length // PART * LANES
    depth = 3 * LANES
    for r in range(held):
        for copy in range(2):
            circle_ref[r, copy * length : (copy + 1) * length, :] = x_ref[:, r].reshape(length, LANES)
        circle_ref[r, 2 * length : 2 * length + 2 * PART, :] = circle_ref[r, 0 : 2 * PART, :]
    for r in range(held):
        entry = cap + sector * held + r
        half_f = jnp.full((1, LANES), table_ref[2 * polar + table_ref[entry]], jnp.int32).astype(F32)
        rate, scale = band_terms(half_f)
        start = lax.rem(2 * full_lon - table_ref[polar + entry] - HMAX, full_lon)
        first = start // LANES
        rest = start - first * LANES
        offset = (
            lanes_of(depth) - lax.broadcasted_iota(jnp.int32, (depth, LANES), 0) + (rest + HMAX)
        ).astype(F32)
        band = jnp.where(jnp.abs(offset) <= half_f, jnp.exp(-rate * (offset * offset)), 0.0) * scale
        values = jnp.concatenate(
            [circle_ref[r, pl.ds(pl.multiple_of((first + u) * PART, PART), length), :] for u in range(3)], axis=1
        )
        result = jnp.dot(values, band.astype(BF16), preferred_element_type=F32)
        out_ref[:, r] = result.astype(BF16).reshape(sectors, block, LANES)


def lat_kernel(rows_ref, near_ref, own_ref, far_ref, reach_ref, blend_ref,
               out_ref, polar_weight_ref, mix_ref, pick_ref):
    shells, row_count, col_count = own_ref.shape
    frame_rows = row_count + 2 * LMAX
    polar = pick_ref.shape[0]
    zone = lax.axis_index("zone")
    cap = jnp.where(zone < 8, 0, polar)
    lane = lanes_of(1)
    for p in range(polar):
        pick_ref[p : p + 1, :] = (lane == rows_ref[cap + p] - zone * row_count + LMAX).astype(F32)
    pick = pick_ref[...]
    zones = lax.axis_size("zone")
    reach = reach_ref[...]
    column = lax.broadcasted_iota(jnp.int32, (row_count, frame_rows), 1)
    away = column - LMAX - lax.broadcasted_iota(jnp.int32, (row_count, frame_rows), 0)
    source = zone * row_count - LMAX + column
    valid = (jnp.abs(away) <= reach) & (source >= 0) & (source < zones * row_count)
    reach_f = reach.astype(F32)
    away_f = away.astype(F32)
    weights = jnp.where(valid, jnp.exp(-(4.5 / (reach_f * reach_f)) * (away_f * away_f)), 0.0)
    weight = (weights / jnp.sum(weights, axis=1, keepdims=True)).astype(BF16)
    length = mix_ref.shape[0]
    group = length // shells
    spread = (
        lax.broadcasted_iota(jnp.int32, (length, shells), 0) // group
        == lax.broadcasted_iota(jnp.int32, (length, shells), 1)
    ).astype(F32).astype(BF16)
    tall = jnp.dot(spread, blend_ref[...], preferred_element_type=F32).astype(BF16)
    full = lax.dot_general(tall, spread, (((1,), (1,)), ((), ())), preferred_element_type=F32)
    same = (
        lax.broadcasted_iota(jnp.int32, (length, length), 0) % group
        == lax.broadcasted_iota(jnp.int32, (length, length), 1) % group
    )
    mix_ref[...] = jnp.where(same, full, 0.0).astype(BF16)
    polar_weight_ref[...] = lax.dot_general(
        weight, pick.astype(BF16), (((1,), (1,)), ((), ())), preferred_element_type=F32
    ).astype(BF16)
    rest = weight.astype(F32) * (1.0 - jnp.sum(pick, axis=0, keepdims=True))
    wide = lanes_of(row_count)
    turned = jnp.where(
        wide < LMAX,
        pltpu.roll(rest, LMAX, 1),
        jnp.where(wide < frame_rows - LMAX, rest, pltpu.roll(rest, frame_rows - LMAX, 1)),
    )
    rest = jnp.where(lax.rem(zone, 2) == 0, turned, rest).astype(BF16)

    def some_shells(block, carry):
        for u in range(4):
            s = block * 4 + u
            values = jnp.concatenate([near_ref[s], own_ref[s], far_ref[s]], axis=0)
            out_ref[s] = jnp.dot(rest, values, preferred_element_type=F32)
        return carry

    lax.fori_loop(0, shells // 4, some_shells, 0)


def own_part():
    zone = lax.axis_index("zone")
    return jnp.where((zone == 0) | (zone == lax.axis_size("zone") - 1), 0, 1)


def add_polar(part, source_ref, weight_ref, lat_ref, polar_ref, sum_ref, sem, put):
    holders, held = source_ref.shape[:2]
    tiles = polar_ref.shape[0]
    polar = holders * held
    pitch = polar + 1
    fetch = pltpu.make_async_copy(lat_ref.at[pl.ds(part * PART, PART)], sum_ref, sem)
    fetch.start()
    for k in range(holders):
        for r in range(held):
            for t in range(tiles):
                polar_ref[t, pl.ds(k * held + r, PART, stride=pitch), :] = source_ref[
                    k, r, t * PART : (t + 1) * PART, :
                ].astype(F32)
    weight = weight_ref[...]
    fetch.wait()

    for s in range(PART):
        values = jnp.concatenate(
            [polar_ref[t, pl.ds(s * pitch, polar), :].astype(BF16) for t in range(tiles)], axis=1
        )
        put(s, sum_ref[s] + jnp.dot(weight, values, preferred_element_type=F32))


def own_kernel(mine_ref, weight_ref, lat_ref, out_ref, polar_ref, sum_ref, sem):
    def put(s, values):
        out_ref[s] = values.astype(BF16)

    add_polar(own_part(), mine_ref, weight_ref, lat_ref, polar_ref, sum_ref, sem, put)


def final_kernel(other_ref, own_ref, weight_ref, mix_ref, lat_ref, out_ref,
                 polar_ref, sum_ref, full_ref, stage_ref, sem, sems):
    shells, row_count, col_count = lat_ref.shape
    part = own_part()

    def put(s, values):
        full_ref[(1 - part) * PART + s] = values

    add_polar(1 - part, other_ref, weight_ref, lat_ref, polar_ref, sum_ref, sem, put)
    for s in range(PART):
        full_ref[part * PART + s] = own_ref[s].astype(F32)
    group = mix_ref.shape[0] // shells
    mix = mix_ref[...]
    stores = []
    for g in range(row_count // (2 * group)):
        mixed = []
        for e in range(2):
            first = (2 * g + e) * group
            values = full_ref[:, first : first + group, :].reshape(shells * group, col_count).astype(BF16)
            mixed.append(jnp.dot(mix, values, preferred_element_type=F32).reshape(shells, group, col_count))
        rows = pl.ds(2 * g * group, 2 * group)
        stage_ref[:, rows, :] = jnp.concatenate(mixed, axis=1).astype(BF16)
        stores.append(pltpu.make_async_copy(stage_ref.at[:, rows], out_ref.at[:, rows], sems.at[g]))
        stores[-1].start()
    for store in stores:
        store.wait()


def call(kernel, name, out_shape, scalars, arrays, scratch, flops=0, moved=0, direct=(), far=False, mib=16):
    smem = pl.BlockSpec(memory_space=pltpu.SMEM)
    vmem = pl.BlockSpec(memory_space=pltpu.VMEM)
    anywhere = pl.BlockSpec(memory_space=pl.ANY)
    many = isinstance(out_shape, tuple)
    return pl.pallas_call(
        kernel,
        out_shape=out_shape,
        in_specs=[smem] * len(scalars) + [vmem] * len(arrays) + [anywhere] * len(direct),
        out_specs=(vmem,) * len(out_shape) if many else anywhere if far else vmem,
        scratch_shapes=scratch,
        compiler_params=pltpu.CompilerParams(vmem_limit_bytes=mib << 20),
        cost_estimate=pl.CostEstimate(flops=flops, bytes_accessed=moved, transcendentals=0),
        name=name,
    )(*scalars, *arrays, *direct)


struct = jax.ShapeDtypeStruct


def pack(polar_rows, kernel, sectors):
    shells, row_count, col_count = kernel.shape
    tiles = col_count // LANES
    held = polar_rows.shape[0] // 2 // sectors
    edge = struct((shells * row_count // 2, LANES), BF16)
    parts = struct((sectors, held, tiles * PART, LANES), BF16)
    vmem = pl.BlockSpec(memory_space=pltpu.VMEM)
    anywhere = pl.BlockSpec(memory_space=pl.ANY)
    return pl.pallas_call(
        first_kernel,
        out_shape=(parts, edge, edge, parts),
        in_specs=[anywhere, anywhere],
        out_specs=(vmem, vmem, vmem, anywhere),
        scratch_shapes=[
            pltpu.VMEM((tiles, PART * PITCH, LANES), F32),
            pltpu.VMEM(kernel.shape, BF16),
            pltpu.VMEM(parts.shape, BF16),
            pltpu.SMEM(polar_rows.shape, jnp.int32),
            pltpu.SemaphoreType.DMA((4,)),
        ],
        compiler_params=pltpu.CompilerParams(vmem_limit_bytes=52 << 20),
        cost_estimate=pl.CostEstimate(flops=0, bytes_accessed=4 << 20, transcendentals=0),
        name="pack_polar_rows_and_edges",
    )(kernel, polar_rows)


def take_given(given, kept):
    anywhere = pl.BlockSpec(memory_space=pl.ANY)
    return pl.pallas_call(
        second_kernel,
        out_shape=struct(kept.shape, BF16),
        in_specs=[anywhere, anywhere],
        out_specs=anywhere,
        scratch_shapes=[pltpu.SemaphoreType.DMA],
        input_output_aliases={1: 0},
        compiler_params=pltpu.CompilerParams(vmem_limit_bytes=4 << 20),
        name="take_given",
    )(given, kept)


def smooth_lon(lon_halo, kernel, near, far):
    shells, row_count, col_count = kernel.shape
    tiles = col_count // LANES
    rows = pltpu.VMEM((row_count, LANES), F32)
    return call(
        lon_kernel,
        "smooth_along_longitude",
        (
            struct((shells, row_count, col_count), BF16),
            struct((shells, LMAX, col_count), BF16),
            struct((shells, LMAX, col_count), BF16),
        ),
        [lon_halo],
        [kernel, near, far],
        [
            pltpu.VMEM((tiles + 1, shells * PITCH, LANES), F32),
            pltpu.VMEM((tiles, shells * PITCH, LANES), F32),
            rows,
            rows,
            rows,
        ],
        flops=1 << 36,
        moved=16 << 20,
        mib=20,
    )


def hold(table, circles, after):
    sectors, held, block, _ = circles.shape
    return call(
        hold_kernel,
        "smooth_and_turn_polar_circles",
        struct(circles.shape, BF16),
        [table],
        [circles],
        [pltpu.VMEM((held, 2 * sectors * block + 2 * PART, LANES), BF16)],
        flops=1 << 30,
        moved=4 << 20,
        direct=[after],
    )


def smooth_lat(polar_rows, near, own, far, reach, blend):
    shells, row_count, _ = own.shape
    frame_rows = row_count + 2 * LMAX
    polar = polar_rows.shape[0] // 2
    return call(
        lat_kernel,
        "smooth_along_latitude",
        (
            struct(own.shape, F32),
            struct((row_count, polar), BF16),
            struct((shells * 8, shells * 8), BF16),
        ),
        [polar_rows],
        [near, own, far, reach, blend],
        [pltpu.VMEM((polar, frame_rows), F32)],
        flops=1 << 36,
        moved=8 << 20,
    )


def add_own(lat, mine, polar_weight):
    shells, row_count, col_count = lat.shape
    half = (PART, row_count, col_count)
    return call(
        own_kernel,
        "add_polar_rows_of_own_shells",
        struct(half, BF16),
        [],
        [mine, polar_weight],
        [
            pltpu.VMEM((col_count // LANES, PART * (polar_weight.shape[1] + 1), LANES), F32),
            pltpu.VMEM(half, F32),
            pltpu.SemaphoreType.DMA,
        ],
        flops=1 << 30,
        moved=4 << 20,
        direct=[lat],
        mib=50,
    )


def finish(lat, other, own, polar_weight, mix):
    shells, row_count, col_count = lat.shape
    return call(
        final_kernel,
        "add_polar_rows_and_blend",
        struct(lat.shape, BF16),
        [],
        [other, own, polar_weight, mix],
        [
            pltpu.VMEM((col_count // LANES, PART * (polar_weight.shape[1] + 1), LANES), F32),
            pltpu.VMEM((PART, row_count, col_count), F32),
            pltpu.VMEM(lat.shape, F32),
            pltpu.VMEM(lat.shape, BF16),
            pltpu.SemaphoreType.DMA,
            pltpu.SemaphoreType.DMA((4,)),
        ],
        flops=1 << 31,
        moved=8 << 20,
        far=True,
        direct=[lat],
        mib=50,
    )


def per_device(kernel, lon_halo, lat_reach, polar_rows, polar_shift, blend):
    shells, row_count, col_count = kernel.shape
    sectors = lax.axis_size("sector")
    zones = lax.axis_size("zone")
    last = zones - 1
    packed, near, far, kept = pack(polar_rows, kernel, sectors)
    given = lax.ppermute(packed, "zone", [(0, 1), (last, last - 1)])
    far = lax.ppermute(far, "sector", [(i, (i + 1 if i % 2 else i - 1) % sectors) for i in range(sectors)])
    near = lax.ppermute(near, "sector", [(i, i ^ 1) for i in range(sectors)])
    parts = take_given(given, kept)
    circles = lax.all_to_all(parts, "sector", 0, 0, tiled=True)
    lon_smooth, near_rows, far_rows = smooth_lon(lon_halo, kernel, near, far)
    turned = hold(jnp.concatenate([polar_rows, polar_shift, lon_halo]), circles, far_rows)
    far_rows = lax.ppermute(
        far_rows, "zone", [(i, i + 1 if i % 2 else i - 1) for i in range(1, zones - 1)]
    )
    near_rows = lax.ppermute(near_rows, "zone", [(i, i ^ 1) for i in range(zones)])
    mine = lax.all_to_all(turned, "sector", 0, 0, tiled=True)
    lat, polar_weight, mix = smooth_lat(
        polar_rows, near_rows, lon_smooth, far_rows, lat_reach[:, None], blend
    )
    mine, lat = lax.optimization_barrier((mine, lat))
    other = lax.ppermute(mine, "zone", [(0, 1), (1, 0), (last, last - 1), (last - 1, last)])
    own = add_own(lat, mine, polar_weight)
    return finish(lat, other, own, polar_weight, mix)


def solution(mesh):
    in_specs = (P(None, "zone", "sector"), P(), P("zone"), P(), P(), P())
    out_specs = P(None, "zone", "sector")
    return jax.shard_map(
        per_device, mesh=mesh, in_specs=in_specs, out_specs=out_specs, check_vma=False
    )
```

```python
import jax
import jax.numpy as jnp
from jax import lax
from jax.experimental import pallas as pl
from jax.experimental.pallas import tpu as pltpu
from jax.sharding import PartitionSpec as P

HMAX = 48
LMAX = 32
LANES = 128
PART = 16
UNROLL = 16
PITCH = 65
F32 = jnp.float32
BF16 = jnp.bfloat16


def lanes_of(rows):
    return lax.broadcasted_iota(jnp.int32, (rows, LANES), 1)


def write_edges(x_ref, near_ref, far_ref):
    shells, row_count, col_count = x_ref.shape
    half = shells // 2
    size = half * row_count
    lane = lanes_of(size)

    def part(column, shell):
        return x_ref[shell : shell + half, :, column : column + LANES].reshape(size, LANES).astype(F32)

    last = col_count - LANES
    even = lax.rem(lax.axis_index("sector"), 2) == 0
    low = jnp.where(lane < HMAX, part(0, 0), pltpu.roll(part(0, half), HMAX, 1))
    high = jnp.where(lane < HMAX, pltpu.roll(part(last, 0), HMAX, 1), pltpu.roll(part(last, half), 2 * HMAX, 1))
    near_ref[...] = jnp.where(even, high, low).astype(BF16)
    far_ref[...] = jnp.where(even, low, high).astype(BF16)


def write_polar(half, rows_ref, x_ref, send_ref, wide_ref):
    _, row_count, col_count = x_ref.shape
    tiles = col_count // LANES
    zone = lax.axis_index("zone")
    for t in range(tiles):
        for s in range(PART):
            wide_ref[t, s * PITCH : s * PITCH + row_count, :] = x_ref[
                half * PART + s, :, t * LANES : (t + 1) * LANES
            ].astype(F32)
    holders, held = send_ref.shape[0], send_ref.shape[1]
    cap = jnp.where(zone < 8, 0, holders * held)
    for k in range(holders):
        for r in range(held):
            row = jnp.clip(rows_ref[cap + k * held + r] - zone * row_count, 0, row_count - 1)
            for t in range(tiles):
                values = wide_ref[t, pl.ds(row, PART, stride=PITCH), :]
                send_ref[k, r, t * PART : (t + 1) * PART, :] = values.astype(BF16)


def first_kernel(x_ref, far_rows_ref, send_ref, near_ref, far_ref, kept_ref,
                 wide_ref, held_ref, stage_ref, rows_ref, sems):
    fetch = pltpu.make_async_copy(far_rows_ref, rows_ref, sems.at[2])
    fetch.start()
    copies = []
    for half in (1, 0):
        shells = pl.ds(half * PART, PART)
        copies.append(pltpu.make_async_copy(x_ref.at[shells], held_ref.at[shells], sems.at[half]))
        copies[-1].start()
    fetch.wait()
    copies[0].wait()
    write_polar(1, rows_ref, held_ref, send_ref, wide_ref)
    copies[1].wait()
    write_polar(0, rows_ref, held_ref, stage_ref, wide_ref)
    store = pltpu.make_async_copy(stage_ref, kept_ref, sems.at[3])
    store.start()
    write_edges(held_ref, near_ref, far_ref)
    store.wait()


def second_kernel(given_ref, kept_ref, out_ref, sem):
    zone = lax.axis_index("zone")

    @pl.when((zone == 1) | (zone == lax.axis_size("zone") - 2))
    def _():
        copy = pltpu.make_async_copy(given_ref, out_ref, sem)
        copy.start()
        copy.wait()


def band_terms(half_f):
    rate = 4.5 / (half_f * half_f)
    tap = (lanes_of(half_f.shape[0]) - HMAX).astype(F32)
    terms = jnp.where(jnp.abs(tap) <= half_f, jnp.exp(-rate * (tap * tap)), 0.0)
    return rate, jnp.broadcast_to(1.0 / jnp.sum(terms, axis=1, keepdims=True), half_f.shape)


def lon_kernel(halo_ref, x_ref, near_ref, far_ref,
               out_ref, near_rows_ref, far_rows_ref, wide_ref, done_ref, half_ref, rate_ref, scale_ref):
    shells, row_count, col_count = x_ref.shape
    total = shells * row_count
    size = total // 2
    tiles = col_count // LANES
    zone = lax.axis_index("zone")
    for i in range(row_count):
        half_ref[i : i + 1, :] = jnp.full((1, LANES), halo_ref[zone * row_count + i], jnp.int32).astype(F32)
    rate_ref[...], scale_ref[...] = band_terms(half_ref[...])
    lane = lanes_of(size)
    even = lax.rem(lax.axis_index("sector"), 2) == 0
    near = near_ref[...].astype(F32)
    far = far_ref[...].astype(F32)
    before = jnp.where(even, far, near)
    after = jnp.where(even, near, far)

    def keep(t, part, values):
        for s in range(shells // 2):
            first = (part * (shells // 2) + s) * PITCH
            wide_ref[t, first : first + row_count, :] = values[s * row_count : (s + 1) * row_count]

    for part in range(2):
        shell = slice(part * (shells // 2), (part + 1) * (shells // 2))
        previous = before if part == 0 else pltpu.roll(before, LANES - HMAX, 1)
        for t in range(tiles):
            turned = pltpu.roll(
                x_ref[shell, :, t * LANES : (t + 1) * LANES].reshape(size, LANES).astype(F32), HMAX, 1
            )
            keep(t, part, jnp.where(lane < HMAX, previous, turned))
            previous = turned
        edge = pltpu.roll(after, HMAX, 1) if part == 0 else after
        keep(tiles, part, jnp.where(lane < HMAX, previous, jnp.where(lane < 2 * HMAX, edge, 0.0)))
    depth = 2 * LANES
    offset = (lanes_of(depth) - lax.broadcasted_iota(jnp.int32, (depth, LANES), 0) + HMAX).astype(F32)
    square = offset * offset
    distance = jnp.abs(offset)

    def some_rows(block, carry):
        for u in range(UNROLL):
            i = block * UNROLL + u
            line = pl.ds(i, 1)
            band = jnp.where(distance <= half_ref[line, :], jnp.exp(-rate_ref[line, :] * square), 0.0)
            band = (band * scale_ref[line, :]).astype(BF16)
            values = [wide_ref[t, pl.ds(i, shells, stride=PITCH), :].astype(BF16) for t in range(tiles + 1)]
            stacked = jnp.concatenate(
                [jnp.concatenate(values[:tiles], axis=0), jnp.concatenate(values[1:], axis=0)], axis=1
            )
            result = jnp.dot(stacked, band, preferred_element_type=F32)
            for t in range(tiles):
                done_ref[t, pl.ds(i, shells, stride=PITCH), :] = result[t * shells : (t + 1) * shells]
        return carry

    lax.fori_loop(0, row_count // UNROLL, some_rows, 0)
    for t in range(tiles):
        for s in range(shells):
            out_ref[s, :, t * LANES : (t + 1) * LANES] = done_ref[t, s * PITCH : s * PITCH + row_count, :].astype(BF16)
    odd = lax.rem(zone, 2)
    last = row_count - LMAX
    near_rows_ref[...] = out_ref[:, pl.ds(pl.multiple_of((1 - odd) * last, LMAX), LMAX), :]
    far_rows_ref[...] = out_ref[:, pl.ds(pl.multiple_of(odd * last, LMAX), LMAX), :]


def hold_kernel(table_ref, x_ref, after_ref, out_ref, circle_ref):
    sectors, held, block, _ = x_ref.shape
    zone, sector = lax.axis_index("zone"), lax.axis_index("sector")
    polar = 2 * sectors * held
    cap = jnp.where(zone < 8, 0, sectors * held)
    length = sectors * block
    full_lon = length // PART * LANES
    depth = 3 * LANES
    for r in range(held):
        for copy in range(2):
            circle_ref[r, copy * length : (copy + 1) * length, :] = x_ref[:, r].reshape(length, LANES)
        circle_ref[r, 2 * length : 2 * length + 2 * PART, :] = circle_ref[r, 0 : 2 * PART, :]
    for r in range(held):
        entry = cap + sector * held + r
        half_f = jnp.full((1, LANES), table_ref[2 * polar + table_ref[entry]], jnp.int32).astype(F32)
        rate, scale = band_terms(half_f)
        start = lax.rem(2 * full_lon - table_ref[polar + entry] - HMAX, full_lon)
        first = start // LANES
        rest = start - first * LANES
        offset = (
            lanes_of(depth) - lax.broadcasted_iota(jnp.int32, (depth, LANES), 0) + (rest + HMAX)
        ).astype(F32)
        band = jnp.where(jnp.abs(offset) <= half_f, jnp.exp(-rate * (offset * offset)), 0.0) * scale
        values = jnp.concatenate(
            [circle_ref[r, pl.ds(pl.multiple_of((first + u) * PART, PART), length), :] for u in range(3)], axis=1
        )
        result = jnp.dot(values, band.astype(BF16), preferred_element_type=F32)
        out_ref[:, r] = result.astype(BF16).reshape(sectors, block, LANES)


def lat_kernel(rows_ref, near_ref, own_ref, far_ref, reach_ref, blend_ref,
               out_ref, polar_weight_ref, mix_ref, pick_ref):
    shells, row_count, col_count = own_ref.shape
    frame_rows = row_count + 2 * LMAX
    polar = pick_ref.shape[0]
    zone = lax.axis_index("zone")
    cap = jnp.where(zone < 8, 0, polar)
    lane = lanes_of(1)
    for p in range(polar):
        pick_ref[p : p + 1, :] = (lane == rows_ref[cap + p] - zone * row_count + LMAX).astype(F32)
    pick = pick_ref[...]
    zones = lax.axis_size("zone")
    reach = reach_ref[...]
    column = lax.broadcasted_iota(jnp.int32, (row_count, frame_rows), 1)
    away = column - LMAX - lax.broadcasted_iota(jnp.int32, (row_count, frame_rows), 0)
    source = zone * row_count - LMAX + column
    valid = (jnp.abs(away) <= reach) & (source >= 0) & (source < zones * row_count)
    reach_f = reach.astype(F32)
    away_f = away.astype(F32)
    weights = jnp.where(valid, jnp.exp(-(4.5 / (reach_f * reach_f)) * (away_f * away_f)), 0.0)
    weight = (weights / jnp.sum(weights, axis=1, keepdims=True)).astype(BF16)
    length = mix_ref.shape[0]
    group = length // shells
    spread = (
        lax.broadcasted_iota(jnp.int32, (length, shells), 0) // group
        == lax.broadcasted_iota(jnp.int32, (length, shells), 1)
    ).astype(F32).astype(BF16)
    tall = jnp.dot(spread, blend_ref[...], preferred_element_type=F32).astype(BF16)
    full = lax.dot_general(tall, spread, (((1,), (1,)), ((), ())), preferred_element_type=F32)
    same = (
        lax.broadcasted_iota(jnp.int32, (length, length), 0) % group
        == lax.broadcasted_iota(jnp.int32, (length, length), 1) % group
    )
    mix_ref[...] = jnp.where(same, full, 0.0).astype(BF16)
    polar_weight_ref[...] = lax.dot_general(
        weight, pick.astype(BF16), (((1,), (1,)), ((), ())), preferred_element_type=F32
    ).astype(BF16)
    rest = weight.astype(F32) * (1.0 - jnp.sum(pick, axis=0, keepdims=True))
    wide = lanes_of(row_count)
    turned = jnp.where(
        wide < LMAX,
        pltpu.roll(rest, LMAX, 1),
        jnp.where(wide < frame_rows - LMAX, rest, pltpu.roll(rest, frame_rows - LMAX, 1)),
    )
    rest = jnp.where(lax.rem(zone, 2) == 0, turned, rest).astype(BF16)

    for s in range(shells):
        values = jnp.concatenate([near_ref[s], own_ref[s], far_ref[s]], axis=0)
        out_ref[s] = jnp.dot(rest, values, preferred_element_type=F32)


def own_part():
    zone = lax.axis_index("zone")
    return jnp.where((zone == 0) | (zone == lax.axis_size("zone") - 1), 0, 1)


def add_polar(part, source_ref, weight_ref, lat_ref, polar_ref, sum_ref, sem, put):
    holders, held = source_ref.shape[:2]
    tiles = polar_ref.shape[0]
    polar = holders * held
    pitch = polar + 1
    fetch = pltpu.make_async_copy(lat_ref.at[pl.ds(part * PART, PART)], sum_ref, sem)
    fetch.start()
    for k in range(holders):
        for r in range(held):
            for t in range(tiles):
                polar_ref[t, pl.ds(k * held + r, PART, stride=pitch), :] = source_ref[
                    k, r, t * PART : (t + 1) * PART, :
                ].astype(F32)
    weight = weight_ref[...]
    fetch.wait()

    for s in range(PART):
        values = jnp.concatenate(
            [polar_ref[t, pl.ds(s * pitch, polar), :].astype(BF16) for t in range(tiles)], axis=1
        )
        put(s, sum_ref[s] + jnp.dot(weight, values, preferred_element_type=F32))


def own_kernel(mine_ref, weight_ref, lat_ref, out_ref, polar_ref, sum_ref, sem):
    def put(s, values):
        out_ref[s] = values.astype(BF16)

    add_polar(own_part(), mine_ref, weight_ref, lat_ref, polar_ref, sum_ref, sem, put)


def final_kernel(other_ref, own_ref, weight_ref, mix_ref, lat_ref, out_ref,
                 polar_ref, sum_ref, full_ref, stage_ref, sem, sems):
    shells, row_count, col_count = lat_ref.shape
    part = own_part()

    def put(s, values):
        full_ref[(1 - part) * PART + s] = values

    add_polar(1 - part, other_ref, weight_ref, lat_ref, polar_ref, sum_ref, sem, put)
    for s in range(PART):
        full_ref[part * PART + s] = own_ref[s].astype(F32)
    group = mix_ref.shape[0] // shells
    mix = mix_ref[...]
    stores = []
    for g in range(row_count // (2 * group)):
        mixed = []
        for e in range(2):
            first = (2 * g + e) * group
            values = full_ref[:, first : first + group, :].reshape(shells * group, col_count).astype(BF16)
            mixed.append(jnp.dot(mix, values, preferred_element_type=F32).reshape(shells, group, col_count))
        rows = pl.ds(2 * g * group, 2 * group)
        stage_ref[:, rows, :] = jnp.concatenate(mixed, axis=1).astype(BF16)
        stores.append(pltpu.make_async_copy(stage_ref.at[:, rows], out_ref.at[:, rows], sems.at[g]))
        stores[-1].start()
    for store in stores:
        store.wait()


def call(kernel, name, out_shape, scalars, arrays, scratch, flops=0, moved=0, direct=(), far=False, mib=16):
    smem = pl.BlockSpec(memory_space=pltpu.SMEM)
    vmem = pl.BlockSpec(memory_space=pltpu.VMEM)
    anywhere = pl.BlockSpec(memory_space=pl.ANY)
    many = isinstance(out_shape, tuple)
    return pl.pallas_call(
        kernel,
        out_shape=out_shape,
        in_specs=[smem] * len(scalars) + [vmem] * len(arrays) + [anywhere] * len(direct),
        out_specs=(vmem,) * len(out_shape) if many else anywhere if far else vmem,
        scratch_shapes=scratch,
        compiler_params=pltpu.CompilerParams(vmem_limit_bytes=mib << 20),
        cost_estimate=pl.CostEstimate(flops=flops, bytes_accessed=moved, transcendentals=0),
        name=name,
    )(*scalars, *arrays, *direct)


struct = jax.ShapeDtypeStruct


def pack(polar_rows, kernel, sectors):
    shells, row_count, col_count = kernel.shape
    tiles = col_count // LANES
    held = polar_rows.shape[0] // 2 // sectors
    edge = struct((shells * row_count // 2, LANES), BF16)
    parts = struct((sectors, held, tiles * PART, LANES), BF16)
    vmem = pl.BlockSpec(memory_space=pltpu.VMEM)
    anywhere = pl.BlockSpec(memory_space=pl.ANY)
    return pl.pallas_call(
        first_kernel,
        out_shape=(parts, edge, edge, parts),
        in_specs=[anywhere, anywhere],
        out_specs=(vmem, vmem, vmem, anywhere),
        scratch_shapes=[
            pltpu.VMEM((tiles, PART * PITCH, LANES), F32),
            pltpu.VMEM(kernel.shape, BF16),
            pltpu.VMEM(parts.shape, BF16),
            pltpu.SMEM(polar_rows.shape, jnp.int32),
            pltpu.SemaphoreType.DMA((4,)),
        ],
        compiler_params=pltpu.CompilerParams(vmem_limit_bytes=52 << 20),
        cost_estimate=pl.CostEstimate(flops=0, bytes_accessed=4 << 20, transcendentals=0),
        name="pack_polar_rows_and_edges",
    )(kernel, polar_rows)


def take_given(given, kept):
    anywhere = pl.BlockSpec(memory_space=pl.ANY)
    return pl.pallas_call(
        second_kernel,
        out_shape=struct(kept.shape, BF16),
        in_specs=[anywhere, anywhere],
        out_specs=anywhere,
        scratch_shapes=[pltpu.SemaphoreType.DMA],
        input_output_aliases={1: 0},
        compiler_params=pltpu.CompilerParams(vmem_limit_bytes=4 << 20),
        name="take_given",
    )(given, kept)


def smooth_lon(lon_halo, kernel, near, far):
    shells, row_count, col_count = kernel.shape
    tiles = col_count // LANES
    rows = pltpu.VMEM((row_count, LANES), F32)
    return call(
        lon_kernel,
        "smooth_along_longitude",
        (
            struct((shells, row_count, col_count), BF16),
            struct((shells, LMAX, col_count), BF16),
            struct((shells, LMAX, col_count), BF16),
        ),
        [lon_halo],
        [kernel, near, far],
        [
            pltpu.VMEM((tiles + 1, shells * PITCH, LANES), F32),
            pltpu.VMEM((tiles, shells * PITCH, LANES), F32),
            rows,
            rows,
            rows,
        ],
        flops=1 << 36,
        moved=16 << 20,
        mib=20,
    )


def hold(table, circles, after):
    sectors, held, block, _ = circles.shape
    return call(
        hold_kernel,
        "smooth_and_turn_polar_circles",
        struct(circles.shape, BF16),
        [table],
        [circles],
        [pltpu.VMEM((held, 2 * sectors * block + 2 * PART, LANES), BF16)],
        flops=1 << 30,
        moved=4 << 20,
        direct=[after],
    )


def smooth_lat(polar_rows, near, own, far, reach, blend):
    shells, row_count, _ = own.shape
    frame_rows = row_count + 2 * LMAX
    polar = polar_rows.shape[0] // 2
    return call(
        lat_kernel,
        "smooth_along_latitude",
        (
            struct(own.shape, F32),
            struct((row_count, polar), BF16),
            struct((shells * 8, shells * 8), BF16),
        ),
        [polar_rows],
        [near, own, far, reach, blend],
        [pltpu.VMEM((polar, frame_rows), F32)],
        flops=1 << 36,
        moved=8 << 20,
    )


def add_own(lat, mine, polar_weight):
    shells, row_count, col_count = lat.shape
    half = (PART, row_count, col_count)
    return call(
        own_kernel,
        "add_polar_rows_of_own_shells",
        struct(half, BF16),
        [],
        [mine, polar_weight],
        [
            pltpu.VMEM((col_count // LANES, PART * (polar_weight.shape[1] + 1), LANES), F32),
            pltpu.VMEM(half, F32),
            pltpu.SemaphoreType.DMA,
        ],
        flops=1 << 30,
        moved=4 << 20,
        direct=[lat],
        mib=50,
    )


def finish(lat, other, own, polar_weight, mix):
    shells, row_count, col_count = lat.shape
    return call(
        final_kernel,
        "add_polar_rows_and_blend",
        struct(lat.shape, BF16),
        [],
        [other, own, polar_weight, mix],
        [
            pltpu.VMEM((col_count // LANES, PART * (polar_weight.shape[1] + 1), LANES), F32),
            pltpu.VMEM((PART, row_count, col_count), F32),
            pltpu.VMEM(lat.shape, F32),
            pltpu.VMEM(lat.shape, BF16),
            pltpu.SemaphoreType.DMA,
            pltpu.SemaphoreType.DMA((4,)),
        ],
        flops=1 << 31,
        moved=8 << 20,
        far=True,
        direct=[lat],
        mib=50,
    )


def per_device(kernel, lon_halo, lat_reach, polar_rows, polar_shift, blend):
    shells, row_count, col_count = kernel.shape
    sectors = lax.axis_size("sector")
    zones = lax.axis_size("zone")
    last = zones - 1
    packed, near, far, kept = pack(polar_rows, kernel, sectors)
    given = lax.ppermute(packed, "zone", [(0, 1), (last, last - 1)])
    far = lax.ppermute(far, "sector", [(i, (i + 1 if i % 2 else i - 1) % sectors) for i in range(sectors)])
    near = lax.ppermute(near, "sector", [(i, i ^ 1) for i in range(sectors)])
    parts = take_given(given, kept)
    circles = lax.all_to_all(parts, "sector", 0, 0, tiled=True)
    lon_smooth, near_rows, far_rows = smooth_lon(lon_halo, kernel, near, far)
    turned = hold(jnp.concatenate([polar_rows, polar_shift, lon_halo]), circles, far_rows)
    far_rows = lax.ppermute(
        far_rows, "zone", [(i, i + 1 if i % 2 else i - 1) for i in range(1, zones - 1)]
    )
    near_rows = lax.ppermute(near_rows, "zone", [(i, i ^ 1) for i in range(zones)])
    mine = lax.all_to_all(turned, "sector", 0, 0, tiled=True)
    lat, polar_weight, mix = smooth_lat(
        polar_rows, near_rows, lon_smooth, far_rows, lat_reach[:, None], blend
    )
    mine, lat = lax.optimization_barrier((mine, lat))
    other = lax.ppermute(mine, "zone", [(0, 1), (1, 0), (last, last - 1), (last - 1, last)])
    own = add_own(lat, mine, polar_weight)
    return finish(lat, other, own, polar_weight, mix)


def solution(mesh):
    in_specs = (P(None, "zone", "sector"), P(), P("zone"), P(), P(), P())
    out_specs = P(None, "zone", "sector")
    return jax.shard_map(
        per_device, mesh=mesh, in_specs=in_specs, out_specs=out_specs, check_vma=False
    )
```

```python
import jax
import jax.numpy as jnp
from jax import lax
from jax.experimental import pallas as pl
from jax.experimental.pallas import tpu as pltpu
from jax.sharding import PartitionSpec as P

HMAX = 48
LMAX = 32
LANES = 128
PART = 16
UNROLL = 16
PITCH = 65
F32 = jnp.float32
BF16 = jnp.bfloat16


def lanes_of(rows):
    return lax.broadcasted_iota(jnp.int32, (rows, LANES), 1)


def write_edges(x_ref, near_ref, far_ref):
    shells, row_count, col_count = x_ref.shape
    half = shells // 2
    size = half * row_count
    lane = lanes_of(size)

    def part(column, shell):
        return x_ref[shell : shell + half, :, column : column + LANES].reshape(size, LANES).astype(F32)

    last = col_count - LANES
    even = lax.rem(lax.axis_index("sector"), 2) == 0
    low = jnp.where(lane < HMAX, part(0, 0), pltpu.roll(part(0, half), HMAX, 1))
    high = jnp.where(lane < HMAX, pltpu.roll(part(last, 0), HMAX, 1), pltpu.roll(part(last, half), 2 * HMAX, 1))
    near_ref[...] = jnp.where(even, high, low).astype(BF16)
    far_ref[...] = jnp.where(even, low, high).astype(BF16)


def write_polar(half, rows_ref, x_ref, send_ref, wide_ref):
    _, row_count, col_count = x_ref.shape
    tiles = col_count // LANES
    zone = lax.axis_index("zone")
    for t in range(tiles):
        for s in range(PART):
            wide_ref[t, s * PITCH : s * PITCH + row_count, :] = x_ref[
                half * PART + s, :, t * LANES : (t + 1) * LANES
            ].astype(F32)
    holders, held = send_ref.shape[0], send_ref.shape[1]
    cap = jnp.where(zone < 8, 0, holders * held)
    for k in range(holders):
        for r in range(held):
            row = jnp.clip(rows_ref[cap + k * held + r] - zone * row_count, 0, row_count - 1)
            for t in range(tiles):
                values = wide_ref[t, pl.ds(row, PART, stride=PITCH), :]
                send_ref[k, r, t * PART : (t + 1) * PART, :] = values.astype(BF16)


def first_kernel(x_ref, far_rows_ref, send_ref, near_ref, far_ref, kept_ref,
                 wide_ref, held_ref, stage_ref, rows_ref, sems):
    fetch = pltpu.make_async_copy(far_rows_ref, rows_ref, sems.at[2])
    fetch.start()
    copies = []
    for half in (0, 1):
        shells = pl.ds(half * PART, PART)
        copies.append(pltpu.make_async_copy(x_ref.at[shells], held_ref.at[shells], sems.at[half]))
        copies[-1].start()
    fetch.wait()
    copies[0].wait()
    write_polar(0, rows_ref, held_ref, stage_ref, wide_ref)
    store = pltpu.make_async_copy(stage_ref, kept_ref, sems.at[3])
    store.start()
    copies[1].wait()
    write_polar(1, rows_ref, held_ref, send_ref, wide_ref)
    write_edges(held_ref, near_ref, far_ref)
    store.wait()


def second_kernel(given_ref, kept_ref, out_ref, sem):
    zone = lax.axis_index("zone")

    @pl.when((zone == 1) | (zone == lax.axis_size("zone") - 2))
    def _():
        copy = pltpu.make_async_copy(given_ref, out_ref, sem)
        copy.start()
        copy.wait()


def band_terms(half_f):
    rate = 4.5 / (half_f * half_f)
    tap = (lanes_of(half_f.shape[0]) - HMAX).astype(F32)
    terms = jnp.where(jnp.abs(tap) <= half_f, jnp.exp(-rate * (tap * tap)), 0.0)
    return rate, jnp.broadcast_to(1.0 / jnp.sum(terms, axis=1, keepdims=True), half_f.shape)


def lon_kernel(halo_ref, x_ref, near_ref, far_ref,
               out_ref, near_rows_ref, far_rows_ref, wide_ref, done_ref, half_ref, rate_ref, scale_ref):
    shells, row_count, col_count = x_ref.shape
    total = shells * row_count
    size = total // 2
    tiles = col_count // LANES
    zone = lax.axis_index("zone")
    for i in range(row_count):
        half_ref[i : i + 1, :] = jnp.full((1, LANES), halo_ref[zone * row_count + i], jnp.int32).astype(F32)
    rate_ref[...], scale_ref[...] = band_terms(half_ref[...])
    lane = lanes_of(size)
    even = lax.rem(lax.axis_index("sector"), 2) == 0
    near = near_ref[...].astype(F32)
    far = far_ref[...].astype(F32)
    before = jnp.where(even, far, near)
    after = jnp.where(even, near, far)

    def keep(t, part, values):
        for s in range(shells // 2):
            first = (part * (shells // 2) + s) * PITCH
            wide_ref[t, first : first + row_count, :] = values[s * row_count : (s + 1) * row_count]

    for part in range(2):
        shell = slice(part * (shells // 2), (part + 1) * (shells // 2))
        previous = before if part == 0 else pltpu.roll(before, LANES - HMAX, 1)
        for t in range(tiles):
            turned = pltpu.roll(
                x_ref[shell, :, t * LANES : (t + 1) * LANES].reshape(size, LANES).astype(F32), HMAX, 1
            )
            keep(t, part, jnp.where(lane < HMAX, previous, turned))
            previous = turned
        edge = pltpu.roll(after, HMAX, 1) if part == 0 else after
        keep(tiles, part, jnp.where(lane < HMAX, previous, jnp.where(lane < 2 * HMAX, edge, 0.0)))
    depth = 2 * LANES
    offset = (lanes_of(depth) - lax.broadcasted_iota(jnp.int32, (depth, LANES), 0) + HMAX).astype(F32)
    square = offset * offset
    distance = jnp.abs(offset)

    def some_rows(block, carry):
        for u in range(UNROLL):
            i = block * UNROLL + u
            line = pl.ds(i, 1)
            band = jnp.where(distance <= half_ref[line, :], jnp.exp(-rate_ref[line, :] * square), 0.0)
            band = (band * scale_ref[line, :]).astype(BF16)
            values = [wide_ref[t, pl.ds(i, shells, stride=PITCH), :].astype(BF16) for t in range(tiles + 1)]
            stacked = jnp.concatenate(
                [jnp.concatenate(values[:tiles], axis=0), jnp.concatenate(values[1:], axis=0)], axis=1
            )
            result = jnp.dot(stacked, band, preferred_element_type=F32)
            for t in range(tiles):
                done_ref[t, pl.ds(i, shells, stride=PITCH), :] = result[t * shells : (t + 1) * shells]
        return carry

    lax.fori_loop(0, row_count // UNROLL, some_rows, 0)
    for t in range(tiles):
        for s in range(shells):
            out_ref[s, :, t * LANES : (t + 1) * LANES] = done_ref[t, s * PITCH : s * PITCH + row_count, :].astype(BF16)
    odd = lax.rem(zone, 2)
    last = row_count - LMAX
    near_rows_ref[...] = out_ref[:, pl.ds(pl.multiple_of((1 - odd) * last, LMAX), LMAX), :]
    far_rows_ref[...] = out_ref[:, pl.ds(pl.multiple_of(odd * last, LMAX), LMAX), :]


def hold_kernel(table_ref, x_ref, after_ref, out_ref, circle_ref):
    sectors, held, block, _ = x_ref.shape
    zone, sector = lax.axis_index("zone"), lax.axis_index("sector")
    polar = 2 * sectors * held
    cap = jnp.where(zone < 8, 0, sectors * held)
    length = sectors * block
    full_lon = length // PART * LANES
    depth = 3 * LANES
    for r in range(held):
        for copy in range(2):
            circle_ref[r, copy * length : (copy + 1) * length, :] = x_ref[:, r].reshape(length, LANES)
        circle_ref[r, 2 * length : 2 * length + 2 * PART, :] = circle_ref[r, 0 : 2 * PART, :]
    for r in range(held):
        entry = cap + sector * held + r
        half_f = jnp.full((1, LANES), table_ref[2 * polar + table_ref[entry]], jnp.int32).astype(F32)
        rate, scale = band_terms(half_f)
        start = lax.rem(2 * full_lon - table_ref[polar + entry] - HMAX, full_lon)
        first = start // LANES
        rest = start - first * LANES
        offset = (
            lanes_of(depth) - lax.broadcasted_iota(jnp.int32, (depth, LANES), 0) + (rest + HMAX)
        ).astype(F32)
        band = jnp.where(jnp.abs(offset) <= half_f, jnp.exp(-rate * (offset * offset)), 0.0) * scale
        values = jnp.concatenate(
            [circle_ref[r, pl.ds(pl.multiple_of((first + u) * PART, PART), length), :] for u in range(3)], axis=1
        )
        result = jnp.dot(values, band.astype(BF16), preferred_element_type=F32)
        out_ref[:, r] = result.astype(BF16).reshape(sectors, block, LANES)


def lat_kernel(rows_ref, near_ref, own_ref, far_ref, reach_ref, blend_ref,
               out_ref, polar_weight_ref, mix_ref, pick_ref):
    shells, row_count, col_count = own_ref.shape
    frame_rows = row_count + 2 * LMAX
    polar = pick_ref.shape[0]
    zone = lax.axis_index("zone")
    cap = jnp.where(zone < 8, 0, polar)
    lane = lanes_of(1)
    for p in range(polar):
        pick_ref[p : p + 1, :] = (lane == rows_ref[cap + p] - zone * row_count + LMAX).astype(F32)
    pick = pick_ref[...]
    zones = lax.axis_size("zone")
    reach = reach_ref[...]
    column = lax.broadcasted_iota(jnp.int32, (row_count, frame_rows), 1)
    away = column - LMAX - lax.broadcasted_iota(jnp.int32, (row_count, frame_rows), 0)
    source = zone * row_count - LMAX + column
    valid = (jnp.abs(away) <= reach) & (source >= 0) & (source < zones * row_count)
    reach_f = reach.astype(F32)
    away_f = away.astype(F32)
    weights = jnp.where(valid, jnp.exp(-(4.5 / (reach_f * reach_f)) * (away_f * away_f)), 0.0)
    weight = (weights / jnp.sum(weights, axis=1, keepdims=True)).astype(BF16)
    length = mix_ref.shape[0]
    group = length // shells
    spread = (
        lax.broadcasted_iota(jnp.int32, (length, shells), 0) // group
        == lax.broadcasted_iota(jnp.int32, (length, shells), 1)
    ).astype(F32).astype(BF16)
    tall = jnp.dot(spread, blend_ref[...], preferred_element_type=F32).astype(BF16)
    full = lax.dot_general(tall, spread, (((1,), (1,)), ((), ())), preferred_element_type=F32)
    same = (
        lax.broadcasted_iota(jnp.int32, (length, length), 0) % group
        == lax.broadcasted_iota(jnp.int32, (length, length), 1) % group
    )
    mix_ref[...] = jnp.where(same, full, 0.0).astype(BF16)
    polar_weight_ref[...] = lax.dot_general(
        weight, pick.astype(BF16), (((1,), (1,)), ((), ())), preferred_element_type=F32
    ).astype(BF16)
    rest = weight.astype(F32) * (1.0 - jnp.sum(pick, axis=0, keepdims=True))
    wide = lanes_of(row_count)
    turned = jnp.where(
        wide < LMAX,
        pltpu.roll(rest, LMAX, 1),
        jnp.where(wide < frame_rows - LMAX, rest, pltpu.roll(rest, frame_rows - LMAX, 1)),
    )
    rest = jnp.where(lax.rem(zone, 2) == 0, turned, rest).astype(BF16)

    for s in range(shells):
        values = jnp.concatenate([near_ref[s], own_ref[s], far_ref[s]], axis=0)
        out_ref[s] = jnp.dot(rest, values, preferred_element_type=F32)


def own_part():
    zone = lax.axis_index("zone")
    return jnp.where((zone == 0) | (zone == lax.axis_size("zone") - 1), 0, 1)


def add_polar(part, source_ref, weight_ref, lat_ref, polar_ref, sum_ref, sem, put):
    holders, held = source_ref.shape[:2]
    tiles = polar_ref.shape[0]
    polar = holders * held
    pitch = polar + 1
    fetch = pltpu.make_async_copy(lat_ref.at[pl.ds(part * PART, PART)], sum_ref, sem)
    fetch.start()
    for k in range(holders):
        for r in range(held):
            for t in range(tiles):
                polar_ref[t, pl.ds(k * held + r, PART, stride=pitch), :] = source_ref[
                    k, r, t * PART : (t + 1) * PART, :
                ].astype(F32)
    weight = weight_ref[...]
    fetch.wait()

    for s in range(PART):
        values = jnp.concatenate(
            [polar_ref[t, pl.ds(s * pitch, polar), :].astype(BF16) for t in range(tiles)], axis=1
        )
        put(s, sum_ref[s] + jnp.dot(weight, values, preferred_element_type=F32))


def own_kernel(mine_ref, weight_ref, lat_ref, out_ref, polar_ref, sum_ref, sem):
    def put(s, values):
        out_ref[s] = values.astype(BF16)

    add_polar(own_part(), mine_ref, weight_ref, lat_ref, polar_ref, sum_ref, sem, put)


def final_kernel(other_ref, own_ref, weight_ref, mix_ref, lat_ref, out_ref,
                 polar_ref, sum_ref, full_ref, stage_ref, sem, sems):
    shells, row_count, col_count = lat_ref.shape
    part = own_part()

    def put(s, values):
        full_ref[(1 - part) * PART + s] = values

    add_polar(1 - part, other_ref, weight_ref, lat_ref, polar_ref, sum_ref, sem, put)
    for s in range(PART):
        full_ref[part * PART + s] = own_ref[s].astype(F32)
    group = mix_ref.shape[0] // shells
    mix = mix_ref[...]
    stores = []
    for g in range(row_count // (2 * group)):
        mixed = []
        for e in range(2):
            first = (2 * g + e) * group
            values = full_ref[:, first : first + group, :].reshape(shells * group, col_count).astype(BF16)
            mixed.append(jnp.dot(mix, values, preferred_element_type=F32).reshape(shells, group, col_count))
        rows = pl.ds(2 * g * group, 2 * group)
        stage_ref[:, rows, :] = jnp.concatenate(mixed, axis=1).astype(BF16)
        stores.append(pltpu.make_async_copy(stage_ref.at[:, rows], out_ref.at[:, rows], sems.at[g]))
        stores[-1].start()
    for store in stores:
        store.wait()


def call(kernel, name, out_shape, scalars, arrays, scratch, flops=0, moved=0, direct=(), far=False, mib=16):
    smem = pl.BlockSpec(memory_space=pltpu.SMEM)
    vmem = pl.BlockSpec(memory_space=pltpu.VMEM)
    anywhere = pl.BlockSpec(memory_space=pl.ANY)
    many = isinstance(out_shape, tuple)
    return pl.pallas_call(
        kernel,
        out_shape=out_shape,
        in_specs=[smem] * len(scalars) + [vmem] * len(arrays) + [anywhere] * len(direct),
        out_specs=(vmem,) * len(out_shape) if many else anywhere if far else vmem,
        scratch_shapes=scratch,
        compiler_params=pltpu.CompilerParams(vmem_limit_bytes=mib << 20),
        cost_estimate=pl.CostEstimate(flops=flops, bytes_accessed=moved, transcendentals=0),
        name=name,
    )(*scalars, *arrays, *direct)


struct = jax.ShapeDtypeStruct


def pack(polar_rows, kernel, sectors):
    shells, row_count, col_count = kernel.shape
    tiles = col_count // LANES
    held = polar_rows.shape[0] // 2 // sectors
    edge = struct((shells * row_count // 2, LANES), BF16)
    parts = struct((sectors, held, tiles * PART, LANES), BF16)
    vmem = pl.BlockSpec(memory_space=pltpu.VMEM)
    anywhere = pl.BlockSpec(memory_space=pl.ANY)
    return pl.pallas_call(
        first_kernel,
        out_shape=(parts, edge, edge, parts),
        in_specs=[anywhere, anywhere],
        out_specs=(vmem, vmem, vmem, anywhere),
        scratch_shapes=[
            pltpu.VMEM((tiles, PART * PITCH, LANES), F32),
            pltpu.VMEM(kernel.shape, BF16),
            pltpu.VMEM(parts.shape, BF16),
            pltpu.SMEM(polar_rows.shape, jnp.int32),
            pltpu.SemaphoreType.DMA((4,)),
        ],
        compiler_params=pltpu.CompilerParams(vmem_limit_bytes=52 << 20),
        cost_estimate=pl.CostEstimate(flops=0, bytes_accessed=4 << 20, transcendentals=0),
        name="pack_polar_rows_and_edges",
    )(kernel, polar_rows)


def take_given(given, kept):
    anywhere = pl.BlockSpec(memory_space=pl.ANY)
    return pl.pallas_call(
        second_kernel,
        out_shape=struct(kept.shape, BF16),
        in_specs=[anywhere, anywhere],
        out_specs=anywhere,
        scratch_shapes=[pltpu.SemaphoreType.DMA],
        input_output_aliases={1: 0},
        compiler_params=pltpu.CompilerParams(vmem_limit_bytes=4 << 20),
        name="take_given",
    )(given, kept)


def smooth_lon(lon_halo, kernel, near, far):
    shells, row_count, col_count = kernel.shape
    tiles = col_count // LANES
    rows = pltpu.VMEM((row_count, LANES), F32)
    return call(
        lon_kernel,
        "smooth_along_longitude",
        (
            struct((shells, row_count, col_count), BF16),
            struct((shells, LMAX, col_count), BF16),
            struct((shells, LMAX, col_count), BF16),
        ),
        [lon_halo],
        [kernel, near, far],
        [
            pltpu.VMEM((tiles + 1, shells * PITCH, LANES), F32),
            pltpu.VMEM((tiles, shells * PITCH, LANES), F32),
            rows,
            rows,
            rows,
        ],
        flops=1 << 36,
        moved=16 << 20,
        mib=20,
    )


def hold(table, circles, after):
    sectors, held, block, _ = circles.shape
    return call(
        hold_kernel,
        "smooth_and_turn_polar_circles",
        struct(circles.shape, BF16),
        [table],
        [circles],
        [pltpu.VMEM((held, 2 * sectors * block + 2 * PART, LANES), BF16)],
        flops=1 << 30,
        moved=4 << 20,
        direct=[after],
    )


def smooth_lat(polar_rows, near, own, far, reach, blend):
    shells, row_count, _ = own.shape
    frame_rows = row_count + 2 * LMAX
    polar = polar_rows.shape[0] // 2
    return call(
        lat_kernel,
        "smooth_along_latitude",
        (
            struct(own.shape, F32),
            struct((row_count, polar), BF16),
            struct((shells * 8, shells * 8), BF16),
        ),
        [polar_rows],
        [near, own, far, reach, blend],
        [pltpu.VMEM((polar, frame_rows), F32)],
        flops=1 << 36,
        moved=8 << 20,
    )


def add_own(lat, mine, polar_weight):
    shells, row_count, col_count = lat.shape
    half = (PART, row_count, col_count)
    return call(
        own_kernel,
        "add_polar_rows_of_own_shells",
        struct(half, BF16),
        [],
        [mine, polar_weight],
        [
            pltpu.VMEM((col_count // LANES, PART * (polar_weight.shape[1] + 1), LANES), F32),
            pltpu.VMEM(half, F32),
            pltpu.SemaphoreType.DMA,
        ],
        flops=1 << 30,
        moved=4 << 20,
        direct=[lat],
        mib=50,
    )


def finish(lat, other, own, polar_weight, mix):
    shells, row_count, col_count = lat.shape
    return call(
        final_kernel,
        "add_polar_rows_and_blend",
        struct(lat.shape, BF16),
        [],
        [other, own, polar_weight, mix],
        [
            pltpu.VMEM((col_count // LANES, PART * (polar_weight.shape[1] + 1), LANES), F32),
            pltpu.VMEM((PART, row_count, col_count), F32),
            pltpu.VMEM(lat.shape, F32),
            pltpu.VMEM(lat.shape, BF16),
            pltpu.SemaphoreType.DMA,
            pltpu.SemaphoreType.DMA((4,)),
        ],
        flops=1 << 31,
        moved=8 << 20,
        far=True,
        direct=[lat],
        mib=50,
    )


def per_device(kernel, lon_halo, lat_reach, polar_rows, polar_shift, blend):
    shells, row_count, col_count = kernel.shape
    sectors = lax.axis_size("sector")
    zones = lax.axis_size("zone")
    last = zones - 1
    packed, near, far, kept = pack(polar_rows, kernel, sectors)
    given = lax.ppermute(packed, "zone", [(0, 1), (last, last - 1)])
    far = lax.ppermute(far, "sector", [(i, (i + 1 if i % 2 else i - 1) % sectors) for i in range(sectors)])
    near = lax.ppermute(near, "sector", [(i, i ^ 1) for i in range(sectors)])
    parts = take_given(given, kept)
    circles = lax.all_to_all(parts, "sector", 0, 0, tiled=True)
    lon_smooth, near_rows, far_rows = smooth_lon(lon_halo, kernel, near, far)
    turned = hold(jnp.concatenate([polar_rows, polar_shift, lon_halo]), circles, far_rows)
    far_rows = lax.ppermute(
        far_rows, "zone", [(i, i + 1 if i % 2 else i - 1) for i in range(1, zones - 1)]
    )
    near_rows = lax.ppermute(near_rows, "zone", [(i, i ^ 1) for i in range(zones)])
    mine = lax.all_to_all(turned, "sector", 0, 0, tiled=True)
    lat, polar_weight, mix = smooth_lat(
        polar_rows, near_rows, lon_smooth, far_rows, lat_reach[:, None], blend
    )
    mine, lat = lax.optimization_barrier((mine, lat))
    other = lax.ppermute(mine, "zone", [(0, 1), (1, 0), (last, last - 1), (last - 1, last)])
    own = add_own(lat, mine, polar_weight)
    return finish(lat, other, own, polar_weight, mix)


def solution(mesh):
    in_specs = (P(None, "zone", "sector"), P(), P("zone"), P(), P(), P())
    out_specs = P(None, "zone", "sector")
    return jax.shard_map(
        per_device, mesh=mesh, in_specs=in_specs, out_specs=out_specs, check_vma=False
    )
```

```python
import jax
import jax.numpy as jnp
from jax import lax
from jax.experimental import pallas as pl
from jax.experimental.pallas import tpu as pltpu
from jax.sharding import PartitionSpec as P

HMAX = 48
LMAX = 32
LANES = 128
PART = 16
UNROLL = 16
PITCH = 65
F32 = jnp.float32
BF16 = jnp.bfloat16


def lanes_of(rows):
    return lax.broadcasted_iota(jnp.int32, (rows, LANES), 1)


def write_edges(x_ref, near_ref, far_ref):
    shells, row_count, col_count = x_ref.shape
    half = shells // 2
    size = half * row_count
    lane = lanes_of(size)

    def part(column, shell):
        return x_ref[shell : shell + half, :, column : column + LANES].reshape(size, LANES).astype(F32)

    last = col_count - LANES
    even = lax.rem(lax.axis_index("sector"), 2) == 0
    low = jnp.where(lane < HMAX, part(0, 0), pltpu.roll(part(0, half), HMAX, 1))
    high = jnp.where(lane < HMAX, pltpu.roll(part(last, 0), HMAX, 1), pltpu.roll(part(last, half), 2 * HMAX, 1))
    near_ref[...] = jnp.where(even, high, low).astype(BF16)
    far_ref[...] = jnp.where(even, low, high).astype(BF16)


def write_polar(half, rows_ref, x_ref, send_ref, wide_ref):
    _, row_count, col_count = x_ref.shape
    tiles = col_count // LANES
    zone = lax.axis_index("zone")
    for t in range(tiles):
        for s in range(PART):
            wide_ref[t, s * PITCH : s * PITCH + row_count, :] = x_ref[
                half * PART + s, :, t * LANES : (t + 1) * LANES
            ].astype(F32)
    holders, held = send_ref.shape[0], send_ref.shape[1]
    cap = jnp.where(zone < 8, 0, holders * held)
    for k in range(holders):
        for r in range(held):
            row = jnp.clip(rows_ref[cap + k * held + r] - zone * row_count, 0, row_count - 1)
            for t in range(tiles):
                values = wide_ref[t, pl.ds(row, PART, stride=PITCH), :]
                send_ref[k, r, t * PART : (t + 1) * PART, :] = values.astype(BF16)


def first_kernel(x_ref, far_rows_ref, send_ref, near_ref, far_ref, kept_ref,
                 wide_ref, held_ref, stage_ref, rows_ref, sems):
    fetch = pltpu.make_async_copy(far_rows_ref, rows_ref, sems.at[2])
    fetch.start()
    copies = []
    for half in (0, 1):
        shells = pl.ds(half * PART, PART)
        copies.append(pltpu.make_async_copy(x_ref.at[shells], held_ref.at[shells], sems.at[half]))
        copies[-1].start()
    fetch.wait()
    copies[0].wait()
    write_polar(0, rows_ref, held_ref, stage_ref, wide_ref)
    store = pltpu.make_async_copy(stage_ref, kept_ref, sems.at[3])
    store.start()
    copies[1].wait()
    write_polar(1, rows_ref, held_ref, send_ref, wide_ref)
    write_edges(held_ref, near_ref, far_ref)
    store.wait()


def second_kernel(given_ref, kept_ref, out_ref, sem):
    zone = lax.axis_index("zone")

    @pl.when((zone == 1) | (zone == lax.axis_size("zone") - 2))
    def _():
        copy = pltpu.make_async_copy(given_ref, out_ref, sem)
        copy.start()
        copy.wait()


def band_terms(half_f):
    rate = 4.5 / (half_f * half_f)
    tap = (lanes_of(half_f.shape[0]) - HMAX).astype(F32)
    terms = jnp.where(jnp.abs(tap) <= half_f, jnp.exp(-rate * (tap * tap)), 0.0)
    return rate, jnp.broadcast_to(1.0 / jnp.sum(terms, axis=1, keepdims=True), half_f.shape)


def lon_kernel(halo_ref, x_ref, near_ref, far_ref,
               out_ref, near_rows_ref, far_rows_ref, wide_ref, done_ref, half_ref, rate_ref, scale_ref):
    shells, row_count, col_count = x_ref.shape
    total = shells * row_count
    size = total // 2
    tiles = col_count // LANES
    zone = lax.axis_index("zone")
    for i in range(row_count):
        half_ref[i : i + 1, :] = jnp.full((1, LANES), halo_ref[zone * row_count + i], jnp.int32).astype(F32)
    rate_ref[...], scale_ref[...] = band_terms(half_ref[...])
    lane = lanes_of(size)
    even = lax.rem(lax.axis_index("sector"), 2) == 0
    near = near_ref[...].astype(F32)
    far = far_ref[...].astype(F32)
    before = jnp.where(even, far, near)
    after = jnp.where(even, near, far)

    def keep(t, part, values):
        for s in range(shells // 2):
            first = (part * (shells // 2) + s) * PITCH
            wide_ref[t, first : first + row_count, :] = values[s * row_count : (s + 1) * row_count]

    for part in range(2):
        shell = slice(part * (shells // 2), (part + 1) * (shells // 2))
        previous = before if part == 0 else pltpu.roll(before, LANES - HMAX, 1)
        for t in range(tiles):
            turned = pltpu.roll(
                x_ref[shell, :, t * LANES : (t + 1) * LANES].reshape(size, LANES).astype(F32), HMAX, 1
            )
            keep(t, part, jnp.where(lane < HMAX, previous, turned))
            previous = turned
        edge = pltpu.roll(after, HMAX, 1) if part == 0 else after
        keep(tiles, part, jnp.where(lane < HMAX, previous, jnp.where(lane < 2 * HMAX, edge, 0.0)))
    depth = 2 * LANES
    offset = (lanes_of(depth) - lax.broadcasted_iota(jnp.int32, (depth, LANES), 0) + HMAX).astype(F32)
    square = offset * offset
    distance = jnp.abs(offset)

    def some_rows(block, carry):
        for u in range(UNROLL):
            i = block * UNROLL + u
            line = pl.ds(i, 1)
            band = jnp.where(distance <= half_ref[line, :], jnp.exp(-rate_ref[line, :] * square), 0.0)
            band = (band * scale_ref[line, :]).astype(BF16)
            values = [wide_ref[t, pl.ds(i, shells, stride=PITCH), :].astype(BF16) for t in range(tiles + 1)]
            stacked = jnp.concatenate(
                [jnp.concatenate(values[:tiles], axis=0), jnp.concatenate(values[1:], axis=0)], axis=1
            )
            result = jnp.dot(stacked, band, preferred_element_type=F32)
            for t in range(tiles):
                done_ref[t, pl.ds(i, shells, stride=PITCH), :] = result[t * shells : (t + 1) * shells]
        return carry

    lax.fori_loop(0, row_count // UNROLL, some_rows, 0)
    for t in range(tiles):
        for s in range(shells):
            out_ref[s, :, t * LANES : (t + 1) * LANES] = done_ref[t, s * PITCH : s * PITCH + row_count, :].astype(BF16)
    odd = lax.rem(zone, 2)
    last = row_count - LMAX
    near_rows_ref[...] = out_ref[:, pl.ds(pl.multiple_of((1 - odd) * last, LMAX), LMAX), :]
    far_rows_ref[...] = out_ref[:, pl.ds(pl.multiple_of(odd * last, LMAX), LMAX), :]


def hold_kernel(table_ref, x_ref, after_ref, out_ref, circle_ref, stage_ref, sems):
    sectors, held, block, _ = x_ref.shape
    zone, sector = lax.axis_index("zone"), lax.axis_index("sector")
    polar = 2 * sectors * held
    cap = jnp.where(zone < 8, 0, sectors * held)
    length = sectors * block
    full_lon = length // PART * LANES
    depth = 3 * LANES
    for r in range(held):
        for copy in range(2):
            circle_ref[r, copy * length : (copy + 1) * length, :] = x_ref[:, r].reshape(length, LANES)
        circle_ref[r, 2 * length : 2 * length + 2 * PART, :] = circle_ref[r, 0 : 2 * PART, :]
    stores = []
    for r in range(held):
        entry = cap + sector * held + r
        half_f = jnp.full((1, LANES), table_ref[2 * polar + table_ref[entry]], jnp.int32).astype(F32)
        rate, scale = band_terms(half_f)
        start = lax.rem(2 * full_lon - table_ref[polar + entry] - HMAX, full_lon)
        first = start // LANES
        rest = start - first * LANES
        offset = (
            lanes_of(depth) - lax.broadcasted_iota(jnp.int32, (depth, LANES), 0) + (rest + HMAX)
        ).astype(F32)
        band = jnp.where(jnp.abs(offset) <= half_f, jnp.exp(-rate * (offset * offset)), 0.0) * scale
        values = jnp.concatenate(
            [circle_ref[r, pl.ds(pl.multiple_of((first + u) * PART, PART), length), :] for u in range(3)], axis=1
        )
        result = jnp.dot(values, band.astype(BF16), preferred_element_type=F32)
        stage_ref[r] = result.astype(BF16).reshape(sectors, block, LANES)
        stores.append(pltpu.make_async_copy(stage_ref.at[r], out_ref.at[:, r], sems.at[r]))
        stores[-1].start()
    for store in stores:
        store.wait()


def lat_kernel(rows_ref, near_ref, own_ref, far_ref, reach_ref, blend_ref,
               out_ref, polar_weight_ref, mix_ref, pick_ref):
    shells, row_count, col_count = own_ref.shape
    frame_rows = row_count + 2 * LMAX
    polar = pick_ref.shape[0]
    zone = lax.axis_index("zone")
    cap = jnp.where(zone < 8, 0, polar)
    lane = lanes_of(1)
    for p in range(polar):
        pick_ref[p : p + 1, :] = (lane == rows_ref[cap + p] - zone * row_count + LMAX).astype(F32)
    pick = pick_ref[...]
    zones = lax.axis_size("zone")
    reach = reach_ref[...]
    column = lax.broadcasted_iota(jnp.int32, (row_count, frame_rows), 1)
    away = column - LMAX - lax.broadcasted_iota(jnp.int32, (row_count, frame_rows), 0)
    source = zone * row_count - LMAX + column
    valid = (jnp.abs(away) <= reach) & (source >= 0) & (source < zones * row_count)
    reach_f = reach.astype(F32)
    away_f = away.astype(F32)
    weights = jnp.where(valid, jnp.exp(-(4.5 / (reach_f * reach_f)) * (away_f * away_f)), 0.0)
    weight = (weights / jnp.sum(weights, axis=1, keepdims=True)).astype(BF16)
    length = mix_ref.shape[0]
    group = length // shells
    spread = (
        lax.broadcasted_iota(jnp.int32, (length, shells), 0) // group
        == lax.broadcasted_iota(jnp.int32, (length, shells), 1)
    ).astype(F32).astype(BF16)
    tall = jnp.dot(spread, blend_ref[...], preferred_element_type=F32).astype(BF16)
    full = lax.dot_general(tall, spread, (((1,), (1,)), ((), ())), preferred_element_type=F32)
    same = (
        lax.broadcasted_iota(jnp.int32, (length, length), 0) % group
        == lax.broadcasted_iota(jnp.int32, (length, length), 1) % group
    )
    mix_ref[...] = jnp.where(same, full, 0.0).astype(BF16)
    polar_weight_ref[...] = lax.dot_general(
        weight, pick.astype(BF16), (((1,), (1,)), ((), ())), preferred_element_type=F32
    ).astype(BF16)
    rest = weight.astype(F32) * (1.0 - jnp.sum(pick, axis=0, keepdims=True))
    wide = lanes_of(row_count)
    turned = jnp.where(
        wide < LMAX,
        pltpu.roll(rest, LMAX, 1),
        jnp.where(wide < frame_rows - LMAX, rest, pltpu.roll(rest, frame_rows - LMAX, 1)),
    )
    rest = jnp.where(lax.rem(zone, 2) == 0, turned, rest).astype(BF16)

    for s in range(shells):
        values = jnp.concatenate([near_ref[s], own_ref[s], far_ref[s]], axis=0)
        out_ref[s] = jnp.dot(rest, values, preferred_element_type=F32)


def own_part():
    zone = lax.axis_index("zone")
    return jnp.where((zone == 0) | (zone == lax.axis_size("zone") - 1), 0, 1)


def add_polar(part, source_ref, weight_ref, lat_ref, polar_ref, sum_ref, sem, put):
    holders, held = source_ref.shape[:2]
    tiles = polar_ref.shape[0]
    polar = holders * held
    pitch = polar + 1
    fetch = pltpu.make_async_copy(lat_ref.at[pl.ds(part * PART, PART)], sum_ref, sem)
    fetch.start()
    for k in range(holders):
        for r in range(held):
            for t in range(tiles):
                polar_ref[t, pl.ds(k * held + r, PART, stride=pitch), :] = source_ref[
                    k, r, t * PART : (t + 1) * PART, :
                ].astype(F32)
    weight = weight_ref[...]
    fetch.wait()

    for s in range(PART):
        values = jnp.concatenate(
            [polar_ref[t, pl.ds(s * pitch, polar), :].astype(BF16) for t in range(tiles)], axis=1
        )
        put(s, sum_ref[s] + jnp.dot(weight, values, preferred_element_type=F32))


def own_kernel(mine_ref, weight_ref, lat_ref, out_ref, polar_ref, sum_ref, sem):
    def put(s, values):
        out_ref[s] = values.astype(BF16)

    add_polar(own_part(), mine_ref, weight_ref, lat_ref, polar_ref, sum_ref, sem, put)


def final_kernel(other_ref, own_ref, weight_ref, mix_ref, lat_ref, out_ref,
                 polar_ref, sum_ref, full_ref, stage_ref, sem, sems):
    shells, row_count, col_count = lat_ref.shape
    part = own_part()

    def put(s, values):
        full_ref[(1 - part) * PART + s] = values

    add_polar(1 - part, other_ref, weight_ref, lat_ref, polar_ref, sum_ref, sem, put)
    for s in range(PART):
        full_ref[part * PART + s] = own_ref[s].astype(F32)
    group = mix_ref.shape[0] // shells
    mix = mix_ref[...]
    stores = []
    for g in range(row_count // (2 * group)):
        mixed = []
        for e in range(2):
            first = (2 * g + e) * group
            values = full_ref[:, first : first + group, :].reshape(shells * group, col_count).astype(BF16)
            mixed.append(jnp.dot(mix, values, preferred_element_type=F32).reshape(shells, group, col_count))
        rows = pl.ds(2 * g * group, 2 * group)
        stage_ref[:, rows, :] = jnp.concatenate(mixed, axis=1).astype(BF16)
        stores.append(pltpu.make_async_copy(stage_ref.at[:, rows], out_ref.at[:, rows], sems.at[g]))
        stores[-1].start()
    for store in stores:
        store.wait()


def call(kernel, name, out_shape, scalars, arrays, scratch, flops=0, moved=0, direct=(), far=False, mib=16):
    smem = pl.BlockSpec(memory_space=pltpu.SMEM)
    vmem = pl.BlockSpec(memory_space=pltpu.VMEM)
    anywhere = pl.BlockSpec(memory_space=pl.ANY)
    many = isinstance(out_shape, tuple)
    return pl.pallas_call(
        kernel,
        out_shape=out_shape,
        in_specs=[smem] * len(scalars) + [vmem] * len(arrays) + [anywhere] * len(direct),
        out_specs=(vmem,) * len(out_shape) if many else anywhere if far else vmem,
        scratch_shapes=scratch,
        compiler_params=pltpu.CompilerParams(vmem_limit_bytes=mib << 20),
        cost_estimate=pl.CostEstimate(flops=flops, bytes_accessed=moved, transcendentals=0),
        name=name,
    )(*scalars, *arrays, *direct)


struct = jax.ShapeDtypeStruct


def pack(polar_rows, kernel, sectors):
    shells, row_count, col_count = kernel.shape
    tiles = col_count // LANES
    held = polar_rows.shape[0] // 2 // sectors
    edge = struct((shells * row_count // 2, LANES), BF16)
    parts = struct((sectors, held, tiles * PART, LANES), BF16)
    vmem = pl.BlockSpec(memory_space=pltpu.VMEM)
    anywhere = pl.BlockSpec(memory_space=pl.ANY)
    return pl.pallas_call(
        first_kernel,
        out_shape=(parts, edge, edge, parts),
        in_specs=[anywhere, anywhere],
        out_specs=(vmem, vmem, vmem, anywhere),
        scratch_shapes=[
            pltpu.VMEM((tiles, PART * PITCH, LANES), F32),
            pltpu.VMEM(kernel.shape, BF16),
            pltpu.VMEM(parts.shape, BF16),
            pltpu.SMEM(polar_rows.shape, jnp.int32),
            pltpu.SemaphoreType.DMA((4,)),
        ],
        compiler_params=pltpu.CompilerParams(vmem_limit_bytes=52 << 20),
        cost_estimate=pl.CostEstimate(flops=0, bytes_accessed=4 << 20, transcendentals=0),
        name="pack_polar_rows_and_edges",
    )(kernel, polar_rows)


def take_given(given, kept):
    anywhere = pl.BlockSpec(memory_space=pl.ANY)
    return pl.pallas_call(
        second_kernel,
        out_shape=struct(kept.shape, BF16),
        in_specs=[anywhere, anywhere],
        out_specs=anywhere,
        scratch_shapes=[pltpu.SemaphoreType.DMA],
        input_output_aliases={1: 0},
        compiler_params=pltpu.CompilerParams(vmem_limit_bytes=4 << 20),
        name="take_given",
    )(given, kept)


def smooth_lon(lon_halo, kernel, near, far):
    shells, row_count, col_count = kernel.shape
    tiles = col_count // LANES
    rows = pltpu.VMEM((row_count, LANES), F32)
    return call(
        lon_kernel,
        "smooth_along_longitude",
        (
            struct((shells, row_count, col_count), BF16),
            struct((shells, LMAX, col_count), BF16),
            struct((shells, LMAX, col_count), BF16),
        ),
        [lon_halo],
        [kernel, near, far],
        [
            pltpu.VMEM((tiles + 1, shells * PITCH, LANES), F32),
            pltpu.VMEM((tiles, shells * PITCH, LANES), F32),
            rows,
            rows,
            rows,
        ],
        flops=1 << 36,
        moved=16 << 20,
        mib=20,
    )


def hold(table, circles, after):
    sectors, held, block, _ = circles.shape
    return call(
        hold_kernel,
        "smooth_and_turn_polar_circles",
        struct(circles.shape, BF16),
        [table],
        [circles],
        [
            pltpu.VMEM((held, 2 * sectors * block + 2 * PART, LANES), BF16),
            pltpu.VMEM((held, sectors, block, LANES), BF16),
            pltpu.SemaphoreType.DMA((held,)),
        ],
        flops=1 << 30,
        moved=4 << 20,
        direct=[after],
        far=True,
    )


def smooth_lat(polar_rows, near, own, far, reach, blend):
    shells, row_count, _ = own.shape
    frame_rows = row_count + 2 * LMAX
    polar = polar_rows.shape[0] // 2
    return call(
        lat_kernel,
        "smooth_along_latitude",
        (
            struct(own.shape, F32),
            struct((row_count, polar), BF16),
            struct((shells * 8, shells * 8), BF16),
        ),
        [polar_rows],
        [near, own, far, reach, blend],
        [pltpu.VMEM((polar, frame_rows), F32)],
        flops=1 << 36,
        moved=8 << 20,
    )


def add_own(lat, mine, polar_weight):
    shells, row_count, col_count = lat.shape
    half = (PART, row_count, col_count)
    return call(
        own_kernel,
        "add_polar_rows_of_own_shells",
        struct(half, BF16),
        [],
        [mine, polar_weight],
        [
            pltpu.VMEM((col_count // LANES, PART * (polar_weight.shape[1] + 1), LANES), F32),
            pltpu.VMEM(half, F32),
            pltpu.SemaphoreType.DMA,
        ],
        flops=1 << 30,
        moved=4 << 20,
        direct=[lat],
        mib=50,
    )


def finish(lat, other, own, polar_weight, mix):
    shells, row_count, col_count = lat.shape
    return call(
        final_kernel,
        "add_polar_rows_and_blend",
        struct(lat.shape, BF16),
        [],
        [other, own, polar_weight, mix],
        [
            pltpu.VMEM((col_count // LANES, PART * (polar_weight.shape[1] + 1), LANES), F32),
            pltpu.VMEM((PART, row_count, col_count), F32),
            pltpu.VMEM(lat.shape, F32),
            pltpu.VMEM(lat.shape, BF16),
            pltpu.SemaphoreType.DMA,
            pltpu.SemaphoreType.DMA((4,)),
        ],
        flops=1 << 31,
        moved=8 << 20,
        far=True,
        direct=[lat],
        mib=50,
    )


def per_device(kernel, lon_halo, lat_reach, polar_rows, polar_shift, blend):
    shells, row_count, col_count = kernel.shape
    sectors = lax.axis_size("sector")
    zones = lax.axis_size("zone")
    last = zones - 1
    packed, near, far, kept = pack(polar_rows, kernel, sectors)
    given = lax.ppermute(packed, "zone", [(0, 1), (last, last - 1)])
    far = lax.ppermute(far, "sector", [(i, (i + 1 if i % 2 else i - 1) % sectors) for i in range(sectors)])
    near = lax.ppermute(near, "sector", [(i, i ^ 1) for i in range(sectors)])
    parts = take_given(given, kept)
    circles = lax.all_to_all(parts, "sector", 0, 0, tiled=True)
    lon_smooth, near_rows, far_rows = smooth_lon(lon_halo, kernel, near, far)
    turned = hold(jnp.concatenate([polar_rows, polar_shift, lon_halo]), circles, far_rows)
    far_rows = lax.ppermute(
        far_rows, "zone", [(i, i + 1 if i % 2 else i - 1) for i in range(1, zones - 1)]
    )
    near_rows = lax.ppermute(near_rows, "zone", [(i, i ^ 1) for i in range(zones)])
    mine = lax.all_to_all(turned, "sector", 0, 0, tiled=True)
    lat, polar_weight, mix = smooth_lat(
        polar_rows, near_rows, lon_smooth, far_rows, lat_reach[:, None], blend
    )
    mine, lat = lax.optimization_barrier((mine, lat))
    other = lax.ppermute(mine, "zone", [(0, 1), (1, 0), (last, last - 1), (last - 1, last)])
    own = add_own(lat, mine, polar_weight)
    return finish(lat, other, own, polar_weight, mix)


def solution(mesh):
    in_specs = (P(None, "zone", "sector"), P(), P("zone"), P(), P(), P())
    out_specs = P(None, "zone", "sector")
    return jax.shard_map(
        per_device, mesh=mesh, in_specs=in_specs, out_specs=out_specs, check_vma=False
    )
```
